512 devices in a mesh: seq: 128 (over y, z, core), head: 4 (over x).
Axes of the slice: x: 4, y: 8, z: 8, core: 2. Of those that a mesh axis runs over, the one named last changes fastest.
Arguments:
- queries: bfloat16 [16384, 2048], P('seq', 'head'), may hold values from -36 to 36
- keys: bfloat16 [16384, 2048], P('seq', 'head'), may hold values from -6 to 6
- values: bfloat16 [16384, 2048], P('seq', 'head'), may hold values from -6 to 6
- rates: float32 [16384, 4], P('seq', 'head'), may hold values from 0.05 to 1
- gate_fast: bfloat16 [4, 512, 256], P('head'), may hold values from -0.25 to 0.25
- up_fast: bfloat16 [4, 512, 256], P('head'), may hold values from -0.25 to 0.25
- down_fast: bfloat16 [4, 512, 256], P('head'), may hold values from -0.375 to 0.375
Outputs:
- mixed: bfloat16 [16384, 2048], P('seq', 'head')
The draws below stay inside these ranges and needn't reach their ends.
All inputs are finite; a program needn't handle non-finite values.
Results may differ from the reference program's by a relative error of at most 0.02.
Values may be sent and summed in bfloat16 or wider, within the bound.
A program may use at most 64 MiB of HBM per device.

```python
import math
import jax
import jax.numpy as jnp
from jax import lax

DH = 512
FH = 256
HEADS = 4
D = 2048
WINDOW = 128
TOKENS = 16384
SPAN = 8192


def draw_keys(key, part):
    key = jax.random.fold_in(key, 3)
    field = jnp.clip(jax.random.normal(key, (TOKENS, D), jnp.float32), -6.0, 6.0)
    return field.astype(jnp.bfloat16)


def draw_queries(key, part):
    key = jax.random.fold_in(key, 5)
    field = jnp.clip(jax.random.normal(key, (TOKENS, D), jnp.float32), -6.0, 6.0)
    return field.astype(jnp.bfloat16)


def block_scale(stream_key, shape, cuts, low, high):
    level, own = 1.0, jax.random.fold_in(stream_key, 6)
    for position, parts in cuts:
        steps = jnp.exp(jax.random.uniform(jax.random.fold_in(own, position), (parts,), jnp.float32, low / len(cuts), high / len(cuts)))
        level = level * jnp.repeat(steps, shape[position] // parts).reshape([-1 if axis == position else 1 for axis in range(len(shape))])
    return level


def centred(own_key, shape, scale, reach, cuts=(), kind=jnp.bfloat16):
    entries = scale * jax.random.normal(own_key, shape, jnp.float32)
    if cuts:
        entries = entries * block_scale(own_key, shape, cuts, -0.22, 0.18)
    return jnp.clip(entries, -reach, reach).astype(kind)


def setup_inputs(seed: int = 0) -> dict:
    key_of = jax.random.split(jax.random.key(seed), 8)
    return {
        "queries": draw_queries(jax.random.fold_in(key_of[7], 71), 0),
        "keys": draw_keys(jax.random.fold_in(key_of[7], 71), 0),
        "values": centred(key_of[2], (TOKENS, D), 1.0, 6.0, ((0, 128), (1, 4))),
        "rates": jnp.clip(jnp.exp(math.log(1.0) - 2.9957323 * jax.random.uniform(key_of[3], (TOKENS, HEADS), jnp.float32) ** block_scale(key_of[3], (TOKENS, HEADS), ((0, 128), (1, 4)), -0.2, 0.2)), 0.05, 1.0),
        "gate_fast": centred(key_of[4], (HEADS, DH, FH), DH ** -0.5, 0.25, ((0, 4),)),
        "up_fast": centred(key_of[5], (HEADS, DH, FH), DH ** -0.5, 0.25, ((0, 4),)),
        "down_fast": centred(key_of[6], (HEADS, DH, FH), FH ** -0.5, 0.375, ((0, 4),)),
    }


def dot_high(a, b):
    return jnp.dot(a, b, precision=lax.Precision.HIGHEST, preferred_element_type=jnp.float32)

def head_attention(q_head, k_head, v_head):
    pad_k = jnp.concatenate([jnp.zeros((WINDOW, DH), jnp.bfloat16), k_head], axis=0)
    pad_v = jnp.concatenate([jnp.zeros((WINDOW, DH), jnp.bfloat16), v_head], axis=0)
    row_pos = jnp.arange(WINDOW)[:, None]
    col_pos = jnp.arange(2 * WINDOW)[None, :]

    def block(index):
        start = (index * WINDOW).astype(jnp.int32)
        q_blk = lax.dynamic_slice_in_dim(q_head, start, WINDOW, 0)
        k_blk = lax.dynamic_slice_in_dim(pad_k, start, 2 * WINDOW, 0)
        v_blk = lax.dynamic_slice_in_dim(pad_v, start, 2 * WINDOW, 0)
        scores = jnp.einsum('td,sd->ts', q_blk, k_blk, preferred_element_type=jnp.float32) / jnp.sqrt(jnp.float32(DH))
        valid = (col_pos > row_pos) & (col_pos <= row_pos + WINDOW) & ((col_pos >= WINDOW) | (index > 0))
        scores = jnp.where(valid, scores, jnp.float32(-1e+30))
        top = lax.optimization_barrier(jnp.max(scores, axis=1, keepdims=True))
        expd = jnp.exp(scores - top)
        probs = (expd / lax.optimization_barrier(jnp.sum(expd, axis=1, keepdims=True))).astype(jnp.bfloat16)
        return jnp.dot(probs, v_blk, preferred_element_type=jnp.float32)
    blocks = lax.map(block, jnp.arange(TOKENS // WINDOW, dtype=jnp.int32))
    return blocks.reshape(TOKENS, DH)

def gradients(xin, yin, rin, w_gate, w_up, w_down):
    h1 = dot_high(xin, w_gate)
    h3 = dot_high(xin, w_up)
    sig = jax.nn.sigmoid(h1)
    s1 = h1 * sig
    gval = s1 * h3
    err = -rin * yin
    g_down = dot_high(err.T, gval)
    dgv = dot_high(err, w_down)
    g_gate = dot_high(xin.T, dgv * h3 * sig * (1.0 + h1 * (1.0 - sig)))
    g_up = dot_high(xin.T, dgv * s1)
    return (g_gate, g_up, g_down)

def update(weight, grad):
    return weight - 0.05 * grad / jnp.sqrt(lax.optimization_barrier(jnp.mean(grad * grad, axis=1, keepdims=True)) + 1e-06)

def apply_fast(qin, w_gate, w_up, w_down):
    hid = jax.nn.silu(dot_high(qin, w_gate)) * dot_high(qin, w_up)
    out = dot_high(hid, w_down.T)
    return (out / jnp.sqrt(lax.optimization_barrier(jnp.mean(out * out, axis=1, keepdims=True)) + 1e-06)).astype(jnp.bfloat16)

def reference(queries, keys, values, rates, gate_fast, up_fast, down_fast):
    columns = []
    for head in range(HEADS):
        lo = head * DH
        q_head = queries[:, lo:lo + DH]
        k_head = keys[:, lo:lo + DH]
        v_head = values[:, lo:lo + DH]
        attn = head_attention(q_head, k_head, v_head)
        w_gate = gate_fast[head].astype(jnp.float32)
        w_up = up_fast[head].astype(jnp.float32)
        w_down = down_fast[head].astype(jnp.float32)
        pieces = []
        for span in range(2):
            c0 = span * SPAN
            xin = k_head[c0:c0 + SPAN].astype(jnp.float32)
            yin = v_head[c0:c0 + SPAN].astype(jnp.float32)
            rin = rates[c0:c0 + SPAN, head:head + 1]
            g_gate, g_up, g_down = gradients(xin, yin, rin, w_gate, w_up, w_down)
            w_gate = update(w_gate, g_gate)
            w_up = update(w_up, g_up)
            w_down = update(w_down, g_down)
            pieces.append(apply_fast(q_head[c0:c0 + SPAN].astype(jnp.float32), w_gate, w_up, w_down))
        fast = jnp.concatenate(pieces, axis=0)
        columns.append((attn + fast.astype(jnp.float32)).astype(jnp.bfloat16))
    return jnp.concatenate(columns, axis=1)
```

```python
import functools
import math

import jax
import jax.numpy as jnp
from jax import lax
from jax.experimental import pallas as pl
from jax.experimental.pallas import tpu as pltpu
from jax.sharding import PartitionSpec as P

T = 128
DH = 512
FH = 256
HALF = 128
LANES = 128
NL = DH // LANES
ROWS = 3 * HALF
MESH = pl.DeviceIdType.MESH
F32 = jnp.float32
BF16 = jnp.bfloat16


def dot_nt(a, b):
    return lax.dot_general(a, b, (((1,), (1,)), ((), ())), preferred_element_type=F32)


def dot_nn(a, b):
    return jnp.dot(a, b, preferred_element_type=F32)


def split(a):
    high = a.astype(BF16)
    return high, (a - high.astype(F32)).astype(BF16)


def far_first(j, n):
    h = (j + 1) // 2
    return lax.rem(n // 2 + n + jnp.where(lax.rem(j, 2) == 1, -h, h), n)


def owner_row(k):
    return (k // 2) * 4 + 1 + lax.rem(k, 2)


def kernel(
    ny, nz,
    q_hbm, k_hbm, v_hbm, r_hbm, wg_hbm, wu_hbm, wd_hbm,
    out_ref,
    qq, kk, vv, hk, hv, r_in, rr, w_in, w_t, w_f, w_b,
    g_own, g_give, g_got, g_send0, g_send1, land0, land1, piece0, piece1, g_all0, g_all1,
    ss_own, ss_got, attn, f_give, f_got,
    in_sem, x_send, x_recv, h_send, h_recv, gh_send, gh_recv,
    rs_send, rs_recv, ag_send, ag_recv, ss_send, ss_recv, f_send, f_recv,
):
    s = lax.axis_index("seq")
    c = lax.rem(s, 2)
    chip = s // 2
    z = lax.rem(chip, nz)
    y = chip // nz
    half_y = ny // 2
    n_own = half_y * nz
    rows = ROWS * NL // n_own
    n_seq = ny * nz * 2
    span = y // half_y
    local_chip = chip - span * n_own
    is_owner0 = lax.rem((y + 1) // 2, 2) == 1
    own0 = (y + 3) // 4 * 2 - 2 + lax.rem(y + 3, 4)
    partner = s + 1 - 2 * c

    loads = [
        pltpu.make_async_copy(wg_hbm.at[0], w_in.at[0], in_sem.at[0]),
        pltpu.make_async_copy(wu_hbm.at[0], w_in.at[1], in_sem.at[1]),
        pltpu.make_async_copy(wd_hbm.at[0], w_in.at[2], in_sem.at[2]),
        pltpu.make_async_copy(k_hbm, kk.at[c], in_sem.at[3]),
        pltpu.make_async_copy(v_hbm, vv.at[c], in_sem.at[4]),
        pltpu.make_async_copy(r_hbm, r_in, in_sem.at[5]),
        pltpu.make_async_copy(q_hbm, qq.at[c], in_sem.at[6]),
    ]
    for load in loads:
        load.start()

    barrier = pltpu.get_barrier_semaphore()

    def greet(i, carry):
        zt = lax.rem(z + far_first(i // ny, nz), nz)
        yt = lax.rem(y + far_first(lax.rem(i, ny), ny), ny)
        target = (yt * nz + zt) * 2 + c

        @pl.when(target != s)
        def _():
            pl.semaphore_signal(barrier, inc=1, device_id={"seq": target}, device_id_type=MESH)

        return carry

    lax.fori_loop(0, ny * nz, greet, 0)
    pl.semaphore_signal(barrier, inc=1, device_id={"seq": partner}, device_id_type=MESH)
    beside = lax.rem(s + 2 * c - 1 + n_seq, n_seq)
    pl.semaphore_signal(barrier, inc=1, device_id={"seq": beside}, device_id_type=MESH)

    for m in range(3):
        loads[m].wait()
        w_t[m] = w_in[m].astype(F32).T.astype(BF16)
    for load in loads[3:]:
        load.wait()
    rr[c] = jnp.broadcast_to(r_in[...], (8, LANES))

    def activations(times, x, y_val, rate):
        h1 = times(0, x)
        h3 = times(1, x)
        dg = times(2, y_val) * (-rate)
        sig = jax.nn.sigmoid(h1)
        s1 = h1 * sig
        a_gate = dg * h3 * sig * (1.0 + h1 * (1.0 - sig))
        a_up = dg * s1
        a_down = (s1 * h3) * (-rate)
        return a_gate.astype(BF16), a_up.astype(BF16), a_down.astype(BF16)

    @pl.when(span == 0)
    def _():
        x, y_val = kk[c], vv[c]
        acts = activations(lambda m, a: dot_nt(w_t[m], a), x, y_val, rr[c][0:1])
        for m in range(3):
            grad = dot_nn(acts[m], x if m < 2 else y_val)
            low, high = grad[:HALF], grad[HALF:]
            mine = jnp.where(c == 0, low, high)
            theirs = jnp.where(c == 0, high, low).astype(BF16)
            for b in range(NL):
                g_own[b, m * HALF:(m + 1) * HALF, :] = mine[:, b * LANES:(b + 1) * LANES]
                g_give[b, m * HALF:(m + 1) * HALF, :] = theirs[:, b * LANES:(b + 1) * LANES]

    pl.semaphore_wait(barrier, ny * nz + 1)

    def to_partner(src, dst, send, recv):
        return pltpu.make_async_remote_copy(
            src_ref=src, dst_ref=dst, send_sem=send, recv_sem=recv, device_id={"seq": partner}, device_id_type=MESH
        )

    give = to_partner(g_give, g_got, gh_send, gh_recv)
    shares = [
        to_partner(ref.at[c], ref.at[c], x_send.at[i], x_recv.at[i]) for i, ref in enumerate((kk, vv, rr, qq))
    ]

    @pl.when(span == 0)
    def _():
        give.start()

    for share in shares:
        share.start()

    def block(ref, o):
        first = pl.multiple_of((o // NL) * rows, 16)
        return ref.at[lax.rem(o, NL), pl.ds(first, rows)]

    def scatter(src, land, y_of, phase):
        def send(i, carry):
            zt = lax.rem(z + far_first(i // half_y, nz), nz)
            k = lax.rem(i, half_y)
            target = (y_of(k) * nz + zt) * 2 + c
            from_ref, to_ref = block(src, k * nz + zt), land.at[local_chip]

            @pl.when(target == s)
            def _():
                pltpu.make_async_copy(from_ref, to_ref, rs_recv.at[phase]).start()

            @pl.when(target != s)
            def _():
                pltpu.make_async_remote_copy(
                    src_ref=from_ref, dst_ref=to_ref, send_sem=rs_send.at[phase], recv_sem=rs_recv.at[phase],
                    device_id={"seq": target}, device_id_type=MESH,
                ).start()

            return carry

        lax.fori_loop(0, n_own, send, 0)

    def reduce_piece(land, piece, phase):
        pltpu.make_async_copy(land, land, rs_recv.at[phase]).wait()
        total = land[0].astype(F32)
        for i in range(1, n_own):
            total = total + land[i].astype(F32)
        piece[...] = total.astype(BF16)

    def gather(piece, o, dst, first_y, sem, phase):
        def send(i, carry):
            zt = lax.rem(z + far_first(i // half_y, nz), nz)
            target = ((first_y + lax.rem(i, half_y)) * nz + zt) * 2 + c
            to_ref = block(dst, o)

            @pl.when(target == s)
            def _():
                pltpu.make_async_copy(piece, to_ref, ag_recv.at[phase]).start()

            @pl.when(target != s)
            def _():
                pltpu.make_async_remote_copy(
                    src_ref=piece, dst_ref=to_ref, send_sem=ag_send.at[sem], recv_sem=ag_recv.at[phase],
                    device_id={"seq": target}, device_id_type=MESH,
                ).start()

            return carry

        lax.fori_loop(0, n_own, send, 0)

    def wait_sent(sem, land, one_stayed):
        @pl.when(one_stayed)
        def _():
            part = land.at[pl.ds(0, n_own - 1)]
            pltpu.make_async_copy(part, part, sem).wait()

        @pl.when(jnp.logical_not(one_stayed))
        def _():
            pltpu.make_async_copy(land, land, sem).wait()

    @pl.when(span == 0)
    def _():
        give.wait_recv()
        g_send0[...] = (g_own[...] + g_got[...].astype(F32)).astype(BF16)
        scatter(g_send0, land0, owner_row, 0)

    halo = [
        pltpu.make_async_remote_copy(
            src_ref=src.at[c], dst_ref=dst, send_sem=h_send.at[i], recv_sem=h_recv.at[i],
            device_id={"seq": beside}, device_id_type=MESH,
        )
        for i, (src, dst) in enumerate(((kk, hk), (vv, hv)))
    ]

    def attention():
        @pl.when(c == 1)
        def _():
            for copy in halo:
                copy.start()

        for share in shares:
            share.wait_recv()

        @pl.when(c == 0)
        def _():
            for copy in halo:
                copy.wait_recv()

        @pl.when(c == 1)
        def _():
            hk[...] = kk[0]
            hv[...] = vv[0]

        q = qq[c]
        inv = jnp.sqrt(jnp.float32(DH))
        before = dot_nt(q, hk[...]) / inv
        here = dot_nt(q, kk[c]) / inv
        row = lax.broadcasted_iota(jnp.int32, (T, T), 0)
        col = lax.broadcasted_iota(jnp.int32, (T, T), 1)
        before = jnp.where((col > row) & (s > 0), before, jnp.float32(-1e30))
        here = jnp.where(col <= row, here, jnp.float32(-1e30))
        top = jnp.maximum(jnp.max(before, axis=1, keepdims=True), jnp.max(here, axis=1, keepdims=True))
        before, here = jnp.exp(before - top), jnp.exp(here - top)
        norm = jnp.sum(before, axis=1, keepdims=True) + jnp.sum(here, axis=1, keepdims=True)
        before, here = (before / norm).astype(BF16), (here / norm).astype(BF16)
        attn[...] = dot_nn(before, hv[...]) + dot_nn(here, vv[c])

    @pl.when(span == 1)
    def _():
        attention()

    @pl.when(is_owner0)
    def _():
        reduce_piece(land0, piece0, 0)
        o = own0 * nz + z
        gather(piece0, o, g_all0, half_y, 0, 0)
        gather(piece0, o, g_all0, 0, 1, 0)

    @pl.when(span == 0)
    def _():
        attention()

    def descend(phase, g_all, old):
        pltpu.make_async_copy(g_all, g_all, ag_recv.at[phase]).wait()
        ss_own[phase] = jnp.zeros((16, LANES), F32)
        for m in range(3):
            for b in range(NL):
                g = g_all[b, m * HALF:(m + 1) * HALF, :].astype(F32)
                ss_own[phase, m * NL + b:m * NL + b + 1, :] = jnp.sum(g * g, axis=0, keepdims=True)
        swap = to_partner(ss_own.at[phase], ss_got.at[phase], ss_send.at[phase], ss_recv.at[phase])
        swap.start()
        swap.wait()
        scale = 0.05 * lax.rsqrt((ss_own[phase] + ss_got[phase]) * (1.0 / FH) + 1e-06)
        for m in range(3):
            for b in range(NL):
                g = g_all[b, m * HALF:(m + 1) * HALF, :].astype(F32)
                j = m * NL + b
                new = old(m, b) - g * scale[j:j + 1]
                w_f[b, m * HALF:(m + 1) * HALF, :] = new
                for i, term in enumerate(split(new)):
                    w_b[i, m * HALF:(m + 1) * HALF, b * LANES:(b + 1) * LANES] = term

    first = pl.multiple_of(c * HALF, HALF)
    descend(0, g_all0, lambda m, b: w_t[m, pl.ds(first, HALF), b * LANES:(b + 1) * LANES].astype(F32))

    @pl.when(span == 1)
    def _():
        x, y_val = kk[...].reshape(2 * T, DH), vv[...].reshape(2 * T, DH)
        rate = jnp.concatenate([rr[0][0:1], rr[1][0:1]], axis=1)
        acts = activations(
            lambda m, a: dot_nt(w_b[0, m * HALF:(m + 1) * HALF], a) + dot_nt(w_b[1, m * HALF:(m + 1) * HALF], a),
            x, y_val, rate,
        )
        for m in range(3):
            grad = dot_nn(acts[m], x if m < 2 else y_val).astype(BF16)
            for b in range(NL):
                g_send1[b, m * HALF:(m + 1) * HALF, :] = grad[:, b * LANES:(b + 1) * LANES]
        scatter(g_send1, land1, lambda k: half_y + k, 1)
        reduce_piece(land1, piece1, 1)
        gather(piece1, local_chip, g_all1, half_y, 2, 1)
        descend(1, g_all1, lambda m, b: w_f[b, m * HALF:(m + 1) * HALF, :])

    q_all = qq[...].reshape(2 * T, DH)
    h1 = dot_nt(q_all, w_b[0, 0:HALF]) + dot_nt(q_all, w_b[1, 0:HALF])
    h3 = dot_nt(q_all, w_b[0, HALF:2 * HALF]) + dot_nt(q_all, w_b[1, HALF:2 * HALF])
    high, low = split(h1 * jax.nn.sigmoid(h1) * h3)
    w_high, w_low = w_b[0, 2 * HALF:ROWS], w_b[1, 2 * HALF:ROWS]
    f = dot_nn(high, w_high) + (dot_nn(low, w_high) + dot_nn(high, w_low))
    mine = jnp.where(c == 0, f[:T], f[T:])
    f_give[...] = jnp.where(c == 0, f[T:], f[:T])
    swap = to_partner(f_give, f_got, f_send, f_recv)
    swap.start()
    swap.wait()
    f = mine + f_got[...]
    fast = (f * lax.rsqrt(jnp.mean(f * f, axis=1, keepdims=True) + 1e-06)).astype(BF16)
    out_ref[...] = (attn[...] + fast.astype(F32)).astype(BF16)

    for share in shares:
        share.wait_send()

    @pl.when(c == 1)
    def _():
        for copy in halo:
            copy.wait_send()

    @pl.when(span == 0)
    def _():
        give.wait_send()
        wait_sent(rs_send.at[0], land0, is_owner0)

    @pl.when(is_owner0)
    def _():
        wait_sent(ag_send.at[0], land0, span == 1)
        wait_sent(ag_send.at[1], land0, span == 0)

    @pl.when(span == 1)
    def _():
        wait_sent(rs_send.at[1], land1, span == 1)
        wait_sent(ag_send.at[2], land1, span == 1)


def local(ny, nz, queries, keys, values, rates, gate_fast, up_fast, down_fast):
    n_own = ny // 2 * nz
    rows = ROWS * NL // n_own
    dma = pltpu.SemaphoreType.DMA
    full = (NL, ROWS, LANES)
    return pl.pallas_call(
        functools.partial(kernel, ny, nz),
        out_shape=jax.ShapeDtypeStruct((T, DH), BF16),
        in_specs=[pl.BlockSpec(memory_space=pl.ANY)] * 7,
        out_specs=pl.BlockSpec(memory_space=pltpu.VMEM),
        scratch_shapes=[
            pltpu.VMEM((2, T, DH), BF16),
            pltpu.VMEM((2, T, DH), BF16),
            pltpu.VMEM((2, T, DH), BF16),
            pltpu.VMEM((T, DH), BF16),
            pltpu.VMEM((T, DH), BF16),
            pltpu.VMEM((1, T), F32),
            pltpu.VMEM((2, 8, LANES), F32),
            pltpu.VMEM((3, DH, FH), BF16),
            pltpu.VMEM((3, FH, DH), BF16),
            pltpu.VMEM(full, F32),
            pltpu.VMEM((2, ROWS, DH), BF16),
            pltpu.VMEM(full, F32),
            pltpu.VMEM(full, BF16),
            pltpu.VMEM(full, BF16),
            pltpu.VMEM(full, BF16),
            pltpu.VMEM(full, BF16),
            pltpu.VMEM((n_own, rows, LANES), BF16),
            pltpu.VMEM((n_own, rows, LANES), BF16),
            pltpu.VMEM((rows, LANES), BF16),
            pltpu.VMEM((rows, LANES), BF16),
            pltpu.VMEM(full, BF16),
            pltpu.VMEM(full, BF16),
            pltpu.VMEM((2, 16, LANES), F32),
            pltpu.VMEM((2, 16, LANES), F32),
            pltpu.VMEM((T, DH), F32),
            pltpu.VMEM((T, DH), F32),
            pltpu.VMEM((T, DH), F32),
            dma((7,)),
            dma((4,)),
            dma((4,)),
            dma((2,)),
            dma((2,)),
            dma,
            dma,
            dma((2,)),
            dma((2,)),
            dma((3,)),
            dma((2,)),
            dma((2,)),
            dma((2,)),
            dma,
            dma,
        ],
        compiler_params=pltpu.CompilerParams(
            collective_id=0, has_side_effects=True, vmem_limit_bytes=60 * 2**20
        ),
        name="fast_layer",
    )(queries, keys, values, rates.reshape(1, T), gate_fast, up_fast, down_fast)


def solution(mesh):
    n_chips = mesh.shape["seq"] // 2
    ny = 1 << ((n_chips.bit_length()) // 2)
    nz = n_chips // ny
    return jax.shard_map(
        functools.partial(local, ny, nz),
        mesh=mesh,
        in_specs=(
            P("seq", "head"),
            P("seq", "head"),
            P("seq", "head"),
            P("seq", "head"),
            P("head", None, None),
            P("head", None, None),
            P("head", None, None),
        ),
        out_specs=P("seq", "head"),
        check_vma=False,
    )
```

```python
import functools
import math

import jax
import jax.numpy as jnp
from jax import lax
from jax.experimental import pallas as pl
from jax.experimental.pallas import tpu as pltpu
from jax.sharding import PartitionSpec as P

T = 128
DH = 512
FH = 256
HALF = 128
LANES = 128
NL = DH // LANES
ROWS = 3 * HALF
MESH = pl.DeviceIdType.MESH
F32 = jnp.float32
BF16 = jnp.bfloat16


def dot_nt(a, b):
    return lax.dot_general(a, b, (((1,), (1,)), ((), ())), preferred_element_type=F32)


def dot_nn(a, b):
    return jnp.dot(a, b, preferred_element_type=F32)


def split(a):
    high = a.astype(BF16)
    return high, (a - high.astype(F32)).astype(BF16)


def far_first(j, n):
    h = (j + 1) // 2
    return lax.rem(n // 2 + n + jnp.where(lax.rem(j, 2) == 1, -h, h), n)


def far_offsets(n):
    return sorted(range(1, n), key=lambda d: -min(d, n - d))


def kernel(
    ny, nz,
    q_hbm, k_hbm, v_hbm, r_hbm, wg_hbm, wu_hbm, wd_hbm,
    out_ref,
    qq, kk, vv, hk, hv, r_in, rr, w_in, w_f, w_b,
    g_own, g_give, g_got, g_send0, g_send1, g_all0, g_all1,
    landz0, landz1, midz0, midz1, finy0, finy1, landy0, landy1, midy0, midy1, finz0, finz1, piece0, piece1,
    ss_own, ss_got, attn, f_give, f_got,
    in_sem, x_send, x_recv, h_send, h_recv, gh_send, gh_recv,
    rs_send, rs_recv, ag_send, ag_recv, ss_send, ss_recv, f_send, f_recv,
):
    s = lax.axis_index("seq")
    c = lax.rem(s, 2)
    chip = s // 2
    z = lax.rem(chip, nz)
    y = chip // nz
    half_y = ny // 2
    rows = ROWS // nz
    nb = NL // half_y
    n_seq = ny * nz * 2
    span = y // half_y
    local_y = y - span * half_y
    partner = s + 1 - 2 * c
    owner0 = jnp.where(c == 0, span == 0, lax.rem((y + 1) // 2, 2) == 1)
    own0 = jnp.where(c == 0, local_y, (y + 3) // 4 * 2 - 2 + lax.rem(y + 3, 4))

    def row0(k):
        return jnp.where(c == 0, k, (k // 2) * 4 + 1 + lax.rem(k, 2))

    def row1(k):
        return half_y + k

    def seq_at(row, column):
        return (row * nz + column) * 2 + c

    loads = [
        pltpu.make_async_copy(k_hbm, kk.at[c], in_sem.at[0]),
        pltpu.make_async_copy(v_hbm, vv.at[c], in_sem.at[1]),
        pltpu.make_async_copy(r_hbm, r_in, in_sem.at[2]),
        pltpu.make_async_copy(wg_hbm.at[0], w_in.at[0], in_sem.at[3]),
        pltpu.make_async_copy(wu_hbm.at[0], w_in.at[1], in_sem.at[4]),
        pltpu.make_async_copy(wd_hbm.at[0], w_in.at[2], in_sem.at[5]),
        pltpu.make_async_copy(q_hbm, qq.at[c], in_sem.at[6]),
    ]
    for load in loads:
        load.start()

    barrier = pltpu.get_barrier_semaphore()

    def greet(target):
        pl.semaphore_signal(barrier, inc=1, device_id={"seq": target}, device_id_type=MESH)

    for i in range(ny - 1):
        greet(seq_at(lax.rem(y + far_offsets(ny)[i], ny), z))
    for i in range(nz - 1):
        greet(seq_at(y, lax.rem(z + far_offsets(nz)[i], nz)))
    beside = lax.rem(s + 2 * c - 1 + n_seq, n_seq)
    greet(beside)
    greet(partner)

    for load in loads:
        load.wait()
    rr[c] = jnp.broadcast_to(r_in[...], (8, LANES))

    def slopes(h1, h3, dg, rate):
        sig = jax.nn.sigmoid(h1)
        s1 = h1 * sig
        a_gate = dg * h3 * sig * (1.0 + h1 * (1.0 - sig))
        return a_gate, dg * s1, (s1 * h3) * rate

    @pl.when(span == 0)
    def _():
        x, y_val = kk[c], vv[c]
        minus_r = -jnp.broadcast_to(r_in[...], (LANES, T)).T[:, 0:1]
        acts = slopes(dot_nn(x, w_in[0]), dot_nn(x, w_in[1]), dot_nn(y_val, w_in[2]) * minus_r, minus_r)
        for m in range(3):
            grad = dot_nn(acts[m].T.astype(BF16), x if m < 2 else y_val)
            low, high = grad[:HALF], grad[HALF:]
            mine = jnp.where(c == 0, low, high)
            theirs = jnp.where(c == 0, high, low).astype(BF16)
            for b in range(NL):
                g_own[b, m * HALF:(m + 1) * HALF, :] = mine[:, b * LANES:(b + 1) * LANES]
                g_give[b, m * HALF:(m + 1) * HALF, :] = theirs[:, b * LANES:(b + 1) * LANES]

    pl.semaphore_wait(barrier, ny + nz)

    def remote(src, dst, send, recv, target):
        return pltpu.make_async_remote_copy(
            src_ref=src, dst_ref=dst, send_sem=send, recv_sem=recv, device_id={"seq": target}, device_id_type=MESH
        )

    give = remote(g_give, g_got, gh_send, gh_recv, partner)
    shares = [
        remote(ref.at[c], ref.at[c], x_send.at[i], x_recv.at[i], partner) for i, ref in enumerate((kk, vv, rr, qq))
    ]

    @pl.when(span == 0)
    def _():
        give.start()

    for share in shares:
        share.start()

    def fan(n, place, src, dst, send, recv):
        def one(i, carry):
            index, target = place(i)
            from_ref, to_ref = src(index), dst(index)

            @pl.when(target == s)
            def _():
                pltpu.make_async_copy(from_ref, to_ref, recv).start()

            @pl.when(target != s)
            def _():
                remote(from_ref, to_ref, send, recv, target).start()

            return carry

        lax.fori_loop(0, n, one, 0)

    def along_z(i):
        zt = lax.rem(z + far_first(i, nz), nz)
        return zt, seq_at(y, zt)

    def along_y(row_of):
        def place(i):
            k = lax.rem(i + y + 1, half_y)
            return k, seq_at(row_of(k), z)

        return place

    def part(column):
        return pl.ds(pl.multiple_of(column * rows, 16), rows)

    def lanes(k):
        return pl.ds(k * nb, nb)

    def arrived(ref, sem):
        pltpu.make_async_copy(ref, ref, sem).wait()

    def total(ref):
        out = ref[0].astype(F32)
        for i in range(1, ref.shape[0]):
            out = out + ref[i].astype(F32)
        return out.astype(BF16)

    def scatter_first(p, g_send, landz, landy, row_of):
        @pl.when(c == 0)
        def _():
            fan(nz, along_z, lambda zt: g_send.at[:, part(zt)], lambda zt: landz.at[z], rs_send.at[p, 0], rs_recv.at[p, 0])

        @pl.when(c == 1)
        def _():
            fan(half_y, along_y(row_of), lambda k: g_send.at[lanes(k)], lambda k: landy.at[local_y],
                rs_send.at[p, 0], rs_recv.at[p, 0])

    def scatter_second(p, in_span, owner, landz, midz, finy, landy, midy, finz, piece, row_of):
        @pl.when((c == 0) & in_span)
        def _():
            arrived(landz, rs_recv.at[p, 0])
            midz[...] = total(landz)
            fan(half_y, along_y(row_of), lambda k: midz.at[lanes(k)], lambda k: finy.at[local_y],
                rs_send.at[p, 1], rs_recv.at[p, 1])

        @pl.when((c == 0) & owner)
        def _():
            arrived(finy, rs_recv.at[p, 1])
            piece[...] = total(finy)

        @pl.when((c == 1) & owner)
        def _():
            arrived(landy, rs_recv.at[p, 0])
            midy[...] = total(landy)
            fan(nz, along_z, lambda zt: midy.at[:, part(zt)], lambda zt: finz.at[z], rs_send.at[p, 1], rs_recv.at[p, 1])
            arrived(finz, rs_recv.at[p, 1])
            piece[...] = total(finz)

    def gather(p, owner, own, piece, g_all, first_rows):
        @pl.when((c == 0) & owner)
        def _():
            for i, first in enumerate(first_rows):
                fan(half_y, along_y(lambda k: first + k), lambda k: piece, lambda k: g_all.at[lanes(own), part(z)],
                    ag_send.at[p, i], ag_recv.at[p, 0])

        @pl.when(c == 0)
        def _():
            arrived(g_all.at[:, part(z)], ag_recv.at[p, 0])

            def one(i, carry):
                zt, target = along_z(i)
                remote(g_all.at[:, part(z)], g_all.at[:, part(z)], ag_send.at[p, 2], ag_recv.at[p, 1], target).start()
                return carry

            lax.fori_loop(0, nz - 1, one, 0)

        @pl.when((c == 1) & owner)
        def _():
            fan(nz, along_z, lambda zt: piece, lambda zt: g_all.at[lanes(own), part(z)], ag_send.at[p, 0], ag_recv.at[p, 0])
            arrived(g_all.at[lanes(own)], ag_recv.at[p, 0])
            for i, first in enumerate(first_rows):

                def one(j, carry):
                    k, target = along_y(lambda k: first + k)(j)

                    @pl.when(target != s)
                    def _():
                        remote(g_all.at[lanes(own)], g_all.at[lanes(own)], ag_send.at[p, 1 + i], ag_recv.at[p, 1], target).start()

                    return carry

                lax.fori_loop(0, half_y, one, 0)

    def gathered(p, owner, g_all):
        @pl.when(c == 0)
        def _():
            arrived(g_all.at[:, pl.ds(0, ROWS - rows)], ag_recv.at[p, 1])

        @pl.when((c == 1) & owner)
        def _():
            arrived(g_all.at[pl.ds(0, NL - nb)], ag_recv.at[p, 1])

        @pl.when((c == 1) & jnp.logical_not(owner))
        def _():
            arrived(g_all, ag_recv.at[p, 1])

    first = pl.multiple_of(c * HALF, HALF)

    def initial_weights():
        for m in range(3):
            w = w_in[m, :, pl.ds(first, HALF)].astype(F32).T
            for b in range(NL):
                w_f[b, m * HALF:(m + 1) * HALF, :] = w[:, b * LANES:(b + 1) * LANES]

    halo = [
        remote(src.at[c], dst, h_send.at[i], h_recv.at[i], beside) for i, (src, dst) in enumerate(((kk, hk), (vv, hv)))
    ]

    def attention():
        @pl.when(c == 1)
        def _():
            for copy in halo:
                copy.start()

        for share in shares:
            share.wait_recv()

        @pl.when(c == 0)
        def _():
            for copy in halo:
                copy.wait_recv()

        @pl.when(c == 1)
        def _():
            hk[...] = kk[0]
            hv[...] = vv[0]

        q = qq[c]
        inv = jnp.sqrt(jnp.float32(DH))
        before = dot_nt(q, hk[...]) / inv
        here = dot_nt(q, kk[c]) / inv
        row = lax.broadcasted_iota(jnp.int32, (T, T), 0)
        col = lax.broadcasted_iota(jnp.int32, (T, T), 1)
        before = jnp.where((col > row) & (s > 0), before, jnp.float32(-1e30))
        here = jnp.where(col <= row, here, jnp.float32(-1e30))
        top = jnp.maximum(jnp.max(before, axis=1, keepdims=True), jnp.max(here, axis=1, keepdims=True))
        before, here = jnp.exp(before - top), jnp.exp(here - top)
        norm = jnp.sum(before, axis=1, keepdims=True) + jnp.sum(here, axis=1, keepdims=True)
        before, here = (before / norm).astype(BF16), (here / norm).astype(BF16)
        attn[...] = dot_nn(before, hv[...]) + dot_nn(here, vv[c])

    @pl.when(span == 0)
    def _():
        give.wait_recv()
        g_send0[...] = (g_own[...] + g_got[...].astype(F32)).astype(BF16)
        scatter_first(0, g_send0, landz0, landy0, row0)

    initial_weights()

    @pl.when(span == 1)
    def _():
        attention()

    scatter_second(0, span == 0, owner0, landz0, midz0, finy0, landy0, midy0, finz0, piece0, row0)
    gather(0, owner0, own0, piece0, g_all0, (half_y, 0))

    @pl.when(span == 0)
    def _():
        attention()

    def descend(p, g_all):
        ss_own[p] = jnp.zeros((16, LANES), F32)
        for m in range(3):
            for b in range(NL):
                g = g_all[b, m * HALF:(m + 1) * HALF, :].astype(F32)
                ss_own[p, m * NL + b:m * NL + b + 1, :] = jnp.sum(g * g, axis=0, keepdims=True)
        swap = remote(ss_own.at[p], ss_got.at[p], ss_send.at[p], ss_recv.at[p], partner)
        swap.start()
        swap.wait()
        scale = 0.05 * lax.rsqrt((ss_own[p] + ss_got[p]) * (1.0 / FH) + 1e-06)
        for m in range(3):
            for b in range(NL):
                g = g_all[b, m * HALF:(m + 1) * HALF, :].astype(F32)
                j = m * NL + b
                new = w_f[b, m * HALF:(m + 1) * HALF, :] - g * scale[j:j + 1]
                w_f[b, m * HALF:(m + 1) * HALF, :] = new
                for i, term in enumerate(split(new)):
                    w_b[i, m * HALF:(m + 1) * HALF, b * LANES:(b + 1) * LANES] = term

    gathered(0, owner0, g_all0)
    descend(0, g_all0)

    @pl.when(span == 1)
    def _():
        x, y_val = kk[...].reshape(2 * T, DH), vv[...].reshape(2 * T, DH)
        minus_r = -jnp.concatenate([rr[0][0:1], rr[1][0:1]], axis=1)

        def times(m, a):
            return dot_nt(w_b[0, m * HALF:(m + 1) * HALF], a) + dot_nt(w_b[1, m * HALF:(m + 1) * HALF], a)

        acts = slopes(times(0, x), times(1, x), times(2, y_val) * minus_r, minus_r)
        for m in range(3):
            grad = dot_nn(acts[m].astype(BF16), x if m < 2 else y_val).astype(BF16)
            for b in range(NL):
                g_send1[b, m * HALF:(m + 1) * HALF, :] = grad[:, b * LANES:(b + 1) * LANES]
        scatter_first(1, g_send1, landz1, landy1, row1)
        scatter_second(1, True, True, landz1, midz1, finy1, landy1, midy1, finz1, piece1, row1)
        gather(1, True, local_y, piece1, g_all1, (half_y,))
        gathered(1, True, g_all1)
        descend(1, g_all1)

    def apply():
        q_all = qq[...].reshape(2 * T, DH)
        h1 = dot_nt(q_all, w_b[0, 0:HALF]) + dot_nt(q_all, w_b[1, 0:HALF])
        h3 = dot_nt(q_all, w_b[0, HALF:2 * HALF]) + dot_nt(q_all, w_b[1, HALF:2 * HALF])
        high, low = split(h1 * jax.nn.sigmoid(h1) * h3)
        w_high, w_low = w_b[0, 2 * HALF:ROWS], w_b[1, 2 * HALF:ROWS]
        f = dot_nn(high, w_high) + (dot_nn(low, w_high) + dot_nn(high, w_low))
        mine = jnp.where(c == 0, f[:T], f[T:])
        f_give[...] = jnp.where(c == 0, f[T:], f[:T])
        swap = remote(f_give, f_got, f_send, f_recv, partner)
        swap.start()
        swap.wait()
        f = mine + f_got[...]
        fast = (f * lax.rsqrt(jnp.mean(f * f, axis=1, keepdims=True) + 1e-06)).astype(BF16)
        out_ref[...] = (attn[...] + fast.astype(F32)).astype(BF16)

    apply()

    for share in shares:
        share.wait_send()

    @pl.when(c == 1)
    def _():
        for copy in halo:
            copy.wait_send()

    def left(sem, land, one_stayed):
        if one_stayed is True:
            arrived(land.at[pl.ds(0, land.shape[0] - 1)], sem)
            return

        @pl.when(one_stayed)
        def _():
            arrived(land.at[pl.ds(0, land.shape[0] - 1)], sem)

        @pl.when(jnp.logical_not(one_stayed))
        def _():
            arrived(land, sem)

    def all_left(p, in_span, owner, landz, finy, landy, finz, spans):
        @pl.when((c == 0) & in_span)
        def _():
            left(rs_send.at[p, 0], landz, True)
            left(rs_send.at[p, 1], finy, owner)

        @pl.when((c == 1) & in_span)
        def _():
            left(rs_send.at[p, 0], landy, owner)

        @pl.when((c == 0) & owner)
        def _():
            for i, k in enumerate(spans):
                left(ag_send.at[p, i], finy, span == k)

        @pl.when(c == 0)
        def _():
            left(ag_send.at[p, 2], landz, True)

        @pl.when((c == 1) & owner)
        def _():
            left(rs_send.at[p, 1], finz, True)
            left(ag_send.at[p, 0], finz, True)
            for i, k in enumerate(spans):
                left(ag_send.at[p, 1 + i], landy, span == k)

    @pl.when(span == 0)
    def _():
        give.wait_send()

    all_left(0, span == 0, owner0, landz0, finy0, landy0, finz0, (1, 0))

    @pl.when(span == 1)
    def _():
        all_left(1, True, True, landz1, finy1, landy1, finz1, (1,))


def local(ny, nz, queries, keys, values, rates, gate_fast, up_fast, down_fast):
    rows = ROWS // nz
    half_y = ny // 2
    nb = NL // half_y
    dma = pltpu.SemaphoreType.DMA
    full = (NL, ROWS, LANES)

    def twice(*shape):
        return [pltpu.VMEM(shape, BF16)] * 2

    return pl.pallas_call(
        functools.partial(kernel, ny, nz),
        out_shape=jax.ShapeDtypeStruct((T, DH), BF16),
        in_specs=[pl.BlockSpec(memory_space=pl.ANY)] * 7,
        out_specs=pl.BlockSpec(memory_space=pltpu.VMEM),
        scratch_shapes=[
            pltpu.VMEM((2, T, DH), BF16),
            pltpu.VMEM((2, T, DH), BF16),
            pltpu.VMEM((2, T, DH), BF16),
            pltpu.VMEM((T, DH), BF16),
            pltpu.VMEM((T, DH), BF16),
            pltpu.VMEM((1, T), F32),
            pltpu.VMEM((2, 8, LANES), F32),
            pltpu.VMEM((3, DH, FH), BF16),
            pltpu.VMEM(full, F32),
            pltpu.VMEM((2, ROWS, DH), BF16),
            pltpu.VMEM(full, F32),
            pltpu.VMEM(full, BF16),
            pltpu.VMEM(full, BF16),
            *twice(*full),
            *twice(*full),
            *twice(nz, NL, rows, LANES),
            *twice(NL, rows, LANES),
            *twice(half_y, nb, rows, LANES),
            *twice(half_y, nb, ROWS, LANES),
            *twice(nb, ROWS, LANES),
            *twice(nz, nb, rows, LANES),
            *twice(nb, rows, LANES),
            pltpu.VMEM((2, 16, LANES), F32),
            pltpu.VMEM((2, 16, LANES), F32),
            pltpu.VMEM((T, DH), F32),
            pltpu.VMEM((T, DH), F32),
            pltpu.VMEM((T, DH), F32),
            dma((7,)),
            dma((4,)),
            dma((4,)),
            dma((2,)),
            dma((2,)),
            dma,
            dma,
            dma((2, 2)),
            dma((2, 2)),
            dma((2, 3)),
            dma((2, 2)),
            dma((2,)),
            dma((2,)),
            dma,
            dma,
        ],
        compiler_params=pltpu.CompilerParams(
            collective_id=0, has_side_effects=True, vmem_limit_bytes=60 * 2**20
        ),
        name="fast_layer",
    )(queries, keys, values, rates.reshape(1, T), gate_fast, up_fast, down_fast)


def solution(mesh):
    n_chips = mesh.shape["seq"] // 2
    ny = 1 << ((n_chips.bit_length()) // 2)
    nz = n_chips // ny
    return jax.shard_map(
        functools.partial(local, ny, nz),
        mesh=mesh,
        in_specs=(
            P("seq", "head"),
            P("seq", "head"),
            P("seq", "head"),
            P("seq", "head"),
            P("head", None, None),
            P("head", None, None),
            P("head", None, None),
        ),
        out_specs=P("seq", "head"),
        check_vma=False,
    )
```

```python
import functools
import math

import jax
import jax.numpy as jnp
from jax import lax
from jax.experimental import pallas as pl
from jax.experimental.pallas import tpu as pltpu
from jax.sharding import PartitionSpec as P

T = 128
DH = 512
FH = 256
HALF = 128
LANES = 128
NL = DH // LANES
NK = 4
BLOCK = HALF // NK
ROWS = NL * 3 * BLOCK
MESH = pl.DeviceIdType.MESH
F32 = jnp.float32
BF16 = jnp.bfloat16


def dot_nt(a, b):
    return lax.dot_general(a, b, (((1,), (1,)), ((), ())), preferred_element_type=F32)


def dot_nn(a, b):
    return jnp.dot(a, b, preferred_element_type=F32)


def split(a):
    high = a.astype(BF16)
    return high, (a - high.astype(F32)).astype(BF16)


def far_first(j, n):
    h = (j + 1) // 2
    return lax.rem(n // 2 + n + jnp.where(lax.rem(j, 2) == 1, -h, h), n)


def far_offsets(n):
    return sorted(range(1, n), key=lambda d: -min(d, n - d))


def kernel(
    ny, nz,
    q_hbm, k_hbm, v_hbm, r_hbm, wg_hbm, wu_hbm, wd_hbm,
    out_ref,
    qq, kk, vv, rr, hk, hv, r_in, w_in, w_f, w_b,
    g_own, g_give, g_got, g_send0, g_send1, g_all0, g_all1,
    landz, midz, finy, landy, midy, finz, land1,
    ss_own, ss_got, attn, f_give, f_got,
    in_sem, x_send, x_recv, h_send, h_recv, gh_send, gh_recv, col_send, col_recv, fwd_send, fwd_recv,
    a_send, a_recv, b_send, b_recv, r1_send, r1_recv, y_send, y_recv, z_send, z_recv, zy_send, zy_recv,
    ss_send, ss_recv, f_send, f_recv,
):
    s = lax.axis_index("seq")
    c = lax.rem(s, 2)
    chip = s // 2
    z = lax.rem(chip, nz)
    y = chip // nz
    rows = ROWS // nz
    n_seq = ny * nz * 2
    span = y // NK
    line = y - span * NK
    partner = s + 1 - 2 * c

    def seq_at(row, column):
        return (row * nz + column) * 2 + c

    loads = [
        pltpu.make_async_copy(k_hbm, kk.at[line, c], in_sem.at[0]),
        pltpu.make_async_copy(v_hbm, vv.at[line, c], in_sem.at[1]),
        pltpu.make_async_copy(r_hbm, r_in, in_sem.at[2]),
        pltpu.make_async_copy(wg_hbm.at[0], w_in.at[0], in_sem.at[3]),
        pltpu.make_async_copy(wu_hbm.at[0], w_in.at[1], in_sem.at[4]),
        pltpu.make_async_copy(wd_hbm.at[0], w_in.at[2], in_sem.at[5]),
        pltpu.make_async_copy(q_hbm, qq.at[c], in_sem.at[6]),
    ]
    for load in loads:
        load.start()

    barrier = pltpu.get_barrier_semaphore()

    def greet(target):
        pl.semaphore_signal(barrier, inc=1, device_id={"seq": target}, device_id_type=MESH)

    for d in far_offsets(ny):
        greet(seq_at(lax.rem(y + d, ny), z))
    for d in far_offsets(nz):
        greet(seq_at(y, lax.rem(z + d, nz)))
    beside = lax.rem(s + 2 * c - 1 + n_seq, n_seq)
    greet(beside)
    greet(partner)

    for load in loads:
        load.wait()
    rr[line, c] = jnp.broadcast_to(r_in[...], (8, LANES))

    def slopes(h1, h3, dg, rate):
        sig = jax.nn.sigmoid(h1)
        s1 = h1 * sig
        a_gate = dg * h3 * sig * (1.0 + h1 * (1.0 - sig))
        return a_gate, dg * s1, (s1 * h3) * rate

    def at(m, b):
        first = (b * 3 + m) * BLOCK
        return slice(first, first + BLOCK)

    @pl.when(span == 0)
    def _():
        x, y_val = kk[line, c], vv[line, c]
        minus_r = -jnp.broadcast_to(r_in[...], (LANES, T)).T[:, 0:1]
        acts = slopes(dot_nn(x, w_in[0]), dot_nn(x, w_in[1]), dot_nn(y_val, w_in[2]) * minus_r, minus_r)
        for m in range(3):
            grad = dot_nn(acts[m].T.astype(BF16), x if m < 2 else y_val)
            low, high = grad[:HALF], grad[HALF:]
            mine = jnp.where(c == 0, low, high)
            theirs = jnp.where(c == 0, high, low).astype(BF16)
            for b in range(NL):
                for k in range(NK):
                    g_own[k, at(m, b), :] = mine[k * BLOCK:(k + 1) * BLOCK, b * LANES:(b + 1) * LANES]
                    g_give[k, at(m, b), :] = theirs[k * BLOCK:(k + 1) * BLOCK, b * LANES:(b + 1) * LANES]

    pl.semaphore_wait(barrier, ny + nz)

    def remote(src, dst, send, recv, target):
        return pltpu.make_async_remote_copy(
            src_ref=src, dst_ref=dst, send_sem=send, recv_sem=recv, device_id={"seq": target}, device_id_type=MESH
        )

    def fan(n, place, src, dst, send, recv):
        def one(i, carry):
            index, target = place(i)
            from_ref, to_ref = src(index), dst(index)

            @pl.when(target == s)
            def _():
                pltpu.make_async_copy(from_ref, to_ref, recv).start()

            @pl.when(target != s)
            def _():
                remote(from_ref, to_ref, send, recv, target).start()

            return carry

        lax.fori_loop(0, n, one, 0)

    def along_z(i):
        zt = lax.rem(z + far_first(i, nz), nz)
        return zt, seq_at(y, zt)

    def along_y(first):
        def place(i):
            k = lax.rem(line + 1 + i, NK)
            return k, seq_at(first + k, z)

        return place

    def part(column):
        return pl.ds(pl.multiple_of(column * rows, 16), rows)

    def arrived(ref, sem):
        pltpu.make_async_copy(ref, ref, sem).wait()

    def total(ref):
        out = ref[0].astype(F32)
        for i in range(1, ref.shape[0]):
            out = out + ref[i].astype(F32)
        return out.astype(BF16)

    give = remote(g_give, g_got, gh_send, gh_recv, partner)
    shares = [
        remote(ref, ref, x_send.at[i], x_recv.at[i], partner)
        for i, ref in enumerate((kk.at[line, c], vv.at[line, c], rr.at[line, c], qq.at[c]))
    ]
    halo = [
        remote(src.at[line, c], dst, h_send.at[i], h_recv.at[i], beside)
        for i, (src, dst) in enumerate(((kk, hk), (vv, hv)))
    ]
    column_of = (kk, vv, rr)

    def scatter0():
        first = y - line

        @pl.when(c == 0)
        def _():
            def send(i, carry):
                k = lax.rem(line + 1 + i, NK)
                fan(nz, along_z, lambda zt: g_send0.at[k, part(zt)], lambda zt: landz.at[k, z], a_send.at[0], a_recv.at[k])
                return carry

            lax.fori_loop(0, NK, send, 0)

        @pl.when(c == 1)
        def _():
            def send(i, carry):
                zt, _ = along_z(i)
                fan(NK, along_y(first), lambda k: g_send0.at[k, part(zt)], lambda k: landy.at[zt, line],
                    a_send.at[0], a_recv.at[zt])
                return carry

            lax.fori_loop(0, nz, send, 0)

    def scatter0_end():
        first = y - line

        @pl.when(c == 0)
        def _():
            def add(i, carry):
                k = lax.rem(line + 1 + i, NK)
                arrived(landz.at[k], a_recv.at[k])
                midz[k] = total(landz.at[k])

                @pl.when(k == line)
                def _():
                    pltpu.make_async_copy(midz.at[k], finy.at[line], b_recv).start()

                @pl.when(k != line)
                def _():
                    remote(midz.at[k], finy.at[line], b_send, b_recv, seq_at(first + k, z)).start()

                return carry

            lax.fori_loop(0, NK, add, 0)
            arrived(finy, b_recv)
            g_all0[line, part(z), :] = total(finy)

        @pl.when(c == 1)
        def _():
            def add(i, carry):
                zt, target = along_z(i)
                arrived(landy.at[zt], a_recv.at[zt])
                midy[zt] = total(landy.at[zt])

                @pl.when(zt == z)
                def _():
                    pltpu.make_async_copy(midy.at[zt], finz.at[z], b_recv).start()

                @pl.when(zt != z)
                def _():
                    remote(midy.at[zt], finz.at[z], b_send, b_recv, target).start()

                return carry

            lax.fori_loop(0, nz, add, 0)
            arrived(finz, b_recv)
            g_all0[line, part(z), :] = total(finz)

    def give_on_z(p, g_all, k):
        def one(i, carry):
            zt, target = along_z(i)
            block = g_all.at[k, part(z)]
            remote(block, block, z_send.at[p], z_recv.at[p], target).start()
            return carry

        lax.fori_loop(0, nz - 1, one, 0)

    def gather0():
        own = g_all0.at[line, part(z)]

        @pl.when(span == 0)
        def _():
            for i in range(NK):
                remote(own, own, y_send.at[0], y_recv.at[0, line], seq_at(NK + lax.rem(line + 2 + i, NK), z)).start()
            give_on_z(0, g_all0, line)
            for i in range(1, NK):
                remote(own, own, y_send.at[1], y_recv.at[0, line], seq_at(lax.rem(line + i, NK), z)).start()

        def forward(i, carry):
            k = jnp.where(span == 0, lax.rem(line + i, NK), jnp.where(y >= 6, i, NK - 1 - i))

            @pl.when((span == 1) | (k != line))
            def _():
                arrived(g_all0.at[k, part(z)], y_recv.at[0, k])
                give_on_z(0, g_all0, k)

            return carry

        lax.fori_loop(0, NK, forward, 0)

    def gather1():
        own = g_all1.at[line, part(z)]
        first = y - line

        def own_on_y(block, send, recv):
            for i in range(1, NK):
                remote(block, block, send, recv, seq_at(first + lax.rem(line + i, NK), z)).start()

        @pl.when(c == 0)
        def _():
            own_on_y(own, y_send.at[1], y_recv.at[1, line])
            give_on_z(1, g_all1, line)

            def forward(i, carry):
                k = lax.rem(line + i, NK)
                arrived(g_all1.at[k, part(z)], y_recv.at[1, k])
                give_on_z(1, g_all1, k)
                return carry

            lax.fori_loop(1, NK, forward, 0)
            arrived(g_all1.at[:, pl.ds(0, ROWS - rows)], z_recv.at[1])

        @pl.when(c == 1)
        def _():
            def one(i, carry):
                _, target = along_z(i)
                remote(own, own, zy_send.at[0], zy_recv.at[z], target).start()
                return carry

            lax.fori_loop(0, nz - 1, one, 0)
            own_on_y(own, zy_send.at[1], y_recv.at[1, 0])

            def forward(i, carry):
                zt, _ = along_z(nz - 1 - i)
                block = g_all1.at[line, part(zt)]
                arrived(block, zy_recv.at[zt])
                own_on_y(block, zy_send.at[1], y_recv.at[1, 0])
                return carry

            lax.fori_loop(1, nz, forward, 0)
            arrived(g_all1.at[pl.ds(0, NK - 1)], y_recv.at[1, 0])

    def initial_weights():
        first = pl.multiple_of(c * HALF, HALF)
        for m in range(3):
            w = w_in[m, :, pl.ds(first, HALF)].astype(F32).T
            for b in range(NL):
                for k in range(NK):
                    w_f[k, at(m, b), :] = w[k * BLOCK:(k + 1) * BLOCK, b * LANES:(b + 1) * LANES]

    def attention():
        @pl.when(c == 0)
        def _():
            for copy in halo:
                copy.wait_recv()

        @pl.when(c == 1)
        def _():
            hk[...] = kk[line, 0]
            hv[...] = vv[line, 0]

        q = qq[c]
        inv = jnp.sqrt(jnp.float32(DH))
        before = dot_nt(q, hk[...]) / inv
        here = dot_nt(q, kk[line, c]) / inv
        row = lax.broadcasted_iota(jnp.int32, (T, T), 0)
        col = lax.broadcasted_iota(jnp.int32, (T, T), 1)
        before = jnp.where((col > row) & (s > 0), before, jnp.float32(-1e30))
        here = jnp.where(col <= row, here, jnp.float32(-1e30))
        top = jnp.maximum(jnp.max(before, axis=1, keepdims=True), jnp.max(here, axis=1, keepdims=True))
        before, here = jnp.exp(before - top), jnp.exp(here - top)
        norm = jnp.sum(before, axis=1, keepdims=True) + jnp.sum(here, axis=1, keepdims=True)
        before, here = (before / norm).astype(BF16), (here / norm).astype(BF16)
        attn[...] = dot_nn(before, hv[...]) + dot_nn(here, vv[line, c])

    @pl.when(span == 0)
    def _():
        give.start()
        for share in shares:
            share.start()
        give.wait_recv()
        g_send0[...] = (g_own[...] + g_got[...].astype(F32)).astype(BF16)
        scatter0()
        initial_weights()
        for share in shares:
            share.wait_recv()
        scatter0_end()
        gather0()

        @pl.when(c == 1)
        def _():
            for copy in halo:
                copy.start()

        attention()

    @pl.when(span == 1)
    def _():
        for share in shares:
            share.start()

        @pl.when(c == 1)
        def _():
            for copy in halo:
                copy.start()

        for i in range(1, NK):
            k = lax.rem(line + i, NK)
            for j, ref in enumerate(column_of):
                own = ref.at[line, c]
                remote(own, own, col_send.at[j], col_recv.at[j, line], seq_at(NK + k, z)).start()
        initial_weights()
        for share in shares:
            share.wait_recv()
        attention()
        gather0()
        for i in range(1, NK):
            k = lax.rem(line + i, NK)
            for j, ref in enumerate(column_of):
                block = ref.at[k, c]
                arrived(block, col_recv.at[j, k])
                remote(block, block, fwd_send.at[j], fwd_recv.at[j, k], partner).start()
        for i in range(1, NK):
            k = lax.rem(line + i, NK)
            for j, ref in enumerate(column_of):
                arrived(ref.at[k, 1 - c], fwd_recv.at[j, k])

    def descend(p, g_all):
        ss_own[p] = jnp.zeros((16, LANES), F32)
        for m in range(3):
            for b in range(NL):
                g = g_all[:, at(m, b), :].astype(F32)
                ss_own[p, m * NL + b:m * NL + b + 1, :] = jnp.sum(jnp.sum(g * g, axis=0), axis=0, keepdims=True)
        swap = remote(ss_own.at[p], ss_got.at[p], ss_send.at[p], ss_recv.at[p], partner)
        swap.start()
        swap.wait()
        scale = 0.05 * lax.rsqrt((ss_own[p] + ss_got[p]) * (1.0 / FH) + 1e-06)
        for m in range(3):
            for b in range(NL):
                for k in range(NK):
                    j = m * NL + b
                    new = w_f[k, at(m, b), :] - g_all[k, at(m, b), :].astype(F32) * scale[j:j + 1]
                    w_f[k, at(m, b), :] = new
                    first = m * HALF + k * BLOCK
                    for i, term in enumerate(split(new)):
                        w_b[i, first:first + BLOCK, b * LANES:(b + 1) * LANES] = term

    arrived(g_all0.at[:, pl.ds(0, ROWS - rows)], z_recv.at[0])
    descend(0, g_all0)

    def gradient1():
        n = 2 * NK * T
        x, y_val = kk[...].reshape(n, DH), vv[...].reshape(n, DH)
        minus_r = -jnp.concatenate([rr[k, i][0:1] for k in range(NK) for i in range(2)], axis=1)

        def block(i, m):
            return w_b[i, pl.ds(pl.multiple_of(m * HALF + line * BLOCK, BLOCK), BLOCK), :]

        h = dot_nt(jnp.concatenate([block(0, 0), block(0, 1), block(1, 0), block(1, 1)], axis=0), x)
        h = h[:2 * BLOCK] + h[2 * BLOCK:]
        dg = dot_nt(jnp.concatenate([block(0, 2), block(1, 2)], axis=0), y_val)
        dg = (dg[:BLOCK] + dg[BLOCK:]) * minus_r
        a_gate, a_up, a_down = slopes(h[:BLOCK], h[BLOCK:], dg, minus_r)
        on_x = dot_nn(jnp.concatenate([a_gate, a_up], axis=0).astype(BF16), x).astype(BF16)
        on_y = dot_nn(a_down.astype(BF16), y_val).astype(BF16)
        for m, grad in enumerate((on_x[:BLOCK], on_x[BLOCK:], on_y)):
            for b in range(NL):
                g_send1[at(m, b), :] = grad[:, b * LANES:(b + 1) * LANES]

    @pl.when(span == 1)
    def _():
        gradient1()
        fan(nz, along_z, lambda zt: g_send1.at[part(zt)], lambda zt: land1.at[z], r1_send, r1_recv)
        arrived(land1, r1_recv)
        g_all1[line, part(z), :] = total(land1)
        gather1()
        descend(1, g_all1)

    def apply():
        q_all = qq[...].reshape(2 * T, DH)
        h1 = dot_nt(q_all, w_b[0, 0:HALF]) + dot_nt(q_all, w_b[1, 0:HALF])
        h3 = dot_nt(q_all, w_b[0, HALF:2 * HALF]) + dot_nt(q_all, w_b[1, HALF:2 * HALF])
        high, low = split(h1 * jax.nn.sigmoid(h1) * h3)
        w_high, w_low = w_b[0, 2 * HALF:3 * HALF], w_b[1, 2 * HALF:3 * HALF]
        f = dot_nn(high, w_high) + (dot_nn(low, w_high) + dot_nn(high, w_low))
        mine = jnp.where(c == 0, f[:T], f[T:])
        f_give[...] = jnp.where(c == 0, f[T:], f[:T])
        swap = remote(f_give, f_got, f_send, f_recv, partner)
        swap.start()
        swap.wait()
        f = mine + f_got[...]
        fast = (f * lax.rsqrt(jnp.mean(f * f, axis=1, keepdims=True) + 1e-06)).astype(BF16)
        out_ref[...] = (attn[...] + fast.astype(F32)).astype(BF16)

    apply()

    most = g_all0.at[:, pl.ds(0, ROWS - rows)]
    for share in shares:
        share.wait_send()

    @pl.when(c == 1)
    def _():
        for copy in halo:
            copy.wait_send()

    arrived(most, z_send.at[0])

    @pl.when(span == 0)
    def _():
        give.wait_send()
        arrived(landy.at[0], y_send.at[0])
        arrived(landy.at[0, pl.ds(0, NK - 1)], y_send.at[1])

        @pl.when(c == 0)
        def _():
            arrived(most, a_send.at[0])
            arrived(finy.at[pl.ds(0, NK - 1)], b_send)

        @pl.when(c == 1)
        def _():
            arrived(g_all0.at[pl.ds(0, NK - 1)], a_send.at[0])
            arrived(finz.at[pl.ds(0, nz - 1)], b_send)

    @pl.when(span == 1)
    def _():
        for j, ref in enumerate(column_of):
            arrived(ref.at[pl.ds(0, NK - 1), 0], col_send.at[j])
            arrived(ref.at[pl.ds(0, NK - 1), 0], fwd_send.at[j])
        arrived(land1.at[pl.ds(0, nz - 1)], r1_send)

        @pl.when(c == 0)
        def _():
            arrived(landy.at[0, pl.ds(0, NK - 1)], y_send.at[1])
            arrived(most, z_send.at[1])

        @pl.when(c == 1)
        def _():
            arrived(land1.at[pl.ds(0, nz - 1)], zy_send.at[0])
            arrived(g_all0.at[pl.ds(0, NK - 1)], zy_send.at[1])


def local(ny, nz, queries, keys, values, rates, gate_fast, up_fast, down_fast):
    rows = ROWS // nz
    dma = pltpu.SemaphoreType.DMA
    full = (NK, ROWS, LANES)
    return pl.pallas_call(
        functools.partial(kernel, ny, nz),
        out_shape=jax.ShapeDtypeStruct((T, DH), BF16),
        in_specs=[pl.BlockSpec(memory_space=pl.ANY)] * 7,
        out_specs=pl.BlockSpec(memory_space=pltpu.VMEM),
        scratch_shapes=[
            pltpu.VMEM((2, T, DH), BF16),
            pltpu.VMEM((NK, 2, T, DH), BF16),
            pltpu.VMEM((NK, 2, T, DH), BF16),
            pltpu.VMEM((NK, 2, 8, LANES), F32),
            pltpu.VMEM((T, DH), BF16),
            pltpu.VMEM((T, DH), BF16),
            pltpu.VMEM((1, T), F32),
            pltpu.VMEM((3, DH, FH), BF16),
            pltpu.VMEM(full, F32),
            pltpu.VMEM((2, 3 * HALF, DH), BF16),
            pltpu.VMEM(full, F32),
            pltpu.VMEM(full, BF16),
            pltpu.VMEM(full, BF16),
            pltpu.VMEM(full, BF16),
            pltpu.VMEM((ROWS, LANES), BF16),
            pltpu.VMEM(full, BF16),
            pltpu.VMEM(full, BF16),
            pltpu.VMEM((NK, nz, rows, LANES), BF16),
            pltpu.VMEM((NK, rows, LANES), BF16),
            pltpu.VMEM((NK, rows, LANES), BF16),
            pltpu.VMEM((nz, NK, rows, LANES), BF16),
            pltpu.VMEM((nz, rows, LANES), BF16),
            pltpu.VMEM((nz, rows, LANES), BF16),
            pltpu.VMEM((nz, rows, LANES), BF16),
            pltpu.VMEM((2, 16, LANES), F32),
            pltpu.VMEM((2, 16, LANES), F32),
            pltpu.VMEM((T, DH), F32),
            pltpu.VMEM((T, DH), F32),
            pltpu.VMEM((T, DH), F32),
            dma((7,)),
            dma((4,)),
            dma((4,)),
            dma((2,)),
            dma((2,)),
            dma,
            dma,
            dma((3,)),
            dma((3, NK)),
            dma((3,)),
            dma((3, NK)),
            dma((1,)),
            dma((max(NK, nz),)),
            dma,
            dma,
            dma,
            dma,
            dma((2,)),
            dma((2, NK)),
            dma((2,)),
            dma((2,)),
            dma((2,)),
            dma((nz,)),
            dma((2,)),
            dma((2,)),
            dma,
            dma,
        ],
        compiler_params=pltpu.CompilerParams(
            collective_id=0, has_side_effects=True, vmem_limit_bytes=60 * 2**20
        ),
        name="fast_layer",
    )(queries, keys, values, rates.reshape(1, T), gate_fast, up_fast, down_fast)


def solution(mesh):
    ny = 2 * NK
    nz = mesh.shape["seq"] // 2 // ny
    return jax.shard_map(
        functools.partial(local, ny, nz),
        mesh=mesh,
        in_specs=(
            P("seq", "head"),
            P("seq", "head"),
            P("seq", "head"),
            P("seq", "head"),
            P("head", None, None),
            P("head", None, None),
            P("head", None, None),
        ),
        out_specs=P("seq", "head"),
        check_vma=False,
    )
```

```python
import functools
import math

import jax
import jax.numpy as jnp
from jax import lax
from jax.experimental import pallas as pl
from jax.experimental.pallas import tpu as pltpu
from jax.sharding import PartitionSpec as P

T = 128
DH = 512
FH = 256
HALF = 128
LANES = 128
NL = DH // LANES
NK = 4
BLOCK = HALF // NK
ROWS = NL * 3 * BLOCK
MESH = pl.DeviceIdType.MESH
F32 = jnp.float32
BF16 = jnp.bfloat16


def dot_nt(a, b):
    return lax.dot_general(a, b, (((1,), (1,)), ((), ())), preferred_element_type=F32)


def dot_nn(a, b):
    return jnp.dot(a, b, preferred_element_type=F32)


def split(a):
    high = a.astype(BF16)
    return high, (a - high.astype(F32)).astype(BF16)


def far_first(j, n):
    h = (j + 1) // 2
    return lax.rem(n // 2 + n + jnp.where(lax.rem(j, 2) == 1, -h, h), n)


def far_offsets(n):
    return sorted(range(1, n), key=lambda d: -min(d, n - d))


def kernel(
    ny, nz,
    q_hbm, k_hbm, v_hbm, r_hbm, wg_hbm, wu_hbm, wd_hbm,
    out_ref,
    qq, kk, vv, rr, hk, hv, r_in, w_in, w_f, w_b,
    g_own, g_give, g_got, g_send0, g_send1, g_all0, g_all1,
    landz, midz, finy, landy, midy, finz, land1,
    ss_own, ss_got, attn, f_give, f_got,
    in_sem, x_send, x_recv, h_send, h_recv, gh_send, gh_recv, col_send, col_recv, fwd_send, fwd_recv,
    az_send, az_recv, ay_send, ay_recv, bz_send, bz_recv, by_send, by_recv, r1_send, r1_recv,
    y_send, y_recv, z_send, z_recv, zy_send, zy_recv, fy_send, fy_recv,
    ss_send, ss_recv, f_send, f_recv,
):
    s = lax.axis_index("seq")
    c = lax.rem(s, 2)
    chip = s // 2
    z = lax.rem(chip, nz)
    y = chip // nz
    rows = ROWS // nz
    n_seq = ny * nz * 2
    span = y // NK
    line = y - span * NK
    partner = s + 1 - 2 * c
    half = nz // 2
    y_first = lax.rem(z + c, 2) == 0
    up, right = lax.rem(line, 2), lax.rem(z, 2)
    group = up * 2 + right

    def seq_at(row, column):
        return (row * nz + column) * 2 + c

    loads = [
        pltpu.make_async_copy(k_hbm, kk.at[group, c], in_sem.at[0]),
        pltpu.make_async_copy(v_hbm, vv.at[group, c], in_sem.at[1]),
        pltpu.make_async_copy(r_hbm, r_in, in_sem.at[2]),
        pltpu.make_async_copy(wg_hbm.at[0], w_in.at[0], in_sem.at[3]),
        pltpu.make_async_copy(wu_hbm.at[0], w_in.at[1], in_sem.at[4]),
        pltpu.make_async_copy(wd_hbm.at[0], w_in.at[2], in_sem.at[5]),
        pltpu.make_async_copy(q_hbm, qq.at[c], in_sem.at[6]),
    ]
    for load in loads:
        load.start()

    barrier = pltpu.get_barrier_semaphore()

    def greet(target):
        pl.semaphore_signal(barrier, inc=1, device_id={"seq": target}, device_id_type=MESH)

    for d in far_offsets(ny):
        greet(seq_at(lax.rem(y + d, ny), z))
    for d in far_offsets(nz):
        greet(seq_at(y, lax.rem(z + d, nz)))
    beside = lax.rem(s + 2 * c - 1 + n_seq, n_seq)
    greet(beside)
    greet(partner)
    y_pair, z_pair = y + 1 - 2 * up, z + 1 - 2 * right
    pairs = [
        (seq_at(y_pair, z_pair), (1 - up) * 2 + 1 - right),
        (seq_at(y_pair, z), (1 - up) * 2 + right),
        (seq_at(y, z_pair), up * 2 + 1 - right),
    ]
    greet(pairs[0][0])
    other_row = y - line + lax.rem(line + 2, NK)
    for d in range(1, half):
        greet(seq_at(other_row, lax.rem(z + 2 * d, nz)))

    for load in loads:
        load.wait()
    rr[group, c] = jnp.broadcast_to(r_in[...], (8, LANES))

    def slopes(h1, h3, dg, rate):
        sig = jax.nn.sigmoid(h1)
        s1 = h1 * sig
        a_gate = dg * h3 * sig * (1.0 + h1 * (1.0 - sig))
        return a_gate, dg * s1, (s1 * h3) * rate

    def at(m, b):
        first = (b * 3 + m) * BLOCK
        return slice(first, first + BLOCK)

    @pl.when(span == 0)
    def _():
        x, y_val = kk[group, c], vv[group, c]
        minus_r = -jnp.broadcast_to(r_in[...], (LANES, T)).T[:, 0:1]
        acts = slopes(dot_nn(x, w_in[0]), dot_nn(x, w_in[1]), dot_nn(y_val, w_in[2]) * minus_r, minus_r)
        for m in range(3):
            grad = dot_nn(acts[m].T.astype(BF16), x if m < 2 else y_val)
            low, high = grad[:HALF], grad[HALF:]
            mine = jnp.where(c == 0, low, high)
            theirs = jnp.where(c == 0, high, low).astype(BF16)
            for b in range(NL):
                for k in range(NK):
                    g_own[k, at(m, b), :] = mine[k * BLOCK:(k + 1) * BLOCK, b * LANES:(b + 1) * LANES]
                    g_give[k, at(m, b), :] = theirs[k * BLOCK:(k + 1) * BLOCK, b * LANES:(b + 1) * LANES]

    pl.semaphore_wait(barrier, ny + nz + half)

    def remote(src, dst, send, recv, target):
        return pltpu.make_async_remote_copy(
            src_ref=src, dst_ref=dst, send_sem=send, recv_sem=recv, device_id={"seq": target}, device_id_type=MESH
        )

    def fan(n, place, src, dst, send, recv):
        def one(i, carry):
            index, target = place(i)
            from_ref, to_ref = src(index), dst(index)

            @pl.when(target == s)
            def _():
                pltpu.make_async_copy(from_ref, to_ref, recv).start()

            @pl.when(target != s)
            def _():
                remote(from_ref, to_ref, send, recv, target).start()

            return carry

        lax.fori_loop(0, n, one, 0)

    def along_z(i):
        zt = lax.rem(z + far_first(i, nz), nz)
        return zt, seq_at(y, zt)

    def column(i, kind):
        return 2 * lax.rem(z // 2 + far_first(i, half), half) + (c if kind == 0 else 1 - c)

    def row(i):
        return lax.rem(line + i, NK)

    def part(i):
        return pl.ds(pl.multiple_of(i * rows, 16), rows)

    def arrived(ref, sem):
        pltpu.make_async_copy(ref, ref, sem).wait()

    def total(ref):
        out = ref[0].astype(F32)
        for i in range(1, ref.shape[0]):
            out = out + ref[i].astype(F32)
        return out.astype(BF16)

    give = remote(g_give, g_got, gh_send, gh_recv, partner)
    shares = [
        remote(ref, ref, x_send.at[i], x_recv.at[i], partner)
        for i, ref in enumerate((kk.at[group, c], vv.at[group, c], rr.at[group, c], qq.at[c]))
    ]
    halo = [
        remote(src.at[group, c], dst, h_send.at[i], h_recv.at[i], beside)
        for i, (src, dst) in enumerate(((kk, hk), (vv, hv)))
    ]
    group_of = (kk, vv, rr)

    def scatter0():
        first = y - line

        def send(i, carry):
            k = row(i + 1)

            def place_z(j):
                zt = column(j, 0)
                return zt, seq_at(y, zt)

            fan(half, place_z, lambda zt: g_send0.at[k, part(zt)], lambda zt: landz.at[k, z], az_send, az_recv.at[k])
            return carry

        def send_y(i, carry):
            zt = column(i, 1)

            def place_y(j):
                k = row(j + 1)
                return k, seq_at(first + k, z)

            fan(NK, place_y, lambda k: g_send0.at[k, part(zt)], lambda k: landy.at[zt // 2, line], ay_send, ay_recv.at[zt // 2])
            return carry

        for i in range(max(NK, half)):
            if i < NK:
                send(i, 0)
            if i < half:
                send_y(i, 0)

    def scatter0_end():
        first = y - line

        def add_z(i):
            k = row(i + 1)
            arrived(landz.at[k], az_recv.at[k])
            midz[k] = total(landz.at[k])

            @pl.when(k == line)
            def _():
                pltpu.make_async_copy(midz.at[k], finy.at[line], by_recv).start()

            @pl.when(k != line)
            def _():
                remote(midz.at[k], finy.at[line], by_send, by_recv, seq_at(first + k, z)).start()

        def add_y(i):
            zt = column(i, 1)
            j = zt // 2
            arrived(landy.at[j], ay_recv.at[j])
            midy[j] = total(landy.at[j])

            @pl.when(zt == z)
            def _():
                pltpu.make_async_copy(midy.at[j], finz.at[z], bz_recv).start()

            @pl.when(zt != z)
            def _():
                remote(midy.at[j], finz.at[z], bz_send, bz_recv, seq_at(y, zt)).start()

        for i in range(max(NK, half)):
            if i < half:
                add_y(i)
            if i < NK:

                @pl.when(y_first)
                def _():
                    add_z(i)

        @pl.when(y_first)
        def _():
            arrived(finy, by_recv)
            g_all0[line, part(z), :] = total(finy)

        @pl.when(jnp.logical_not(y_first))
        def _():
            arrived(finz, bz_recv)
            g_all0[line, part(z), :] = total(finz)

    def to_z(block, send, recv):
        def one(i, carry):
            _, target = along_z(i)
            remote(block, block, send, recv, target).start()
            return carry

        lax.fori_loop(0, nz - 1, one, 0)

    def to_own_span(block, send, recv):
        for i in range(1, NK):
            remote(block, block, send, recv, seq_at(y - line + row(i), z)).start()

    def to_span1(block, send, recv):
        for i in range(NK):
            remote(block, block, send, recv, seq_at(NK + row(i + 2), z)).start()

    def gather0():
        def block(k, zt):
            return g_all0.at[k, part(zt)]

        own = block(line, z)

        def forward_z(k):
            arrived(block(k, z), y_recv.at[0, k])
            to_z(block(k, z), z_send.at[0], z_recv.at[0])

        @pl.when(span == 0)
        def _():
            @pl.when(y_first)
            def _():
                to_span1(own, y_send.at[0], y_recv.at[0, line])
                to_own_span(own, y_send.at[1], y_recv.at[0, line])

            @pl.when(jnp.logical_not(y_first))
            def _():
                to_z(own, zy_send.at[0], zy_recv.at[0, z])
                to_span1(own, fy_send.at[0], fy_recv.at[0])

            for i in range(half):
                zt = column(half - 1 - i, 1)

                @pl.when(zt != z)
                def _():
                    arrived(block(line, zt), zy_recv.at[0, zt])
                    to_span1(block(line, zt), fy_send.at[0], fy_recv.at[0])

            for i in range(half):
                to_own_span(block(line, column(i, 1)), fy_send.at[1], fy_recv.at[0])

            @pl.when(y_first)
            def _():
                to_z(own, z_send.at[0], z_recv.at[0])
                for i in range(1, NK):
                    forward_z(row(i))

        @pl.when((span == 1) & y_first)
        def _():
            for i in range(NK):
                forward_z(jnp.where(line >= 2, i, NK - 1 - i))

    def gathered(p):
        @pl.when(y_first)
        def _():
            arrived(landz.at[:, pl.ds(0, half - 1)], z_recv.at[p])

        @pl.when(jnp.logical_not(y_first))
        def _():
            arrived(landz.at[:, pl.ds(0, half)], z_recv.at[p])

    def place1(k, zt):
        return g_all1.at[lax.rem(k, 2) * 2 + lax.rem(zt, 2), part(k // 2 * half + zt // 2)]

    def gather1():
        own = place1(line, z)

        @pl.when(y_first)
        def _():
            to_own_span(own, y_send.at[0], y_recv.at[1, line])
            to_z(own, z_send.at[1], z_recv.at[1])

        @pl.when(jnp.logical_not(y_first))
        def _():
            to_z(own, zy_send.at[1], zy_recv.at[1, z])
            to_own_span(own, fy_send.at[0], fy_recv.at[1])

        for i in range(max(NK, half)):
            if i < half:
                zt = column(half - 1 - i, 1)

                @pl.when(zt != z)
                def _():
                    arrived(place1(line, zt), zy_recv.at[1, zt])
                    to_own_span(place1(line, zt), fy_send.at[0], fy_recv.at[1])

            if 1 <= i < NK:

                @pl.when(y_first)
                def _():
                    k = row(i)
                    arrived(place1(k, z), y_recv.at[1, k])
                    to_z(place1(k, z), z_send.at[1], z_recv.at[1])

    def initial_weights():
        first = pl.multiple_of(c * HALF, HALF)
        for m in range(3):
            w = w_in[m, :, pl.ds(first, HALF)].astype(F32).T
            for b in range(NL):
                for k in range(NK):
                    w_f[k, at(m, b), :] = w[k * BLOCK:(k + 1) * BLOCK, b * LANES:(b + 1) * LANES]

    def attention():
        @pl.when(c == 0)
        def _():
            for copy in halo:
                copy.wait_recv()

        @pl.when(c == 1)
        def _():
            hk[...] = kk[group, 0]
            hv[...] = vv[group, 0]

        q = qq[c]
        inv = jnp.sqrt(jnp.float32(DH))
        before = dot_nt(q, hk[...]) / inv
        here = dot_nt(q, kk[group, c]) / inv
        t_q = lax.broadcasted_iota(jnp.int32, (T, T), 0)
        t_k = lax.broadcasted_iota(jnp.int32, (T, T), 1)
        before = jnp.where((t_k > t_q) & (s > 0), before, jnp.float32(-1e30))
        here = jnp.where(t_k <= t_q, here, jnp.float32(-1e30))
        top = jnp.maximum(jnp.max(before, axis=1, keepdims=True), jnp.max(here, axis=1, keepdims=True))
        before, here = jnp.exp(before - top), jnp.exp(here - top)
        norm = jnp.sum(before, axis=1, keepdims=True) + jnp.sum(here, axis=1, keepdims=True)
        before, here = (before / norm).astype(BF16), (here / norm).astype(BF16)
        attn[...] = dot_nn(before, hv[...]) + dot_nn(here, vv[group, c])

    last_chip = chip == NK * nz - 1

    def start_halo():
        for copy in halo:
            copy.start()

    @pl.when(span == 0)
    def _():
        give.start()
        for share in shares:
            share.start()
        pl.when((c == 1) & last_chip)(start_halo)
        give.wait_recv()
        g_send0[...] = (g_own[...] + g_got[...].astype(F32)).astype(BF16)
        scatter0()
        initial_weights()
        for share in shares:
            share.wait_recv()
        scatter0_end()
        gather0()
        pl.when((c == 1) & jnp.logical_not(last_chip))(start_halo)
        attention()
        arrived(landy.at[:, pl.ds(0, NK - 1)], fy_recv.at[0])

    @pl.when(span == 1)
    def _():
        for share in shares:
            share.start()
        pl.when(c == 1)(start_halo)
        for target, _ in pairs:
            for j, ref in enumerate(group_of):
                own = ref.at[group, c]
                remote(own, own, col_send.at[j], col_recv.at[j, group], target).start()
        initial_weights()
        for share in shares:
            share.wait_recv()
        attention()
        for _, k in pairs:
            for j, ref in enumerate(group_of):
                block = ref.at[k, c]
                arrived(block, col_recv.at[j, k])
                remote(block, block, fwd_send.at[j], fwd_recv.at[j, k], partner).start()
        gather0()
        for _, k in pairs:
            for j, ref in enumerate(group_of):
                arrived(ref.at[k, 1 - c], fwd_recv.at[j, k])
        arrived(landy, fy_recv.at[0])

    def descend(p, g_all):
        ss_own[p] = jnp.zeros((16, LANES), F32)
        for m in range(3):
            for b in range(NL):
                g = g_all[:, at(m, b), :].astype(F32)
                ss_own[p, m * NL + b:m * NL + b + 1, :] = jnp.sum(jnp.sum(g * g, axis=0), axis=0, keepdims=True)
        swap = remote(ss_own.at[p], ss_got.at[p], ss_send.at[p], ss_recv.at[p], partner)
        swap.start()
        swap.wait()
        scale = 0.05 * lax.rsqrt((ss_own[p] + ss_got[p]) * (1.0 / FH) + 1e-06)
        for m in range(3):
            for b in range(NL):
                for k in range(NK):
                    j = m * NL + b
                    new = w_f[k, at(m, b), :] - g_all[k, at(m, b), :].astype(F32) * scale[j:j + 1]
                    w_f[k, at(m, b), :] = new
                    first = m * HALF + k * BLOCK
                    for i, term in enumerate(split(new)):
                        w_b[i, first:first + BLOCK, b * LANES:(b + 1) * LANES] = term

    gathered(0)
    descend(0, g_all0)

    def gradient1():
        n = 2 * NK * T
        x, y_val = kk[...].reshape(n, DH), vv[...].reshape(n, DH)
        minus_r = -jnp.concatenate([rr[k, i][0:1] for k in range(NK) for i in range(2)], axis=1)

        def block(i, m):
            return w_b[i, pl.ds(pl.multiple_of(m * HALF + group * BLOCK, BLOCK), BLOCK), :]

        h = dot_nt(jnp.concatenate([block(0, 0), block(0, 1), block(1, 0), block(1, 1)], axis=0), x)
        h = h[:2 * BLOCK] + h[2 * BLOCK:]
        dg = dot_nt(jnp.concatenate([block(0, 2), block(1, 2)], axis=0), y_val)
        dg = (dg[:BLOCK] + dg[BLOCK:]) * minus_r
        a_gate, a_up, a_down = slopes(h[:BLOCK], h[BLOCK:], dg, minus_r)
        on_x = dot_nn(jnp.concatenate([a_gate, a_up], axis=0).astype(BF16), x).astype(BF16)
        on_y = dot_nn(a_down.astype(BF16), y_val).astype(BF16)
        for m, grad in enumerate((on_x[:BLOCK], on_x[BLOCK:], on_y)):
            for b in range(NL):
                g_send1[at(m, b), :] = grad[:, b * LANES:(b + 1) * LANES]

    @pl.when(span == 1)
    def _():
        gradient1()

        def counterpart(i):
            k = lax.rem(line + 2 - 2 * lax.rem(i, 2), NK)
            zt = 2 * lax.rem(z // 2 + far_first(i // 2, half), half) + right
            return k // 2 * half + zt // 2, seq_at(NK + k, zt)

        mine = line // 2 * half + z // 2
        fan(nz, counterpart, lambda i: g_send1.at[part(i)], lambda i: land1.at[mine], r1_send, r1_recv)
        arrived(land1, r1_recv)
        g_all1[group, part(mine), :] = total(land1)
        gather1()
        arrived(landy.at[:, pl.ds(0, NK - 1)], fy_recv.at[1])
        gathered(1)
        descend(1, g_all1)

    def apply():
        q_all = qq[...].reshape(2 * T, DH)
        h1 = dot_nt(q_all, w_b[0, 0:HALF]) + dot_nt(q_all, w_b[1, 0:HALF])
        h3 = dot_nt(q_all, w_b[0, HALF:2 * HALF]) + dot_nt(q_all, w_b[1, HALF:2 * HALF])
        high, low = split(h1 * jax.nn.sigmoid(h1) * h3)
        w_high, w_low = w_b[0, 2 * HALF:3 * HALF], w_b[1, 2 * HALF:3 * HALF]
        f = dot_nn(high, w_high) + (dot_nn(low, w_high) + dot_nn(high, w_low))
        mine = jnp.where(c == 0, f[:T], f[T:])
        f_give[...] = jnp.where(c == 0, f[T:], f[:T])
        swap = remote(f_give, f_got, f_send, f_recv, partner)
        swap.start()
        swap.wait()
        f = mine + f_got[...]
        fast = (f * lax.rsqrt(jnp.mean(f * f, axis=1, keepdims=True) + 1e-06)).astype(BF16)
        out_ref[...] = (attn[...] + fast.astype(F32)).astype(BF16)

    apply()

    def left(whole, sem, one_stayed):
        @pl.when(one_stayed)
        def _():
            arrived(whole(1), sem)

        @pl.when(jnp.logical_not(one_stayed))
        def _():
            arrived(whole(0), sem)

    most = g_all0.at[:, pl.ds(0, ROWS - rows)]
    three = finy.at[pl.ds(0, NK - 1)]
    z_first = jnp.logical_not(y_first)
    for share in shares:
        share.wait_send()

    @pl.when(c == 1)
    def _():
        for copy in halo:
            copy.wait_send()

    @pl.when(y_first)
    def _():
        arrived(most, z_send.at[0])

    @pl.when(span == 0)
    def _():
        give.wait_send()
        left(lambda n: landz.at[:, pl.ds(0, half - n)], az_send, y_first)
        arrived(landy.at[:, pl.ds(0, NK - 1)], ay_send)
        left(lambda n: finz.at[pl.ds(0, half - n)], bz_send, z_first)
        arrived(landy, fy_send.at[0])
        arrived(landy.at[:, pl.ds(0, NK - 1)], fy_send.at[1])

        @pl.when(y_first)
        def _():
            arrived(three, by_send)
            arrived(finy, y_send.at[0])
            arrived(three, y_send.at[1])

        @pl.when(z_first)
        def _():
            arrived(finz.at[pl.ds(0, nz - 1)], zy_send.at[0])

    @pl.when(span == 1)
    def _():
        for j, ref in enumerate(group_of):
            arrived(ref.at[pl.ds(0, 3), 0], col_send.at[j])
            arrived(ref.at[pl.ds(0, 3), 0], fwd_send.at[j])
        arrived(land1.at[pl.ds(0, nz - 1)], r1_send)
        arrived(landy.at[:, pl.ds(0, NK - 1)], fy_send.at[0])

        @pl.when(y_first)
        def _():
            arrived(three, y_send.at[0])
            arrived(most, z_send.at[1])

        @pl.when(z_first)
        def _():
            arrived(finz.at[pl.ds(0, nz - 1)], zy_send.at[1])


def local(ny, nz, queries, keys, values, rates, gate_fast, up_fast, down_fast):
    rows = ROWS // nz
    dma = pltpu.SemaphoreType.DMA
    full = (NK, ROWS, LANES)
    return pl.pallas_call(
        functools.partial(kernel, ny, nz),
        out_shape=jax.ShapeDtypeStruct((T, DH), BF16),
        in_specs=[pl.BlockSpec(memory_space=pl.ANY)] * 7,
        out_specs=pl.BlockSpec(memory_space=pltpu.VMEM),
        scratch_shapes=[
            pltpu.VMEM((2, T, DH), BF16),
            pltpu.VMEM((NK, 2, T, DH), BF16),
            pltpu.VMEM((NK, 2, T, DH), BF16),
            pltpu.VMEM((NK, 2, 8, LANES), F32),
            pltpu.VMEM((T, DH), BF16),
            pltpu.VMEM((T, DH), BF16),
            pltpu.VMEM((1, T), F32),
            pltpu.VMEM((3, DH, FH), BF16),
            pltpu.VMEM(full, F32),
            pltpu.VMEM((2, 3 * HALF, DH), BF16),
            pltpu.VMEM(full, F32),
            pltpu.VMEM(full, BF16),
            pltpu.VMEM(full, BF16),
            pltpu.VMEM(full, BF16),
            pltpu.VMEM((ROWS, LANES), BF16),
            pltpu.VMEM(full, BF16),
            pltpu.VMEM(full, BF16),
            pltpu.VMEM((NK, nz, rows, LANES), BF16),
            pltpu.VMEM((NK, rows, LANES), BF16),
            pltpu.VMEM((NK, rows, LANES), BF16),
            pltpu.VMEM((nz // 2, NK, rows, LANES), BF16),
            pltpu.VMEM((nz // 2, rows, LANES), BF16),
            pltpu.VMEM((nz, rows, LANES), BF16),
            pltpu.VMEM((nz, rows, LANES), BF16),
            pltpu.VMEM((2, 16, LANES), F32),
            pltpu.VMEM((2, 16, LANES), F32),
            pltpu.VMEM((T, DH), F32),
            pltpu.VMEM((T, DH), F32),
            pltpu.VMEM((T, DH), F32),
            dma((7,)),
            dma((4,)),
            dma((4,)),
            dma((2,)),
            dma((2,)),
            dma,
            dma,
            dma((3,)),
            dma((3, NK)),
            dma((3,)),
            dma((3, NK)),
            dma,
            dma((NK,)),
            dma,
            dma((nz // 2,)),
            dma,
            dma,
            dma,
            dma,
            dma,
            dma,
            dma((2,)),
            dma((2, NK)),
            dma((2,)),
            dma((2,)),
            dma((2,)),
            dma((2, nz)),
            dma((2,)),
            dma((2,)),
            dma((2,)),
            dma((2,)),
            dma,
            dma,
        ],
        compiler_params=pltpu.CompilerParams(
            collective_id=0, has_side_effects=True, vmem_limit_bytes=60 * 2**20
        ),
        name="fast_layer",
    )(queries, keys, values, rates.reshape(1, T), gate_fast, up_fast, down_fast)


def solution(mesh):
    ny = 2 * NK
    nz = mesh.shape["seq"] // 2 // ny
    return jax.shard_map(
        functools.partial(local, ny, nz),
        mesh=mesh,
        in_specs=(
            P("seq", "head"),
            P("seq", "head"),
            P("seq", "head"),
            P("seq", "head"),
            P("head", None, None),
            P("head", None, None),
            P("head", None, None),
        ),
        out_specs=P("seq", "head"),
        check_vma=False,
    )
```

```python
import functools
import math

import jax
import jax.numpy as jnp
from jax import lax
from jax.experimental import pallas as pl
from jax.experimental.pallas import tpu as pltpu
from jax.sharding import PartitionSpec as P

T = 128
DH = 512
FH = 256
HALF = 128
LANES = 128
NL = DH // LANES
NK = 4
BLOCK = HALF // NK
ROWS = NL * 3 * BLOCK
MESH = pl.DeviceIdType.MESH
F32 = jnp.float32
BF16 = jnp.bfloat16


def dot_nt(a, b):
    return lax.dot_general(a, b, (((1,), (1,)), ((), ())), preferred_element_type=F32)


def dot_nn(a, b):
    return jnp.dot(a, b, preferred_element_type=F32)


def split(a):
    high = a.astype(BF16)
    return high, (a - high.astype(F32)).astype(BF16)


def far_first(j, n):
    h = (j + 1) // 2
    return lax.rem(n // 2 + n + jnp.where(lax.rem(j, 2) == 1, -h, h), n)


def far_offsets(n):
    return sorted(range(1, n), key=lambda d: -min(d, n - d))


def kernel(
    ny, nz,
    q_hbm, k_hbm, v_hbm, r_hbm, wg_hbm, wu_hbm, wd_hbm,
    out_ref,
    qq, kk, vv, rr, hk, hv, r_in, w_in, w_f, w_b,
    g_own, g_give, g_got, g_send0, g_send1, g_all0, g_all1,
    landz, midz, finy, landy, midy, finz, land1,
    ss_own, ss_got, attn, f_give, f_got,
    in_sem, x_send, x_recv, h_send, h_recv, gh_send, gh_recv, col_send, col_recv, fwd_send, fwd_recv,
    az_send, az_recv, ay_send, ay_recv, bz_send, bz_recv, by_send, by_recv, r1_send, r1_recv,
    y_send, y_recv, z_send, z_recv, zy_send, zy_recv, fy_send, fy_recv,
    ss_send, ss_recv, f_send, f_recv,
):
    s = lax.axis_index("seq")
    c = lax.rem(s, 2)
    chip = s // 2
    z = lax.rem(chip, nz)
    y = chip // nz
    rows = ROWS // nz
    n_seq = ny * nz * 2
    span = y // NK
    line = y - span * NK
    partner = s + 1 - 2 * c
    half = nz // 2
    y_first = lax.rem(z + c, 2) == 0
    fourth = nz // 4
    y_first0 = lax.rem(z + 2 * c, 4) != 3
    up, right = lax.rem(line, 2), lax.rem(z, 2)
    group = up * 2 + right

    def seq_at(row, column):
        return (row * nz + column) * 2 + c

    loads = [
        pltpu.make_async_copy(k_hbm, kk.at[group, c], in_sem.at[0]),
        pltpu.make_async_copy(v_hbm, vv.at[group, c], in_sem.at[1]),
        pltpu.make_async_copy(r_hbm, r_in, in_sem.at[2]),
        pltpu.make_async_copy(wg_hbm.at[0], w_in.at[0], in_sem.at[3]),
        pltpu.make_async_copy(wu_hbm.at[0], w_in.at[1], in_sem.at[4]),
        pltpu.make_async_copy(wd_hbm.at[0], w_in.at[2], in_sem.at[5]),
        pltpu.make_async_copy(q_hbm, qq.at[c], in_sem.at[6]),
    ]
    for load in loads:
        load.start()

    barrier = pltpu.get_barrier_semaphore()

    def greet(target):
        pl.semaphore_signal(barrier, inc=1, device_id={"seq": target}, device_id_type=MESH)

    for d in far_offsets(ny):
        greet(seq_at(lax.rem(y + d, ny), z))
    for d in far_offsets(nz):
        greet(seq_at(y, lax.rem(z + d, nz)))
    beside = lax.rem(s + 2 * c - 1 + n_seq, n_seq)
    greet(beside)
    greet(partner)
    y_pair, z_pair = y + 1 - 2 * up, z + 1 - 2 * right
    pairs = [
        (seq_at(y_pair, z_pair), (1 - up) * 2 + 1 - right),
        (seq_at(y_pair, z), (1 - up) * 2 + right),
        (seq_at(y, z_pair), up * 2 + 1 - right),
    ]
    greet(pairs[0][0])
    other_row = y - line + lax.rem(line + 2, NK)
    for d in range(1, half):
        greet(seq_at(other_row, lax.rem(z + 2 * d, nz)))

    for load in loads:
        load.wait()
    rr[group, c] = jnp.broadcast_to(r_in[...], (8, LANES))

    def slopes(h1, h3, dg, rate):
        sig = jax.nn.sigmoid(h1)
        s1 = h1 * sig
        a_gate = dg * h3 * sig * (1.0 + h1 * (1.0 - sig))
        return a_gate, dg * s1, (s1 * h3) * rate

    def at(m, b):
        first = (b * 3 + m) * BLOCK
        return slice(first, first + BLOCK)

    @pl.when(span == 0)
    def _():
        x, y_val = kk[group, c], vv[group, c]
        minus_r = -jnp.broadcast_to(r_in[...], (LANES, T)).T[:, 0:1]
        acts = slopes(dot_nn(x, w_in[0]), dot_nn(x, w_in[1]), dot_nn(y_val, w_in[2]) * minus_r, minus_r)
        for m in range(3):
            grad = dot_nn(acts[m].T.astype(BF16), x if m < 2 else y_val)
            low, high = grad[:HALF], grad[HALF:]
            mine = jnp.where(c == 0, low, high)
            theirs = jnp.where(c == 0, high, low).astype(BF16)
            for b in range(NL):
                for k in range(NK):
                    g_own[k, at(m, b), :] = mine[k * BLOCK:(k + 1) * BLOCK, b * LANES:(b + 1) * LANES]
                    g_give[k, at(m, b), :] = theirs[k * BLOCK:(k + 1) * BLOCK, b * LANES:(b + 1) * LANES]

    pl.semaphore_wait(barrier, ny + nz + half)

    def remote(src, dst, send, recv, target):
        return pltpu.make_async_remote_copy(
            src_ref=src, dst_ref=dst, send_sem=send, recv_sem=recv, device_id={"seq": target}, device_id_type=MESH
        )

    def fan(n, place, src, dst, send, recv):
        def one(i, carry):
            index, target = place(i)
            from_ref, to_ref = src(index), dst(index)

            @pl.when(target == s)
            def _():
                pltpu.make_async_copy(from_ref, to_ref, recv).start()

            @pl.when(target != s)
            def _():
                remote(from_ref, to_ref, send, recv, target).start()

            return carry

        lax.fori_loop(0, n, one, 0)

    def along_z(i):
        zt = lax.rem(z + far_first(i, nz), nz)
        return zt, seq_at(y, zt)

    def column(i, kind):
        return 2 * lax.rem(z // 2 + far_first(i, half), half) + (c if kind == 0 else 1 - c)

    def row(i):
        return lax.rem(line + i, NK)

    def part(i):
        return pl.ds(pl.multiple_of(i * rows, 16), rows)

    def arrived(ref, sem):
        pltpu.make_async_copy(ref, ref, sem).wait()

    def total(ref):
        out = ref[0].astype(F32)
        for i in range(1, ref.shape[0]):
            out = out + ref[i].astype(F32)
        return out.astype(BF16)

    give = remote(g_give, g_got, gh_send, gh_recv, partner)
    shares = [
        remote(ref, ref, x_send.at[i], x_recv.at[i], partner)
        for i, ref in enumerate((kk.at[group, c], vv.at[group, c], rr.at[group, c], qq.at[c]))
    ]
    halo = [
        remote(src.at[group, c], dst, h_send.at[i], h_recv.at[i], beside)
        for i, (src, dst) in enumerate(((kk, hk), (vv, hv)))
    ]
    group_of = (kk, vv, rr)

    def scatter0():
        first = y - line

        def send(i, carry):
            k = row(i + 1)

            def place_z(j):
                zt = column(j, 0)
                return zt, seq_at(y, zt)

            fan(half, place_z, lambda zt: g_send0.at[k, part(zt)], lambda zt: landz.at[k, z], az_send, az_recv.at[k])
            return carry

        def send_y(i, carry):
            zt = column(i, 1)

            def place_y(j):
                k = row(j + 1)
                return k, seq_at(first + k, z)

            fan(NK, place_y, lambda k: g_send0.at[k, part(zt)], lambda k: landy.at[zt // 2, line], ay_send, ay_recv.at[zt // 2])
            return carry

        for i in range(max(NK, half)):
            if i < NK:
                send(i, 0)
            if i < half:
                send_y(i, 0)

    def scatter0_end():
        first = y - line

        def add_z(i):
            k = row(i + 1)
            arrived(landz.at[k], az_recv.at[k])
            midz[k] = total(landz.at[k])

            @pl.when(k == line)
            def _():
                pltpu.make_async_copy(midz.at[k], finy.at[line], by_recv).start()

            @pl.when(k != line)
            def _():
                remote(midz.at[k], finy.at[line], by_send, by_recv, seq_at(first + k, z)).start()

        def add_y(i):
            zt = column(i, 1)
            j = zt // 2
            arrived(landy.at[j], ay_recv.at[j])
            midy[j] = total(landy.at[j])

            @pl.when(zt == z)
            def _():
                pltpu.make_async_copy(midy.at[j], finz.at[z], bz_recv).start()

            @pl.when(zt != z)
            def _():
                remote(midy.at[j], finz.at[z], bz_send, bz_recv, seq_at(y, zt)).start()

        for i in range(max(NK, half)):
            if i < half:
                add_y(i)
            if i < NK:

                @pl.when(y_first)
                def _():
                    add_z(i)

        @pl.when(y_first)
        def _():
            arrived(finy, by_recv)
            g_all0[line, part(z), :] = total(finy)

        @pl.when(jnp.logical_not(y_first))
        def _():
            arrived(finz, bz_recv)
            g_all0[line, part(z), :] = total(finz)

    def to_z(block, send, recv):
        def one(i, carry):
            _, target = along_z(i)
            remote(block, block, send, recv, target).start()
            return carry

        lax.fori_loop(0, nz - 1, one, 0)

    def to_own_span(block, send, recv):
        for i in range(1, NK):
            remote(block, block, send, recv, seq_at(y - line + row(i), z)).start()

    def to_span1(block, send, recv):
        for i in range(NK):
            remote(block, block, send, recv, seq_at(NK + row(i + 2), z)).start()

    def gather0():
        def block(k, zt):
            return g_all0.at[k, part(zt)]

        def column0(i):
            return 4 * lax.rem(z // 4 + i, fourth) + 3 - 2 * c

        own = block(line, z)

        def forward_z(k):
            arrived(block(k, z), y_recv.at[0, k])
            to_z(block(k, z), z_send.at[0], z_recv.at[0])

        @pl.when(span == 0)
        def _():
            @pl.when(y_first0)
            def _():
                to_span1(own, y_send.at[0], y_recv.at[0, line])
                to_own_span(own, y_send.at[1], y_recv.at[0, line])

            @pl.when(jnp.logical_not(y_first0))
            def _():
                to_z(own, zy_send.at[0], zy_recv.at[0, z])
                to_span1(own, fy_send.at[0], fy_recv.at[0])

            for i in range(fourth):
                zt = column0(i)

                @pl.when(zt != z)
                def _():
                    arrived(block(line, zt), zy_recv.at[0, zt])
                    to_span1(block(line, zt), fy_send.at[0], fy_recv.at[0])

            for i in range(fourth):
                to_own_span(block(line, column0(i)), fy_send.at[1], fy_recv.at[0])

            @pl.when(y_first0)
            def _():
                to_z(own, z_send.at[0], z_recv.at[0])
                for i in range(1, NK):
                    forward_z(row(i))

        @pl.when((span == 1) & y_first0)
        def _():
            for i in range(NK):
                forward_z(jnp.where(line >= 2, i, NK - 1 - i))

    def gathered(p, along_y_first, columns):
        @pl.when(along_y_first)
        def _():
            arrived(landz.at[:, pl.ds(0, columns - 1)], z_recv.at[p])

        @pl.when(jnp.logical_not(along_y_first))
        def _():
            arrived(landz.at[:, pl.ds(0, columns)], z_recv.at[p])

    def place1(k, zt):
        return g_all1.at[lax.rem(k, 2) * 2 + lax.rem(zt, 2), part(k // 2 * half + zt // 2)]

    def gather1():
        own = place1(line, z)

        @pl.when(y_first)
        def _():
            to_own_span(own, y_send.at[0], y_recv.at[1, line])
            to_z(own, z_send.at[1], z_recv.at[1])

        @pl.when(jnp.logical_not(y_first))
        def _():
            to_z(own, zy_send.at[1], zy_recv.at[1, z])
            to_own_span(own, fy_send.at[0], fy_recv.at[1])

        for i in range(max(NK, half)):
            if i < half:
                zt = column(half - 1 - i, 1)

                @pl.when(zt != z)
                def _():
                    arrived(place1(line, zt), zy_recv.at[1, zt])
                    to_own_span(place1(line, zt), fy_send.at[0], fy_recv.at[1])

            if 1 <= i < NK:

                @pl.when(y_first)
                def _():
                    k = row(i)
                    arrived(place1(k, z), y_recv.at[1, k])
                    to_z(place1(k, z), z_send.at[1], z_recv.at[1])

    def initial_weights():
        first = pl.multiple_of(c * HALF, HALF)
        for m in range(3):
            w = w_in[m, :, pl.ds(first, HALF)].astype(F32).T
            for b in range(NL):
                for k in range(NK):
                    w_f[k, at(m, b), :] = w[k * BLOCK:(k + 1) * BLOCK, b * LANES:(b + 1) * LANES]

    def attention():
        @pl.when(c == 0)
        def _():
            for copy in halo:
                copy.wait_recv()

        @pl.when(c == 1)
        def _():
            hk[...] = kk[group, 0]
            hv[...] = vv[group, 0]

        q = qq[c]
        inv = jnp.sqrt(jnp.float32(DH))
        before = dot_nt(q, hk[...]) / inv
        here = dot_nt(q, kk[group, c]) / inv
        t_q = lax.broadcasted_iota(jnp.int32, (T, T), 0)
        t_k = lax.broadcasted_iota(jnp.int32, (T, T), 1)
        before = jnp.where((t_k > t_q) & (s > 0), before, jnp.float32(-1e30))
        here = jnp.where(t_k <= t_q, here, jnp.float32(-1e30))
        top = jnp.maximum(jnp.max(before, axis=1, keepdims=True), jnp.max(here, axis=1, keepdims=True))
        before, here = jnp.exp(before - top), jnp.exp(here - top)
        norm = jnp.sum(before, axis=1, keepdims=True) + jnp.sum(here, axis=1, keepdims=True)
        before, here = (before / norm).astype(BF16), (here / norm).astype(BF16)
        attn[...] = dot_nn(before, hv[...]) + dot_nn(here, vv[group, c])

    last_chip = chip == NK * nz - 1

    def start_halo():
        for copy in halo:
            copy.start()

    @pl.when(span == 0)
    def _():
        give.start()
        for share in shares:
            share.start()
        pl.when((c == 1) & last_chip)(start_halo)
        give.wait_recv()
        g_send0[...] = (g_own[...] + g_got[...].astype(F32)).astype(BF16)
        scatter0()
        initial_weights()
        for share in shares:
            share.wait_recv()
        scatter0_end()
        gather0()
        pl.when((c == 1) & jnp.logical_not(last_chip))(start_halo)
        attention()
        arrived(landy.at[pl.ds(0, fourth), pl.ds(0, NK - 1)], fy_recv.at[0])

    @pl.when(span == 1)
    def _():
        for share in shares:
            share.start()
        pl.when(c == 1)(start_halo)
        for target, _ in pairs:
            for j, ref in enumerate(group_of):
                own = ref.at[group, c]
                remote(own, own, col_send.at[j], col_recv.at[j, group], target).start()
        initial_weights()
        gather0()
        for _, k in pairs:
            for j, ref in enumerate(group_of):
                block = ref.at[k, c]
                arrived(block, col_recv.at[j, k])
                remote(block, block, fwd_send.at[j], fwd_recv.at[j, k], partner).start()
        for share in shares:
            share.wait_recv()
        attention()
        for _, k in pairs:
            for j, ref in enumerate(group_of):
                arrived(ref.at[k, 1 - c], fwd_recv.at[j, k])
        arrived(landy.at[pl.ds(0, fourth)], fy_recv.at[0])

    def row_scales(p, g_all):
        ss_own[p] = jnp.zeros((16, LANES), F32)
        for m in range(3):
            for b in range(NL):
                g = g_all[:, at(m, b), :].astype(F32)
                ss_own[p, m * NL + b:m * NL + b + 1, :] = jnp.sum(jnp.sum(g * g, axis=0), axis=0, keepdims=True)
        swap = remote(ss_own.at[p], ss_got.at[p], ss_send.at[p], ss_recv.at[p], partner)
        swap.start()
        swap.wait()

    def descend(p, g_all, blocks):
        scale = 0.05 * lax.rsqrt((ss_own[p] + ss_got[p]) * (1.0 / FH) + 1e-06)
        for k in blocks:
            for m in range(3):
                for b in range(NL):
                    j = m * NL + b
                    new = w_f[k, at(m, b), :] - g_all[k, at(m, b), :].astype(F32) * scale[j:j + 1]
                    w_f[k, at(m, b), :] = new
                    first = m * HALF + k * BLOCK
                    place = slice(first, first + BLOCK) if isinstance(k, int) else pl.ds(pl.multiple_of(first, BLOCK), BLOCK)
                    for i, term in enumerate(split(new)):
                        w_b[i, place, b * LANES:(b + 1) * LANES] = term

    gathered(0, y_first0, nz - fourth)
    row_scales(0, g_all0)

    @pl.when(span == 0)
    def _():
        descend(0, g_all0, range(NK))

    def gradient1():
        n = 2 * NK * T
        x, y_val = kk[...].reshape(n, DH), vv[...].reshape(n, DH)
        minus_r = -jnp.concatenate([rr[k, i][0:1] for k in range(NK) for i in range(2)], axis=1)

        def block(i, m):
            return w_b[i, pl.ds(pl.multiple_of(m * HALF + group * BLOCK, BLOCK), BLOCK), :]

        h = dot_nt(jnp.concatenate([block(0, 0), block(0, 1), block(1, 0), block(1, 1)], axis=0), x)
        h = h[:2 * BLOCK] + h[2 * BLOCK:]
        dg = dot_nt(jnp.concatenate([block(0, 2), block(1, 2)], axis=0), y_val)
        dg = (dg[:BLOCK] + dg[BLOCK:]) * minus_r
        a_gate, a_up, a_down = slopes(h[:BLOCK], h[BLOCK:], dg, minus_r)
        on_x = dot_nn(jnp.concatenate([a_gate, a_up], axis=0).astype(BF16), x).astype(BF16)
        on_y = dot_nn(a_down.astype(BF16), y_val).astype(BF16)
        for m, grad in enumerate((on_x[:BLOCK], on_x[BLOCK:], on_y)):
            for b in range(NL):
                g_send1[at(m, b), :] = grad[:, b * LANES:(b + 1) * LANES]

    @pl.when(span == 1)
    def _():
        descend(0, g_all0, [group])
        gradient1()

        def counterpart(i):
            k = lax.rem(line + 2 - 2 * lax.rem(i, 2), NK)
            zt = 2 * lax.rem(z // 2 + far_first(i // 2, half), half) + right
            return k // 2 * half + zt // 2, seq_at(NK + k, zt)

        mine = line // 2 * half + z // 2
        fan(nz, counterpart, lambda i: g_send1.at[part(i)], lambda i: land1.at[mine], r1_send, r1_recv)
        descend(0, g_all0, [lax.rem(group + i, NK) for i in range(1, NK)])
        arrived(land1, r1_recv)
        g_all1[group, part(mine), :] = total(land1)
        gather1()
        arrived(landy.at[:, pl.ds(0, NK - 1)], fy_recv.at[1])
        gathered(1, y_first, half)
        row_scales(1, g_all1)
        descend(1, g_all1, range(NK))

    def apply():
        def half_sum(q):
            h1 = dot_nt(q, w_b[0, 0:HALF]) + dot_nt(q, w_b[1, 0:HALF])
            h3 = dot_nt(q, w_b[0, HALF:2 * HALF]) + dot_nt(q, w_b[1, HALF:2 * HALF])
            high, low = split(h1 * jax.nn.sigmoid(h1) * h3)
            w_high, w_low = w_b[0, 2 * HALF:3 * HALF], w_b[1, 2 * HALF:3 * HALF]
            return dot_nn(high, w_high) + (dot_nn(low, w_high) + dot_nn(high, w_low))

        f_give[...] = half_sum(qq[1 - c])
        swap = remote(f_give, f_got, f_send, f_recv, partner)
        swap.start()
        mine = half_sum(qq[c])
        swap.wait()
        f = mine + f_got[...]
        fast = (f * lax.rsqrt(jnp.mean(f * f, axis=1, keepdims=True) + 1e-06)).astype(BF16)
        out_ref[...] = (attn[...] + fast.astype(F32)).astype(BF16)

    apply()

    def left(whole, sem, one_stayed):
        @pl.when(one_stayed)
        def _():
            arrived(whole(1), sem)

        @pl.when(jnp.logical_not(one_stayed))
        def _():
            arrived(whole(0), sem)

    most = g_all0.at[:, pl.ds(0, ROWS - rows)]
    three = finy.at[pl.ds(0, NK - 1)]
    z_first = jnp.logical_not(y_first)
    for share in shares:
        share.wait_send()

    @pl.when(c == 1)
    def _():
        for copy in halo:
            copy.wait_send()

    @pl.when(y_first0)
    def _():
        arrived(most, z_send.at[0])

    @pl.when(span == 0)
    def _():
        give.wait_send()
        left(lambda n: landz.at[:, pl.ds(0, half - n)], az_send, y_first)
        arrived(landy.at[:, pl.ds(0, NK - 1)], ay_send)
        left(lambda n: finz.at[pl.ds(0, half - n)], bz_send, z_first)
        arrived(landy.at[pl.ds(0, fourth)], fy_send.at[0])
        arrived(landy.at[pl.ds(0, fourth), pl.ds(0, NK - 1)], fy_send.at[1])

        @pl.when(y_first)
        def _():
            arrived(three, by_send)

        @pl.when(y_first0)
        def _():
            arrived(finy, y_send.at[0])
            arrived(three, y_send.at[1])

        @pl.when(jnp.logical_not(y_first0))
        def _():
            arrived(finz.at[pl.ds(0, nz - 1)], zy_send.at[0])

    @pl.when(span == 1)
    def _():
        for j, ref in enumerate(group_of):
            arrived(ref.at[pl.ds(0, 3), 0], col_send.at[j])
            arrived(ref.at[pl.ds(0, 3), 0], fwd_send.at[j])
        arrived(land1.at[pl.ds(0, nz - 1)], r1_send)
        arrived(landy.at[:, pl.ds(0, NK - 1)], fy_send.at[0])

        @pl.when(y_first)
        def _():
            arrived(three, y_send.at[0])
            arrived(most, z_send.at[1])

        @pl.when(z_first)
        def _():
            arrived(finz.at[pl.ds(0, nz - 1)], zy_send.at[1])


def local(ny, nz, queries, keys, values, rates, gate_fast, up_fast, down_fast):
    rows = ROWS // nz
    dma = pltpu.SemaphoreType.DMA
    full = (NK, ROWS, LANES)
    return pl.pallas_call(
        functools.partial(kernel, ny, nz),
        out_shape=jax.ShapeDtypeStruct((T, DH), BF16),
        in_specs=[pl.BlockSpec(memory_space=pl.ANY)] * 7,
        out_specs=pl.BlockSpec(memory_space=pltpu.VMEM),
        scratch_shapes=[
            pltpu.VMEM((2, T, DH), BF16),
            pltpu.VMEM((NK, 2, T, DH), BF16),
            pltpu.VMEM((NK, 2, T, DH), BF16),
            pltpu.VMEM((NK, 2, 8, LANES), F32),
            pltpu.VMEM((T, DH), BF16),
            pltpu.VMEM((T, DH), BF16),
            pltpu.VMEM((1, T), F32),
            pltpu.VMEM((3, DH, FH), BF16),
            pltpu.VMEM(full, F32),
            pltpu.VMEM((2, 3 * HALF, DH), BF16),
            pltpu.VMEM(full, F32),
            pltpu.VMEM(full, BF16),
            pltpu.VMEM(full, BF16),
            pltpu.VMEM(full, BF16),
            pltpu.VMEM((ROWS, LANES), BF16),
            pltpu.VMEM(full, BF16),
            pltpu.VMEM(full, BF16),
            pltpu.VMEM((NK, nz, rows, LANES), BF16),
            pltpu.VMEM((NK, rows, LANES), BF16),
            pltpu.VMEM((NK, rows, LANES), BF16),
            pltpu.VMEM((nz // 2, NK, rows, LANES), BF16),
            pltpu.VMEM((nz // 2, rows, LANES), BF16),
            pltpu.VMEM((nz, rows, LANES), BF16),
            pltpu.VMEM((nz, rows, LANES), BF16),
            pltpu.VMEM((2, 16, LANES), F32),
            pltpu.VMEM((2, 16, LANES), F32),
            pltpu.VMEM((T, DH), F32),
            pltpu.VMEM((T, DH), F32),
            pltpu.VMEM((T, DH), F32),
            dma((7,)),
            dma((4,)),
            dma((4,)),
            dma((2,)),
            dma((2,)),
            dma,
            dma,
            dma((3,)),
            dma((3, NK)),
            dma((3,)),
            dma((3, NK)),
            dma,
            dma((NK,)),
            dma,
            dma((nz // 2,)),
            dma,
            dma,
            dma,
            dma,
            dma,
            dma,
            dma((2,)),
            dma((2, NK)),
            dma((2,)),
            dma((2,)),
            dma((2,)),
            dma((2, nz)),
            dma((2,)),
            dma((2,)),
            dma((2,)),
            dma((2,)),
            dma,
            dma,
        ],
        compiler_params=pltpu.CompilerParams(
            collective_id=0, has_side_effects=True, vmem_limit_bytes=60 * 2**20
        ),
        name="fast_layer",
    )(queries, keys, values, rates.reshape(1, T), gate_fast, up_fast, down_fast)


def solution(mesh):
    ny = 2 * NK
    nz = mesh.shape["seq"] // 2 // ny
    return jax.shard_map(
        functools.partial(local, ny, nz),
        mesh=mesh,
        in_specs=(
            P("seq", "head"),
            P("seq", "head"),
            P("seq", "head"),
            P("seq", "head"),
            P("head", None, None),
            P("head", None, None),
            P("head", None, None),
        ),
        out_specs=P("seq", "head"),
        check_vma=False,
    )
```

```python
import functools
import math

import jax
import jax.numpy as jnp
from jax import lax
from jax.experimental import pallas as pl
from jax.experimental.pallas import tpu as pltpu
from jax.sharding import PartitionSpec as P

T = 128
DH = 512
FH = 256
HALF = 128
LANES = 128
NL = DH // LANES
NK = 4
BLOCK = HALF // NK
ROWS = NL * 3 * BLOCK
MESH = pl.DeviceIdType.MESH
F32 = jnp.float32
BF16 = jnp.bfloat16


def dot_nt(a, b):
    return lax.dot_general(a, b, (((1,), (1,)), ((), ())), preferred_element_type=F32)


def dot_nn(a, b):
    return jnp.dot(a, b, preferred_element_type=F32)


def split(a):
    high = a.astype(BF16)
    return high, (a - high.astype(F32)).astype(BF16)


def far_first(j, n):
    h = (j + 1) // 2
    return lax.rem(n // 2 + n + jnp.where(lax.rem(j, 2) == 1, -h, h), n)


def far_offsets(n):
    return sorted(range(1, n), key=lambda d: -min(d, n - d))


def kernel(
    ny, nz,
    q_hbm, k_hbm, v_hbm, r_hbm, wg_hbm, wu_hbm, wd_hbm,
    out_ref,
    qq, kk, vv, rr, hk, hv, r_in, w_in, w_f, w_b,
    g_own, g_give, g_got, g_send0, g_send1, g_all0, g_all1,
    landz, midz, landp, finy, landy, midy, finz, land1,
    ss_own, ss_got, attn, f_give, f_got,
    in_sem, x_send, x_recv, h_send, h_recv, gh_send, gh_recv, col_send, col_recv, fwd_send, fwd_recv,
    az_send, az_recv, ay_send, ay_recv, bz_send, bz_recv, p_send, p_recv, r1_send, r1_recv,
    y_send, y_recv, z_send, z_recv, zy_send, zy_recv, fy_send, fy_recv,
    ss_send, ss_recv, f_send, f_recv,
):
    s = lax.axis_index("seq")
    c = lax.rem(s, 2)
    chip = s // 2
    z = lax.rem(chip, nz)
    y = chip // nz
    rows = ROWS // nz
    n_seq = ny * nz * 2
    span = y // NK
    line = y - span * NK
    partner = s + 1 - 2 * c
    half = nz // 2
    y_first = lax.rem(z + c, 2) == 0
    fourth = nz // 4
    y_first0 = lax.rem(z + c, 4) != 3
    up, right = lax.rem(line, 2), lax.rem(z, 2)
    group = up * 2 + right

    def seq_at(row, column):
        return (row * nz + column) * 2 + c

    loads = [
        pltpu.make_async_copy(k_hbm, kk.at[group, c], in_sem.at[0]),
        pltpu.make_async_copy(v_hbm, vv.at[group, c], in_sem.at[1]),
        pltpu.make_async_copy(r_hbm, r_in, in_sem.at[2]),
        pltpu.make_async_copy(wg_hbm.at[0], w_in.at[0], in_sem.at[3]),
        pltpu.make_async_copy(wu_hbm.at[0], w_in.at[1], in_sem.at[4]),
        pltpu.make_async_copy(wd_hbm.at[0], w_in.at[2], in_sem.at[5]),
        pltpu.make_async_copy(q_hbm, qq.at[c], in_sem.at[6]),
    ]
    for load in loads:
        load.start()

    barrier = pltpu.get_barrier_semaphore()

    def greet(target):
        pl.semaphore_signal(barrier, inc=1, device_id={"seq": target}, device_id_type=MESH)

    for d in far_offsets(ny):
        greet(seq_at(lax.rem(y + d, ny), z))
    for d in far_offsets(nz):
        greet(seq_at(y, lax.rem(z + d, nz)))
    beside = lax.rem(s + 2 * c - 1 + n_seq, n_seq)
    greet(beside)
    greet(partner)
    y_pair, z_pair = y + 1 - 2 * up, z + 1 - 2 * right
    pairs = [
        (seq_at(y_pair, z_pair), (1 - up) * 2 + 1 - right),
        (seq_at(y_pair, z), (1 - up) * 2 + right),
        (seq_at(y, z_pair), up * 2 + 1 - right),
    ]
    greet(pairs[0][0])
    other_row = y - line + lax.rem(line + 2, NK)
    for d in range(1, half):
        greet(seq_at(other_row, lax.rem(z + 2 * d, nz)))

    for load in loads:
        load.wait()
    rr[group, c] = jnp.broadcast_to(r_in[...], (8, LANES))

    def slopes(h1, h3, dg, rate):
        sig = jax.nn.sigmoid(h1)
        s1 = h1 * sig
        a_gate = dg * h3 * sig * (1.0 + h1 * (1.0 - sig))
        return a_gate, dg * s1, (s1 * h3) * rate

    def at(m, b):
        first = (b * 3 + m) * BLOCK
        return slice(first, first + BLOCK)

    @pl.when(span == 0)
    def _():
        x, y_val = kk[group, c], vv[group, c]
        minus_r = -jnp.broadcast_to(r_in[...], (LANES, T)).T[:, 0:1]
        acts = slopes(dot_nn(x, w_in[0]), dot_nn(x, w_in[1]), dot_nn(y_val, w_in[2]) * minus_r, minus_r)
        for m in range(3):
            grad = dot_nn(acts[m].T.astype(BF16), x if m < 2 else y_val)
            low, high = grad[:HALF], grad[HALF:]
            mine = jnp.where(c == 0, low, high)
            theirs = jnp.where(c == 0, high, low).astype(BF16)
            for b in range(NL):
                for k in range(NK):
                    g_own[k, at(m, b), :] = mine[k * BLOCK:(k + 1) * BLOCK, b * LANES:(b + 1) * LANES]
                    g_give[k, at(m, b), :] = theirs[k * BLOCK:(k + 1) * BLOCK, b * LANES:(b + 1) * LANES]

    pl.semaphore_wait(barrier, ny + nz + half)

    def remote(src, dst, send, recv, target):
        return pltpu.make_async_remote_copy(
            src_ref=src, dst_ref=dst, send_sem=send, recv_sem=recv, device_id={"seq": target}, device_id_type=MESH
        )

    def fan(n, place, src, dst, send, recv):
        def one(i, carry):
            index, target = place(i)
            from_ref, to_ref = src(index), dst(index)

            @pl.when(target == s)
            def _():
                pltpu.make_async_copy(from_ref, to_ref, recv).start()

            @pl.when(target != s)
            def _():
                remote(from_ref, to_ref, send, recv, target).start()

            return carry

        lax.fori_loop(0, n, one, 0)

    def along_z(i):
        zt = lax.rem(z + far_first(i, nz), nz)
        return zt, seq_at(y, zt)

    def column(i, kind):
        return 2 * lax.rem(z // 2 + far_first(i, half), half) + (c if kind == 0 else 1 - c)

    def row(i):
        return lax.rem(line + i, NK)

    def near(i):
        back = line >= 2
        me = jnp.where(back, NK - 1 - line, line)
        k = i - 1 + (i - 1 >= me).astype(jnp.int32)
        return jnp.where(back, NK - 1 - k, k)

    def part(i):
        return pl.ds(pl.multiple_of(i * rows, 16), rows)

    def arrived(ref, sem):
        pltpu.make_async_copy(ref, ref, sem).wait()

    def total(ref):
        out = ref[0].astype(F32)
        for i in range(1, ref.shape[0]):
            out = out + ref[i].astype(F32)
        return out.astype(BF16)

    give = remote(g_give, g_got, gh_send, gh_recv, partner)
    shares = [
        remote(ref, ref, x_send.at[i], x_recv.at[i], partner)
        for i, ref in enumerate((kk.at[group, c], vv.at[group, c], rr.at[group, c], qq.at[c]))
    ]
    halo = [
        remote(src.at[group, c], dst, h_send.at[i], h_recv.at[i], beside)
        for i, (src, dst) in enumerate(((kk, hk), (vv, hv)))
    ]
    group_of = (kk, vv, rr)

    def scatter0():
        first = y - line

        def send(i, carry):
            k = i

            def place_z(j):
                zt = column(j, 0)
                return zt, seq_at(y, zt)

            fan(half, place_z, lambda zt: g_send0.at[k, part(zt)], lambda zt: landz.at[k, z], az_send, az_recv.at[k])
            return carry

        def send_y(i, carry):
            zt = column(i, 1)

            def place_y(j):
                k = row(j + 1)
                return k, seq_at(first + k, z)

            fan(NK, place_y, lambda k: g_send0.at[k, part(zt)], lambda k: landy.at[zt // 2, line], ay_send, ay_recv.at[zt // 2])
            return carry

        for i in range(max(NK, half)):
            if i < NK:
                send(i, 0)
            if i < half:
                send_y(i, 0)

    def scatter0_end():
        def add_z(k):
            arrived(landz.at[k], az_recv.at[k])
            midz[k] = total(landz.at[k])
            pltpu.make_async_copy(midz.at[k], landp.at[k, line], p_recv.at[k]).start()
            for i in range(NK):
                remote(midz.at[k], landp.at[k, line], p_send.at[0], p_recv.at[k], seq_at(NK + row(i + 2), z)).start()

        def add_y(i):
            zt = column(i, 1)
            j = zt // 2
            arrived(landy.at[j], ay_recv.at[j])
            midy[j] = total(landy.at[j])

            @pl.when(zt == z)
            def _():
                pltpu.make_async_copy(midy.at[j], finz.at[z], bz_recv).start()

            @pl.when(zt != z)
            def _():
                remote(midy.at[j], finz.at[z], bz_send, bz_recv, seq_at(y, zt)).start()

        for i in range(max(NK, half)):
            if i < half:
                add_y(i)
            if i < NK:

                @pl.when(y_first)
                def _():
                    add_z(i)

        @pl.when(jnp.logical_not(y_first))
        def _():
            arrived(finz, bz_recv)
            g_all0[line, part(z), :] = total(finz)

    def to_z(block, send, recv):
        def one(i, carry):
            _, target = along_z(i)
            remote(block, block, send, recv, target).start()
            return carry

        lax.fori_loop(0, nz - 1, one, 0)

    def to_own_span(block, send, recv):
        for i in range(NK - 1, 0, -1):
            remote(block, block, send, recv, seq_at(y - line + near(i), z)).start()

    def to_span1(block, send, recv):
        for i in range(NK):
            remote(block, block, send, recv, seq_at(NK + row(i + 2), z)).start()

    def gather0():
        def block(k, zt):
            return g_all0.at[k, part(zt)]

        def column0(i):
            return 4 * lax.rem(z // 4 + i, fourth) + 3 - c

        own = block(line, z)

        def forward_z(k):
            arrived(block(k, z), y_recv.at[0, k])
            to_z(block(k, z), z_send.at[0], z_recv.at[0])

        def add_rows(k):
            arrived(landp.at[k], p_recv.at[k])
            g_all0[k, part(z), :] = total(landp.at[k])
            to_z(block(k, z), z_send.at[0], z_recv.at[0])

        owner_y = y_first0 & jnp.logical_not(y_first)

        @pl.when(span == 0)
        def _():
            @pl.when(owner_y)
            def _():
                to_span1(own, y_send.at[0], y_recv.at[0, line])
                to_own_span(own, y_send.at[1], y_recv.at[0, line])

            @pl.when(jnp.logical_not(y_first0))
            def _():
                to_z(own, zy_send.at[0], zy_recv.at[0, z])
                to_span1(own, fy_send.at[0], fy_recv.at[0])

            for i in range(fourth):
                zt = column0(i)

                @pl.when(zt != z)
                def _():
                    arrived(block(line, zt), zy_recv.at[0, zt])
                    to_span1(block(line, zt), fy_send.at[0], fy_recv.at[0])

            for i in range(fourth):
                to_own_span(block(line, column0(i)), fy_send.at[1], fy_recv.at[0])

            @pl.when(y_first)
            def _():
                for k in range(NK):
                    for i in range(1, NK):
                        remote(midz.at[k], landp.at[k, line], p_send.at[1], p_recv.at[k], seq_at(row(i), z)).start()

            @pl.when(owner_y)
            def _():
                to_z(own, z_send.at[0], z_recv.at[0])
                for i in range(1, NK):
                    forward_z(row(i))

        @pl.when((span == 1) & owner_y)
        def _():
            for i in range(NK):
                forward_z(jnp.where(line >= 2, i, NK - 1 - i))

        @pl.when(y_first)
        def _():
            for k in range(NK):
                add_rows(k)

    def gathered(p, along_y_first, columns):
        @pl.when(along_y_first)
        def _():
            arrived(landz.at[:, pl.ds(0, columns - 1)], z_recv.at[p])

        @pl.when(jnp.logical_not(along_y_first))
        def _():
            arrived(landz.at[:, pl.ds(0, columns)], z_recv.at[p])

    def place1(k, zt):
        return g_all1.at[lax.rem(k, 2) * 2 + lax.rem(zt, 2), part(k // 2 * half + zt // 2)]

    def gather1():
        own = place1(line, z)

        @pl.when(y_first)
        def _():
            to_own_span(own, y_send.at[0], y_recv.at[1, line])
            to_z(own, z_send.at[1], z_recv.at[1])

        @pl.when(jnp.logical_not(y_first))
        def _():
            to_z(own, zy_send.at[1], zy_recv.at[1, z])
            to_own_span(own, fy_send.at[0], fy_recv.at[1])

        for i in range(max(NK, half)):
            if i < half:
                zt = column(half - 1 - i, 1)

                @pl.when(zt != z)
                def _():
                    arrived(place1(line, zt), zy_recv.at[1, zt])
                    to_own_span(place1(line, zt), fy_send.at[0], fy_recv.at[1])

            if 1 <= i < NK:

                @pl.when(y_first)
                def _():
                    k = near(i)
                    arrived(place1(k, z), y_recv.at[1, k])
                    to_z(place1(k, z), z_send.at[1], z_recv.at[1])

    def initial_weights():
        first = pl.multiple_of(c * HALF, HALF)
        for m in range(3):
            w = w_in[m, :, pl.ds(first, HALF)].astype(F32).T
            for b in range(NL):
                for k in range(NK):
                    w_f[k, at(m, b), :] = w[k * BLOCK:(k + 1) * BLOCK, b * LANES:(b + 1) * LANES]

    def attention():
        @pl.when(c == 0)
        def _():
            for copy in halo:
                copy.wait_recv()

        @pl.when(c == 1)
        def _():
            hk[...] = kk[group, 0]
            hv[...] = vv[group, 0]

        q = qq[c]
        inv = jnp.sqrt(jnp.float32(DH))
        before = dot_nt(q, hk[...]) / inv
        here = dot_nt(q, kk[group, c]) / inv
        t_q = lax.broadcasted_iota(jnp.int32, (T, T), 0)
        t_k = lax.broadcasted_iota(jnp.int32, (T, T), 1)
        before = jnp.where((t_k > t_q) & (s > 0), before, jnp.float32(-1e30))
        here = jnp.where(t_k <= t_q, here, jnp.float32(-1e30))
        top = jnp.maximum(jnp.max(before, axis=1, keepdims=True), jnp.max(here, axis=1, keepdims=True))
        before, here = jnp.exp(before - top), jnp.exp(here - top)
        norm = jnp.sum(before, axis=1, keepdims=True) + jnp.sum(here, axis=1, keepdims=True)
        before, here = (before / norm).astype(BF16), (here / norm).astype(BF16)
        attn[...] = dot_nn(before, hv[...]) + dot_nn(here, vv[group, c])

    last_chip = chip == NK * nz - 1

    def start_halo():
        for copy in halo:
            copy.start()

    @pl.when(span == 0)
    def _():
        give.start()
        for share in shares:
            share.start()
        pl.when((c == 1) & last_chip)(start_halo)
        give.wait_recv()
        g_send0[...] = (g_own[...] + g_got[...].astype(F32)).astype(BF16)
        scatter0()
        initial_weights()
        for share in shares:
            share.wait_recv()
        scatter0_end()
        gather0()
        pl.when((c == 1) & jnp.logical_not(last_chip))(start_halo)
        attention()
        arrived(landy.at[pl.ds(0, fourth), pl.ds(0, NK - 1)], fy_recv.at[0])

    @pl.when(span == 1)
    def _():
        for share in shares:
            share.start()
        pl.when(c == 1)(start_halo)
        for target, _ in pairs:
            for j, ref in enumerate(group_of):
                own = ref.at[group, c]
                remote(own, own, col_send.at[j], col_recv.at[j, group], target).start()
        initial_weights()
        gather0()
        for _, k in pairs:
            for j, ref in enumerate(group_of):
                block = ref.at[k, c]
                arrived(block, col_recv.at[j, k])
                remote(block, block, fwd_send.at[j], fwd_recv.at[j, k], partner).start()
        for share in shares:
            share.wait_recv()
        attention()
        for _, k in pairs:
            for j, ref in enumerate(group_of):
                arrived(ref.at[k, 1 - c], fwd_recv.at[j, k])
        arrived(landy.at[pl.ds(0, fourth)], fy_recv.at[0])

    def row_scales(p, g_all):
        ss_own[p] = jnp.zeros((16, LANES), F32)
        for m in range(3):
            for b in range(NL):
                g = g_all[:, at(m, b), :].astype(F32)
                ss_own[p, m * NL + b:m * NL + b + 1, :] = jnp.sum(jnp.sum(g * g, axis=0), axis=0, keepdims=True)
        swap = remote(ss_own.at[p], ss_got.at[p], ss_send.at[p], ss_recv.at[p], partner)
        swap.start()
        swap.wait()

    def descend(p, g_all, blocks):
        scale = 0.05 * lax.rsqrt((ss_own[p] + ss_got[p]) * (1.0 / FH) + 1e-06)
        for k in blocks:
            for m in range(3):
                for b in range(NL):
                    j = m * NL + b
                    new = w_f[k, at(m, b), :] - g_all[k, at(m, b), :].astype(F32) * scale[j:j + 1]
                    w_f[k, at(m, b), :] = new
                    first = m * HALF + k * BLOCK
                    place = slice(first, first + BLOCK) if isinstance(k, int) else pl.ds(pl.multiple_of(first, BLOCK), BLOCK)
                    for i, term in enumerate(split(new)):
                        w_b[i, place, b * LANES:(b + 1) * LANES] = term

    gathered(0, y_first0, nz - fourth)
    row_scales(0, g_all0)

    @pl.when(span == 0)
    def _():
        descend(0, g_all0, range(NK))

    def gradient1():
        n = 2 * NK * T
        x, y_val = kk[...].reshape(n, DH), vv[...].reshape(n, DH)
        minus_r = -jnp.concatenate([rr[k, i][0:1] for k in range(NK) for i in range(2)], axis=1)

        def block(i, m):
            return w_b[i, pl.ds(pl.multiple_of(m * HALF + group * BLOCK, BLOCK), BLOCK), :]

        h = dot_nt(jnp.concatenate([block(0, 0), block(0, 1), block(1, 0), block(1, 1)], axis=0), x)
        h = h[:2 * BLOCK] + h[2 * BLOCK:]
        dg = dot_nt(jnp.concatenate([block(0, 2), block(1, 2)], axis=0), y_val)
        dg = (dg[:BLOCK] + dg[BLOCK:]) * minus_r
        a_gate, a_up, a_down = slopes(h[:BLOCK], h[BLOCK:], dg, minus_r)
        on_x = dot_nn(jnp.concatenate([a_gate, a_up], axis=0).astype(BF16), x).astype(BF16)
        on_y = dot_nn(a_down.astype(BF16), y_val).astype(BF16)
        for m, grad in enumerate((on_x[:BLOCK], on_x[BLOCK:], on_y)):
            for b in range(NL):
                g_send1[at(m, b), :] = grad[:, b * LANES:(b + 1) * LANES]

    @pl.when(span == 1)
    def _():
        descend(0, g_all0, [group])
        gradient1()

        def counterpart(i):
            k = lax.rem(line + 2 - 2 * lax.rem(i, 2), NK)
            zt = 2 * lax.rem(z // 2 + far_first(i // 2, half), half) + right
            return k // 2 * half + zt // 2, seq_at(NK + k, zt)

        mine = line // 2 * half + z // 2
        fan(nz, counterpart, lambda i: g_send1.at[part(i)], lambda i: land1.at[mine], r1_send, r1_recv)
        descend(0, g_all0, [lax.rem(group + i, NK) for i in range(1, NK)])
        arrived(land1, r1_recv)
        g_all1[group, part(mine), :] = total(land1)
        gather1()
        arrived(landy.at[:, pl.ds(0, NK - 1)], fy_recv.at[1])
        gathered(1, y_first, half)
        row_scales(1, g_all1)
        descend(1, g_all1, range(NK))

    def apply():
        def half_sum(q):
            h1 = dot_nt(q, w_b[0, 0:HALF]) + dot_nt(q, w_b[1, 0:HALF])
            h3 = dot_nt(q, w_b[0, HALF:2 * HALF]) + dot_nt(q, w_b[1, HALF:2 * HALF])
            high, low = split(h1 * jax.nn.sigmoid(h1) * h3)
            w_high, w_low = w_b[0, 2 * HALF:3 * HALF], w_b[1, 2 * HALF:3 * HALF]
            return dot_nn(high, w_high) + (dot_nn(low, w_high) + dot_nn(high, w_low))

        f_give[...] = half_sum(qq[1 - c])
        swap = remote(f_give, f_got, f_send, f_recv, partner)
        swap.start()
        mine = half_sum(qq[c])
        swap.wait()
        f = mine + f_got[...]
        fast = (f * lax.rsqrt(jnp.mean(f * f, axis=1, keepdims=True) + 1e-06)).astype(BF16)
        out_ref[...] = (attn[...] + fast.astype(F32)).astype(BF16)

    apply()

    def left(whole, sem, one_stayed):
        @pl.when(one_stayed)
        def _():
            arrived(whole(1), sem)

        @pl.when(jnp.logical_not(one_stayed))
        def _():
            arrived(whole(0), sem)

    most = g_all0.at[:, pl.ds(0, ROWS - rows)]
    three = finy.at[pl.ds(0, NK - 1)]
    z_first = jnp.logical_not(y_first)
    for share in shares:
        share.wait_send()

    @pl.when(c == 1)
    def _():
        for copy in halo:
            copy.wait_send()

    @pl.when(y_first0)
    def _():
        arrived(most, z_send.at[0])

    @pl.when(span == 0)
    def _():
        give.wait_send()
        left(lambda n: landz.at[:, pl.ds(0, half - n)], az_send, y_first)
        arrived(landy.at[:, pl.ds(0, NK - 1)], ay_send)
        left(lambda n: finz.at[pl.ds(0, half - n)], bz_send, z_first)
        arrived(landy.at[pl.ds(0, fourth)], fy_send.at[0])
        arrived(landy.at[pl.ds(0, fourth), pl.ds(0, NK - 1)], fy_send.at[1])

        @pl.when(y_first)
        def _():
            arrived(landp, p_send.at[0])
            arrived(landp.at[:, pl.ds(0, NK - 1)], p_send.at[1])

        @pl.when(y_first0 & z_first)
        def _():
            arrived(finy, y_send.at[0])
            arrived(three, y_send.at[1])

        @pl.when(jnp.logical_not(y_first0))
        def _():
            arrived(finz.at[pl.ds(0, nz - 1)], zy_send.at[0])

    @pl.when(span == 1)
    def _():
        for j, ref in enumerate(group_of):
            arrived(ref.at[pl.ds(0, 3), 0], col_send.at[j])
            arrived(ref.at[pl.ds(0, 3), 0], fwd_send.at[j])
        arrived(land1.at[pl.ds(0, nz - 1)], r1_send)
        arrived(landy.at[:, pl.ds(0, NK - 1)], fy_send.at[0])

        @pl.when(y_first)
        def _():
            arrived(three, y_send.at[0])
            arrived(most, z_send.at[1])

        @pl.when(z_first)
        def _():
            arrived(finz.at[pl.ds(0, nz - 1)], zy_send.at[1])


def local(ny, nz, queries, keys, values, rates, gate_fast, up_fast, down_fast):
    rows = ROWS // nz
    dma = pltpu.SemaphoreType.DMA
    full = (NK, ROWS, LANES)
    return pl.pallas_call(
        functools.partial(kernel, ny, nz),
        out_shape=jax.ShapeDtypeStruct((T, DH), BF16),
        in_specs=[pl.BlockSpec(memory_space=pl.ANY)] * 7,
        out_specs=pl.BlockSpec(memory_space=pltpu.VMEM),
        scratch_shapes=[
            pltpu.VMEM((2, T, DH), BF16),
            pltpu.VMEM((NK, 2, T, DH), BF16),
            pltpu.VMEM((NK, 2, T, DH), BF16),
            pltpu.VMEM((NK, 2, 8, LANES), F32),
            pltpu.VMEM((T, DH), BF16),
            pltpu.VMEM((T, DH), BF16),
            pltpu.VMEM((1, T), F32),
            pltpu.VMEM((3, DH, FH), BF16),
            pltpu.VMEM(full, F32),
            pltpu.VMEM((2, 3 * HALF, DH), BF16),
            pltpu.VMEM(full, F32),
            pltpu.VMEM(full, BF16),
            pltpu.VMEM(full, BF16),
            pltpu.VMEM(full, BF16),
            pltpu.VMEM((ROWS, LANES), BF16),
            pltpu.VMEM(full, BF16),
            pltpu.VMEM(full, BF16),
            pltpu.VMEM((NK, nz, rows, LANES), BF16),
            pltpu.VMEM((NK, rows, LANES), BF16),
            pltpu.VMEM((NK, NK, rows, LANES), BF16),
            pltpu.VMEM((NK, rows, LANES), BF16),
            pltpu.VMEM((nz // 2, NK, rows, LANES), BF16),
            pltpu.VMEM((nz // 2, rows, LANES), BF16),
            pltpu.VMEM((nz, rows, LANES), BF16),
            pltpu.VMEM((nz, rows, LANES), BF16),
            pltpu.VMEM((2, 16, LANES), F32),
            pltpu.VMEM((2, 16, LANES), F32),
            pltpu.VMEM((T, DH), F32),
            pltpu.VMEM((T, DH), F32),
            pltpu.VMEM((T, DH), F32),
            dma((7,)),
            dma((4,)),
            dma((4,)),
            dma((2,)),
            dma((2,)),
            dma,
            dma,
            dma((3,)),
            dma((3, NK)),
            dma((3,)),
            dma((3, NK)),
            dma,
            dma((NK,)),
            dma,
            dma((nz // 2,)),
            dma,
            dma,
            dma((2,)),
            dma((NK,)),
            dma,
            dma,
            dma((2,)),
            dma((2, NK)),
            dma((2,)),
            dma((2,)),
            dma((2,)),
            dma((2, nz)),
            dma((2,)),
            dma((2,)),
            dma((2,)),
            dma((2,)),
            dma,
            dma,
        ],
        compiler_params=pltpu.CompilerParams(
            collective_id=0, has_side_effects=True, vmem_limit_bytes=60 * 2**20
        ),
        name="fast_layer",
    )(queries, keys, values, rates.reshape(1, T), gate_fast, up_fast, down_fast)


def solution(mesh):
    ny = 2 * NK
    nz = mesh.shape["seq"] // 2 // ny
    return jax.shard_map(
        functools.partial(local, ny, nz),
        mesh=mesh,
        in_specs=(
            P("seq", "head"),
            P("seq", "head"),
            P("seq", "head"),
            P("seq", "head"),
            P("head", None, None),
            P("head", None, None),
            P("head", None, None),
        ),
        out_specs=P("seq", "head"),
        check_vma=False,
    )
```

```python
import functools
import math

import jax
import jax.numpy as jnp
from jax import lax
from jax.experimental import pallas as pl
from jax.experimental.pallas import tpu as pltpu
from jax.sharding import PartitionSpec as P

T = 128
DH = 512
FH = 256
HALF = 128
LANES = 128
NL = DH // LANES
NK = 4
BLOCK = HALF // NK
ROWS = NL * 3 * BLOCK
MESH = pl.DeviceIdType.MESH
F32 = jnp.float32
BF16 = jnp.bfloat16


def dot_nt(a, b):
    return lax.dot_general(a, b, (((1,), (1,)), ((), ())), preferred_element_type=F32)


def dot_nn(a, b):
    return jnp.dot(a, b, preferred_element_type=F32)


def split(a):
    high = a.astype(BF16)
    return high, (a - high.astype(F32)).astype(BF16)


def far_first(j, n):
    h = (j + 1) // 2
    return lax.rem(n // 2 + n + jnp.where(lax.rem(j, 2) == 1, -h, h), n)


def far_offsets(n):
    return sorted(range(1, n), key=lambda d: -min(d, n - d))


def kernel(
    ny, nz,
    q_hbm, k_hbm, v_hbm, r_hbm, wg_hbm, wu_hbm, wd_hbm,
    out_ref,
    qq, kk, vv, rr, hk, hv, r_in, w_in, w_f, w_b,
    g_own, g_give, g_got, g_send0, g_send1, g_all0, g_all1,
    landz, midz, landp, finy, landy, midy, finz, land1,
    ss_own, ss_got, attn, f_give, f_got,
    in_sem, x_send, x_recv, h_send, h_recv, gh_send, gh_recv, col_send, col_recv, fwd_send, fwd_recv,
    az_send, az_recv, ay_send, ay_recv, bz_send, bz_recv, p_send, p_recv, r1_send, r1_recv,
    y_send, y_recv, z_send, z_recv, zy_send, zy_recv, fy_send, fy_recv,
    ss_send, ss_recv, f_send, f_recv,
):
    s = lax.axis_index("seq")
    c = lax.rem(s, 2)
    chip = s // 2
    z = lax.rem(chip, nz)
    y = chip // nz
    rows = ROWS // nz
    n_seq = ny * nz * 2
    span = y // NK
    line = y - span * NK
    partner = s + 1 - 2 * c
    half = nz // 2
    y_first = lax.rem(z + c, 2) == 0
    fourth = nz // 4
    y_first0 = lax.rem(z + c, 4) != 3
    up, right = lax.rem(line, 2), lax.rem(z, 2)
    group = up * 2 + right

    def seq_at(row, column):
        return (row * nz + column) * 2 + c

    loads = [
        pltpu.make_async_copy(k_hbm, kk.at[group, c], in_sem.at[0]),
        pltpu.make_async_copy(v_hbm, vv.at[group, c], in_sem.at[1]),
        pltpu.make_async_copy(r_hbm, r_in, in_sem.at[2]),
        pltpu.make_async_copy(wg_hbm.at[0], w_in.at[0], in_sem.at[3]),
        pltpu.make_async_copy(wu_hbm.at[0], w_in.at[1], in_sem.at[4]),
        pltpu.make_async_copy(wd_hbm.at[0], w_in.at[2], in_sem.at[5]),
        pltpu.make_async_copy(q_hbm, qq.at[c], in_sem.at[6]),
    ]
    for load in loads:
        load.start()

    barrier = pltpu.get_barrier_semaphore()

    def greet(target):
        pl.semaphore_signal(barrier, inc=1, device_id={"seq": target}, device_id_type=MESH)

    for d in far_offsets(ny):
        greet(seq_at(lax.rem(y + d, ny), z))
    for d in far_offsets(nz):
        greet(seq_at(y, lax.rem(z + d, nz)))
    beside = lax.rem(s + 2 * c - 1 + n_seq, n_seq)
    greet(beside)
    greet(partner)
    y_pair, z_pair = y + 1 - 2 * up, z + 1 - 2 * right
    pairs = [
        (seq_at(y_pair, z_pair), (1 - up) * 2 + 1 - right),
        (seq_at(y_pair, z), (1 - up) * 2 + right),
        (seq_at(y, z_pair), up * 2 + 1 - right),
    ]
    greet(pairs[0][0])
    other_row = y - line + lax.rem(line + 2, NK)
    for d in range(1, half):
        greet(seq_at(other_row, lax.rem(z + 2 * d, nz)))

    for load in loads:
        load.wait()
    rr[group, c] = jnp.broadcast_to(r_in[...], (8, LANES))

    def slopes(h1, h3, dg, rate):
        sig = jax.nn.sigmoid(h1)
        s1 = h1 * sig
        a_gate = dg * h3 * sig * (1.0 + h1 * (1.0 - sig))
        return a_gate, dg * s1, (s1 * h3) * rate

    def at(m, b):
        first = (b * 3 + m) * BLOCK
        return slice(first, first + BLOCK)

    @pl.when(span == 0)
    def _():
        x, y_val = kk[group, c], vv[group, c]
        minus_r = -jnp.broadcast_to(r_in[...], (LANES, T)).T[:, 0:1]
        acts = slopes(dot_nn(x, w_in[0]), dot_nn(x, w_in[1]), dot_nn(y_val, w_in[2]) * minus_r, minus_r)
        for m in range(3):
            grad = dot_nn(acts[m].T.astype(BF16), x if m < 2 else y_val)
            low, high = grad[:HALF], grad[HALF:]
            mine = jnp.where(c == 0, low, high)
            theirs = jnp.where(c == 0, high, low).astype(BF16)
            for b in range(NL):
                for k in range(NK):
                    g_own[k, at(m, b), :] = mine[k * BLOCK:(k + 1) * BLOCK, b * LANES:(b + 1) * LANES]
                    g_give[k, at(m, b), :] = theirs[k * BLOCK:(k + 1) * BLOCK, b * LANES:(b + 1) * LANES]

    pl.semaphore_wait(barrier, ny + nz + half)

    def remote(src, dst, send, recv, target):
        return pltpu.make_async_remote_copy(
            src_ref=src, dst_ref=dst, send_sem=send, recv_sem=recv, device_id={"seq": target}, device_id_type=MESH
        )

    def fan(n, place, src, dst, send, recv):
        def one(i, carry):
            index, target = place(i)
            from_ref, to_ref = src(index), dst(index)

            @pl.when(target == s)
            def _():
                pltpu.make_async_copy(from_ref, to_ref, recv).start()

            @pl.when(target != s)
            def _():
                remote(from_ref, to_ref, send, recv, target).start()

            return carry

        lax.fori_loop(0, n, one, 0)

    def along_z(i):
        zt = lax.rem(z + far_first(i, nz), nz)
        return zt, seq_at(y, zt)

    def column(i, kind):
        return 2 * lax.rem(z // 2 + far_first(i, half), half) + (c if kind == 0 else 1 - c)

    def row(i):
        return lax.rem(line + i, NK)

    def near(i):
        back = line >= 2
        me = jnp.where(back, NK - 1 - line, line)
        k = i - 1 + (i - 1 >= me).astype(jnp.int32)
        return jnp.where(back, NK - 1 - k, k)

    def part(i):
        return pl.ds(pl.multiple_of(i * rows, 16), rows)

    def arrived(ref, sem):
        pltpu.make_async_copy(ref, ref, sem).wait()

    def total(ref):
        out = ref[0].astype(F32)
        for i in range(1, ref.shape[0]):
            out = out + ref[i].astype(F32)
        return out.astype(BF16)

    give = remote(g_give, g_got, gh_send, gh_recv, partner)
    shares = [
        remote(ref, ref, x_send.at[i], x_recv.at[i], partner)
        for i, ref in enumerate((kk.at[group, c], vv.at[group, c], rr.at[group, c], qq.at[c]))
    ]
    halo = [
        remote(src.at[group, c], dst, h_send.at[i], h_recv.at[i], beside)
        for i, (src, dst) in enumerate(((kk, hk), (vv, hv)))
    ]
    group_of = (kk, vv, rr)

    def scatter0():
        first = y - line

        def send(i, carry):
            k = i

            def place_z(j):
                zt = column(j, 0)
                return zt, seq_at(y, zt)

            fan(half, place_z, lambda zt: g_send0.at[k, part(zt)], lambda zt: landz.at[k, z], az_send, az_recv.at[k])
            return carry

        def send_y(i, carry):
            zt = column(i, 1)

            def place_y(j):
                k = row(j + 1)
                return k, seq_at(first + k, z)

            fan(NK, place_y, lambda k: g_send0.at[k, part(zt)], lambda k: landy.at[zt // 2, line], ay_send, ay_recv.at[zt // 2])
            return carry

        for i in range(max(NK, half)):
            if i < NK:
                send(i, 0)
            if i < half:
                send_y(i, 0)

    def scatter0_end():
        def add_z(k):
            arrived(landz.at[k], az_recv.at[k])
            midz[k] = total(landz.at[k])
            pltpu.make_async_copy(midz.at[k], landp.at[k, line], p_recv.at[k]).start()
            for i in range(NK):
                remote(midz.at[k], landp.at[k, line], p_send.at[0], p_recv.at[k], seq_at(NK + row(i + 2), z)).start()

        def add_y(i):
            zt = column(i, 1)
            j = zt // 2
            arrived(landy.at[j], ay_recv.at[j])
            midy[j] = total(landy.at[j])

            @pl.when(zt == z)
            def _():
                pltpu.make_async_copy(midy.at[j], finz.at[z], bz_recv).start()

            @pl.when(zt != z)
            def _():
                remote(midy.at[j], finz.at[z], bz_send, bz_recv, seq_at(y, zt)).start()

        for i in range(max(NK, half)):
            if i < half:
                add_y(i)
            if i < NK:

                @pl.when(y_first)
                def _():
                    add_z(i)

        @pl.when(jnp.logical_not(y_first))
        def _():
            arrived(finz, bz_recv)
            g_all0[line, part(z), :] = total(finz)

    def to_z(block, send, recv):
        def one(i, carry):
            _, target = along_z(i)
            remote(block, block, send, recv, target).start()
            return carry

        lax.fori_loop(0, nz - 1, one, 0)

    def to_own_span(block, send, recv):
        for i in range(NK - 1, 0, -1):
            remote(block, block, send, recv, seq_at(y - line + near(i), z)).start()

    def to_span1(block, send, recv):
        for i in range(NK):
            remote(block, block, send, recv, seq_at(NK + row(i + 2), z)).start()

    def gather0():
        def block(k, zt):
            return g_all0.at[k, part(zt)]

        def column0(i):
            return 4 * lax.rem(z // 4 + i, fourth) + 3 - c

        own = block(line, z)

        def forward_z(k):
            arrived(block(k, z), y_recv.at[0, k])
            to_z(block(k, z), z_send.at[0], z_recv.at[0])

        def add_rows(k):
            arrived(landp.at[k], p_recv.at[k])
            g_all0[k, part(z), :] = total(landp.at[k])
            to_z(block(k, z), z_send.at[0], z_recv.at[0])

        owner_y = y_first0 & jnp.logical_not(y_first)

        @pl.when(span == 0)
        def _():
            @pl.when(owner_y)
            def _():
                to_span1(own, y_send.at[0], y_recv.at[0, line])
                to_own_span(own, y_send.at[1], y_recv.at[0, line])

            @pl.when(jnp.logical_not(y_first0))
            def _():
                to_z(own, zy_send.at[0], zy_recv.at[0, z])
                to_span1(own, fy_send.at[0], fy_recv.at[0])

            for i in range(fourth):
                zt = column0(i)

                @pl.when(zt != z)
                def _():
                    arrived(block(line, zt), zy_recv.at[0, zt])
                    to_span1(block(line, zt), fy_send.at[0], fy_recv.at[0])

            for i in range(fourth):
                to_own_span(block(line, column0(i)), fy_send.at[1], fy_recv.at[0])

            @pl.when(y_first)
            def _():
                for k in range(NK):
                    for i in range(1, NK):
                        remote(midz.at[k], landp.at[k, line], p_send.at[1], p_recv.at[k], seq_at(row(i), z)).start()

            @pl.when(owner_y)
            def _():
                to_z(own, z_send.at[0], z_recv.at[0])
                for i in range(1, NK):
                    forward_z(row(i))

        @pl.when((span == 1) & owner_y)
        def _():
            for i in range(NK):
                forward_z(jnp.where(line >= 2, i, NK - 1 - i))

        @pl.when(y_first)
        def _():
            for k in range(NK):
                add_rows(k)

    def gathered(p, along_y_first, columns):
        @pl.when(along_y_first)
        def _():
            arrived(landz.at[:, pl.ds(0, columns - 1)], z_recv.at[p])

        @pl.when(jnp.logical_not(along_y_first))
        def _():
            arrived(landz.at[:, pl.ds(0, columns)], z_recv.at[p])

    def place1(k, zt):
        return g_all1.at[lax.rem(k, 2) * 2 + lax.rem(zt, 2), part(k // 2 * half + zt // 2)]

    def gather1():
        own = place1(line, z)

        @pl.when(y_first)
        def _():
            to_own_span(own, y_send.at[0], y_recv.at[1, line])
            to_z(own, z_send.at[1], z_recv.at[1])

        @pl.when(jnp.logical_not(y_first))
        def _():
            to_z(own, zy_send.at[1], zy_recv.at[1, z])
            to_own_span(own, fy_send.at[0], fy_recv.at[1])

        for i in range(max(NK, half)):
            if 1 <= i < NK:

                @pl.when(y_first)
                def _():
                    k = near(i)
                    arrived(place1(k, z), y_recv.at[1, k])
                    to_z(place1(k, z), z_send.at[1], z_recv.at[1])

            if i < half:
                zt = column(half - 1 - i, 1)

                @pl.when(zt != z)
                def _():
                    arrived(place1(line, zt), zy_recv.at[1, zt])
                    to_own_span(place1(line, zt), fy_send.at[0], fy_recv.at[1])

    def initial_weights():
        first = pl.multiple_of(c * HALF, HALF)
        for m in range(3):
            w = w_in[m, :, pl.ds(first, HALF)].astype(F32).T
            for b in range(NL):
                for k in range(NK):
                    w_f[k, at(m, b), :] = w[k * BLOCK:(k + 1) * BLOCK, b * LANES:(b + 1) * LANES]

    def attention():
        @pl.when(c == 0)
        def _():
            for copy in halo:
                copy.wait_recv()

        @pl.when(c == 1)
        def _():
            hk[...] = kk[group, 0]
            hv[...] = vv[group, 0]

        q = qq[c]
        inv = jnp.sqrt(jnp.float32(DH))
        before = dot_nt(q, hk[...]) / inv
        here = dot_nt(q, kk[group, c]) / inv
        t_q = lax.broadcasted_iota(jnp.int32, (T, T), 0)
        t_k = lax.broadcasted_iota(jnp.int32, (T, T), 1)
        before = jnp.where((t_k > t_q) & (s > 0), before, jnp.float32(-1e30))
        here = jnp.where(t_k <= t_q, here, jnp.float32(-1e30))
        top = jnp.maximum(jnp.max(before, axis=1, keepdims=True), jnp.max(here, axis=1, keepdims=True))
        before, here = jnp.exp(before - top), jnp.exp(here - top)
        norm = jnp.sum(before, axis=1, keepdims=True) + jnp.sum(here, axis=1, keepdims=True)
        before, here = (before / norm).astype(BF16), (here / norm).astype(BF16)
        attn[...] = dot_nn(before, hv[...]) + dot_nn(here, vv[group, c])

    last_chip = chip == NK * nz - 1

    def start_halo():
        for copy in halo:
            copy.start()

    @pl.when(span == 0)
    def _():
        give.start()
        for share in shares:
            share.start()
        pl.when((c == 1) & last_chip)(start_halo)
        give.wait_recv()
        g_send0[...] = (g_own[...] + g_got[...].astype(F32)).astype(BF16)
        scatter0()
        initial_weights()
        for share in shares:
            share.wait_recv()
        scatter0_end()
        gather0()
        pl.when((c == 1) & jnp.logical_not(last_chip))(start_halo)
        attention()
        arrived(landy.at[pl.ds(0, fourth), pl.ds(0, NK - 1)], fy_recv.at[0])

    @pl.when(span == 1)
    def _():
        for share in shares:
            share.start()
        pl.when(c == 1)(start_halo)
        for target, _ in pairs:
            for j, ref in enumerate(group_of):
                own = ref.at[group, c]
                remote(own, own, col_send.at[j], col_recv.at[j, group], target).start()
        initial_weights()
        gather0()
        for _, k in pairs:
            for j, ref in enumerate(group_of):
                block = ref.at[k, c]
                arrived(block, col_recv.at[j, k])
                remote(block, block, fwd_send.at[j], fwd_recv.at[j, k], partner).start()
        for share in shares:
            share.wait_recv()
        attention()
        for _, k in pairs:
            for j, ref in enumerate(group_of):
                arrived(ref.at[k, 1 - c], fwd_recv.at[j, k])
        arrived(landy.at[pl.ds(0, fourth)], fy_recv.at[0])

    def row_scales(p, g_all):
        ss_own[p] = jnp.zeros((16, LANES), F32)
        for m in range(3):
            for b in range(NL):
                g = g_all[:, at(m, b), :].astype(F32)
                ss_own[p, m * NL + b:m * NL + b + 1, :] = jnp.sum(jnp.sum(g * g, axis=0), axis=0, keepdims=True)
        swap = remote(ss_own.at[p], ss_got.at[p], ss_send.at[p], ss_recv.at[p], partner)
        swap.start()
        swap.wait()

    def descend(p, g_all, blocks):
        scale = 0.05 * lax.rsqrt((ss_own[p] + ss_got[p]) * (1.0 / FH) + 1e-06)
        for k in blocks:
            for m in range(3):
                for b in range(NL):
                    j = m * NL + b
                    new = w_f[k, at(m, b), :] - g_all[k, at(m, b), :].astype(F32) * scale[j:j + 1]
                    w_f[k, at(m, b), :] = new
                    first = m * HALF + k * BLOCK
                    place = slice(first, first + BLOCK) if isinstance(k, int) else pl.ds(pl.multiple_of(first, BLOCK), BLOCK)
                    for i, term in enumerate(split(new)):
                        w_b[i, place, b * LANES:(b + 1) * LANES] = term

    gathered(0, y_first0, nz - fourth)
    row_scales(0, g_all0)

    @pl.when(span == 0)
    def _():
        descend(0, g_all0, range(NK))

    def gradient1():
        n = 2 * NK * T
        x, y_val = kk[...].reshape(n, DH), vv[...].reshape(n, DH)
        minus_r = -jnp.concatenate([rr[k, i][0:1] for k in range(NK) for i in range(2)], axis=1)

        def block(i, m):
            return w_b[i, pl.ds(pl.multiple_of(m * HALF + group * BLOCK, BLOCK), BLOCK), :]

        h = dot_nt(jnp.concatenate([block(0, 0), block(0, 1), block(1, 0), block(1, 1)], axis=0), x)
        h = h[:2 * BLOCK] + h[2 * BLOCK:]
        dg = dot_nt(jnp.concatenate([block(0, 2), block(1, 2)], axis=0), y_val)
        dg = (dg[:BLOCK] + dg[BLOCK:]) * minus_r
        a_gate, a_up, a_down = slopes(h[:BLOCK], h[BLOCK:], dg, minus_r)
        on_x = dot_nn(jnp.concatenate([a_gate, a_up], axis=0).astype(BF16), x).astype(BF16)
        on_y = dot_nn(a_down.astype(BF16), y_val).astype(BF16)
        for m, grad in enumerate((on_x[:BLOCK], on_x[BLOCK:], on_y)):
            for b in range(NL):
                g_send1[at(m, b), :] = grad[:, b * LANES:(b + 1) * LANES]

    @pl.when(span == 1)
    def _():
        descend(0, g_all0, [group])
        gradient1()

        def counterpart(i):
            k = lax.rem(line + 2 - 2 * lax.rem(i, 2), NK)
            zt = 2 * lax.rem(z // 2 + far_first(i // 2, half), half) + right
            return k // 2 * half + zt // 2, seq_at(NK + k, zt)

        mine = line // 2 * half + z // 2
        fan(nz, counterpart, lambda i: g_send1.at[part(i)], lambda i: land1.at[mine], r1_send, r1_recv)
        descend(0, g_all0, [lax.rem(group + i, NK) for i in range(1, NK)])
        arrived(land1, r1_recv)
        g_all1[group, part(mine), :] = total(land1)
        gather1()
        arrived(landy.at[:, pl.ds(0, NK - 1)], fy_recv.at[1])
        gathered(1, y_first, half)
        row_scales(1, g_all1)
        descend(1, g_all1, range(NK))

    def apply():
        def half_sum(q):
            h1 = dot_nt(q, w_b[0, 0:HALF]) + dot_nt(q, w_b[1, 0:HALF])
            h3 = dot_nt(q, w_b[0, HALF:2 * HALF]) + dot_nt(q, w_b[1, HALF:2 * HALF])
            high, low = split(h1 * jax.nn.sigmoid(h1) * h3)
            w_high, w_low = w_b[0, 2 * HALF:3 * HALF], w_b[1, 2 * HALF:3 * HALF]
            return dot_nn(high, w_high) + (dot_nn(low, w_high) + dot_nn(high, w_low))

        f_give[...] = half_sum(qq[1 - c])
        swap = remote(f_give, f_got, f_send, f_recv, partner)
        swap.start()
        mine = half_sum(qq[c])
        swap.wait()
        f = mine + f_got[...]
        fast = (f * lax.rsqrt(jnp.mean(f * f, axis=1, keepdims=True) + 1e-06)).astype(BF16)
        out_ref[...] = (attn[...] + fast.astype(F32)).astype(BF16)

    apply()

    def left(whole, sem, one_stayed):
        @pl.when(one_stayed)
        def _():
            arrived(whole(1), sem)

        @pl.when(jnp.logical_not(one_stayed))
        def _():
            arrived(whole(0), sem)

    most = g_all0.at[:, pl.ds(0, ROWS - rows)]
    three = finy.at[pl.ds(0, NK - 1)]
    z_first = jnp.logical_not(y_first)
    for share in shares:
        share.wait_send()

    @pl.when(c == 1)
    def _():
        for copy in halo:
            copy.wait_send()

    @pl.when(y_first0)
    def _():
        arrived(most, z_send.at[0])

    @pl.when(span == 0)
    def _():
        give.wait_send()
        left(lambda n: landz.at[:, pl.ds(0, half - n)], az_send, y_first)
        arrived(landy.at[:, pl.ds(0, NK - 1)], ay_send)
        left(lambda n: finz.at[pl.ds(0, half - n)], bz_send, z_first)
        arrived(landy.at[pl.ds(0, fourth)], fy_send.at[0])
        arrived(landy.at[pl.ds(0, fourth), pl.ds(0, NK - 1)], fy_send.at[1])

        @pl.when(y_first)
        def _():
            arrived(landp, p_send.at[0])
            arrived(landp.at[:, pl.ds(0, NK - 1)], p_send.at[1])

        @pl.when(y_first0 & z_first)
        def _():
            arrived(finy, y_send.at[0])
            arrived(three, y_send.at[1])

        @pl.when(jnp.logical_not(y_first0))
        def _():
            arrived(finz.at[pl.ds(0, nz - 1)], zy_send.at[0])

    @pl.when(span == 1)
    def _():
        for j, ref in enumerate(group_of):
            arrived(ref.at[pl.ds(0, 3), 0], col_send.at[j])
            arrived(ref.at[pl.ds(0, 3), 0], fwd_send.at[j])
        arrived(land1.at[pl.ds(0, nz - 1)], r1_send)
        arrived(landy.at[:, pl.ds(0, NK - 1)], fy_send.at[0])

        @pl.when(y_first)
        def _():
            arrived(three, y_send.at[0])
            arrived(most, z_send.at[1])

        @pl.when(z_first)
        def _():
            arrived(finz.at[pl.ds(0, nz - 1)], zy_send.at[1])


def local(ny, nz, queries, keys, values, rates, gate_fast, up_fast, down_fast):
    rows = ROWS // nz
    dma = pltpu.SemaphoreType.DMA
    full = (NK, ROWS, LANES)
    return pl.pallas_call(
        functools.partial(kernel, ny, nz),
        out_shape=jax.ShapeDtypeStruct((T, DH), BF16),
        in_specs=[pl.BlockSpec(memory_space=pl.ANY)] * 7,
        out_specs=pl.BlockSpec(memory_space=pltpu.VMEM),
        scratch_shapes=[
            pltpu.VMEM((2, T, DH), BF16),
            pltpu.VMEM((NK, 2, T, DH), BF16),
            pltpu.VMEM((NK, 2, T, DH), BF16),
            pltpu.VMEM((NK, 2, 8, LANES), F32),
            pltpu.VMEM((T, DH), BF16),
            pltpu.VMEM((T, DH), BF16),
            pltpu.VMEM((1, T), F32),
            pltpu.VMEM((3, DH, FH), BF16),
            pltpu.VMEM(full, F32),
            pltpu.VMEM((2, 3 * HALF, DH), BF16),
            pltpu.VMEM(full, F32),
            pltpu.VMEM(full, BF16),
            pltpu.VMEM(full, BF16),
            pltpu.VMEM(full, BF16),
            pltpu.VMEM((ROWS, LANES), BF16),
            pltpu.VMEM(full, BF16),
            pltpu.VMEM(full, BF16),
            pltpu.VMEM((NK, nz, rows, LANES), BF16),
            pltpu.VMEM((NK, rows, LANES), BF16),
            pltpu.VMEM((NK, NK, rows, LANES), BF16),
            pltpu.VMEM((NK, rows, LANES), BF16),
            pltpu.VMEM((nz // 2, NK, rows, LANES), BF16),
            pltpu.VMEM((nz // 2, rows, LANES), BF16),
            pltpu.VMEM((nz, rows, LANES), BF16),
            pltpu.VMEM((nz, rows, LANES), BF16),
            pltpu.VMEM((2, 16, LANES), F32),
            pltpu.VMEM((2, 16, LANES), F32),
            pltpu.VMEM((T, DH), F32),
            pltpu.VMEM((T, DH), F32),
            pltpu.VMEM((T, DH), F32),
            dma((7,)),
            dma((4,)),
            dma((4,)),
            dma((2,)),
            dma((2,)),
            dma,
            dma,
            dma((3,)),
            dma((3, NK)),
            dma((3,)),
            dma((3, NK)),
            dma,
            dma((NK,)),
            dma,
            dma((nz // 2,)),
            dma,
            dma,
            dma((2,)),
            dma((NK,)),
            dma,
            dma,
            dma((2,)),
            dma((2, NK)),
            dma((2,)),
            dma((2,)),
            dma((2,)),
            dma((2, nz)),
            dma((2,)),
            dma((2,)),
            dma((2,)),
            dma((2,)),
            dma,
            dma,
        ],
        compiler_params=pltpu.CompilerParams(
            collective_id=0, has_side_effects=True, vmem_limit_bytes=55040 * 1024
        ),
        name="fast_layer",
    )(queries, keys, values, rates.reshape(1, T), gate_fast, up_fast, down_fast)


def solution(mesh):
    ny = 2 * NK
    nz = mesh.shape["seq"] // 2 // ny
    return jax.shard_map(
        functools.partial(local, ny, nz),
        mesh=mesh,
        in_specs=(
            P("seq", "head"),
            P("seq", "head"),
            P("seq", "head"),
            P("seq", "head"),
            P("head", None, None),
            P("head", None, None),
            P("head", None, None),
        ),
        out_specs=P("seq", "head"),
        check_vma=False,
    )
```

```python
import functools
import math

import jax
import jax.numpy as jnp
from jax import lax
from jax.experimental import pallas as pl
from jax.experimental.pallas import tpu as pltpu
from jax.sharding import PartitionSpec as P

T = 128
DH = 512
FH = 256
HALF = 128
LANES = 128
NL = DH // LANES
NK = 4
BLOCK = HALF // NK
ROWS = NL * 3 * BLOCK
MESH = pl.DeviceIdType.MESH
F32 = jnp.float32
BF16 = jnp.bfloat16


def dot_nt(a, b):
    return lax.dot_general(a, b, (((1,), (1,)), ((), ())), preferred_element_type=F32)


def dot_nn(a, b):
    return jnp.dot(a, b, preferred_element_type=F32)


def split(a):
    high = a.astype(BF16)
    return high, (a - high.astype(F32)).astype(BF16)


def far_first(j, n):
    h = (j + 1) // 2
    return lax.rem(n // 2 + n + jnp.where(lax.rem(j, 2) == 1, -h, h), n)


def far_offsets(n):
    return sorted(range(1, n), key=lambda d: -min(d, n - d))


def kernel(
    ny, nz,
    q_hbm, k_hbm, v_hbm, r_hbm, wg_hbm, wu_hbm, wd_hbm,
    out_ref,
    qq, kk, vv, rr, hk, hv, r_in, w_in, w_f, w_b,
    g_own, g_give, g_got, g_send0, g_send1, g_all0, g_all1,
    landz, midz, landp, finy, landy, midy, finz, land1,
    ss_own, ss_got, attn, f_give, f_got,
    in_sem, x_send, x_recv, h_send, h_recv, gh_send, gh_recv, col_send, col_recv, fwd_send, fwd_recv,
    az_send, az_recv, ay_send, ay_recv, bz_send, bz_recv, p_send, p_recv, r1_send, r1_recv,
    y_send, y_recv, z_send, z_recv, zy_send, zy_recv, fy_send, fy_recv,
    ss_send, ss_recv, f_send, f_recv,
):
    s = lax.axis_index("seq")
    c = lax.rem(s, 2)
    chip = s // 2
    z = lax.rem(chip, nz)
    y = chip // nz
    rows = ROWS // nz
    n_seq = ny * nz * 2
    span = y // NK
    line = y - span * NK
    partner = s + 1 - 2 * c
    half = nz // 2
    y_first = lax.rem(z + c, 2) == 0
    fourth = nz // 4
    y_first0 = lax.rem(z + c, 4) != 3
    up, right = lax.rem(line, 2), lax.rem(z, 2)
    group = up * 2 + right

    def seq_at(row, column):
        return (row * nz + column) * 2 + c

    loads = [
        pltpu.make_async_copy(k_hbm, kk.at[group, c], in_sem.at[0]),
        pltpu.make_async_copy(v_hbm, vv.at[group, c], in_sem.at[1]),
        pltpu.make_async_copy(r_hbm, r_in, in_sem.at[2]),
        pltpu.make_async_copy(wg_hbm.at[0], w_in.at[0], in_sem.at[3]),
        pltpu.make_async_copy(wu_hbm.at[0], w_in.at[1], in_sem.at[4]),
        pltpu.make_async_copy(wd_hbm.at[0], w_in.at[2], in_sem.at[5]),
        pltpu.make_async_copy(q_hbm, qq.at[c], in_sem.at[6]),
    ]
    for load in loads:
        load.start()

    barrier = pltpu.get_barrier_semaphore()

    def greet(target):
        pl.semaphore_signal(barrier, inc=1, device_id={"seq": target}, device_id_type=MESH)

    for d in far_offsets(ny):
        greet(seq_at(lax.rem(y + d, ny), z))
    for d in far_offsets(nz):
        greet(seq_at(y, lax.rem(z + d, nz)))
    beside = lax.rem(s + 2 * c - 1 + n_seq, n_seq)
    greet(beside)
    greet(partner)
    y_pair, z_pair = y + 1 - 2 * up, z + 1 - 2 * right
    pairs = [
        (seq_at(y_pair, z_pair), (1 - up) * 2 + 1 - right),
        (seq_at(y_pair, z), (1 - up) * 2 + right),
        (seq_at(y, z_pair), up * 2 + 1 - right),
    ]
    greet(pairs[0][0])
    other_row = y - line + lax.rem(line + 2, NK)
    for d in range(1, half):
        greet(seq_at(other_row, lax.rem(z + 2 * d, nz)))

    for load in loads:
        load.wait()
    rr[group, c] = jnp.broadcast_to(r_in[...], (8, LANES))

    def slopes(h1, h3, dg, rate):
        sig = jax.nn.sigmoid(h1)
        s1 = h1 * sig
        a_gate = dg * h3 * sig * (1.0 + h1 * (1.0 - sig))
        return a_gate, dg * s1, (s1 * h3) * rate

    def at(m, b):
        first = (b * 3 + m) * BLOCK
        return slice(first, first + BLOCK)

    @pl.when(span == 0)
    def _():
        x, y_val = kk[group, c], vv[group, c]
        minus_r = -jnp.broadcast_to(r_in[...], (LANES, T)).T[:, 0:1]
        acts = slopes(dot_nn(x, w_in[0]), dot_nn(x, w_in[1]), dot_nn(y_val, w_in[2]) * minus_r, minus_r)
        for m in range(3):
            grad = dot_nn(acts[m].T.astype(BF16), x if m < 2 else y_val)
            low, high = grad[:HALF], grad[HALF:]
            mine = jnp.where(c == 0, low, high)
            theirs = jnp.where(c == 0, high, low).astype(BF16)
            for b in range(NL):
                for k in range(NK):
                    g_own[k, at(m, b), :] = mine[k * BLOCK:(k + 1) * BLOCK, b * LANES:(b + 1) * LANES]
                    g_give[k, at(m, b), :] = theirs[k * BLOCK:(k + 1) * BLOCK, b * LANES:(b + 1) * LANES]

    pl.semaphore_wait(barrier, ny + nz + half)

    def remote(src, dst, send, recv, target):
        return pltpu.make_async_remote_copy(
            src_ref=src, dst_ref=dst, send_sem=send, recv_sem=recv, device_id={"seq": target}, device_id_type=MESH
        )

    def fan(n, place, src, dst, send, recv):
        def one(i, carry):
            index, target = place(i)
            from_ref, to_ref = src(index), dst(index)

            @pl.when(target == s)
            def _():
                pltpu.make_async_copy(from_ref, to_ref, recv).start()

            @pl.when(target != s)
            def _():
                remote(from_ref, to_ref, send, recv, target).start()

            return carry

        lax.fori_loop(0, n, one, 0)

    def along_z(i):
        zt = lax.rem(z + far_first(i, nz), nz)
        return zt, seq_at(y, zt)

    def column(i, kind):
        return 2 * lax.rem(z // 2 + far_first(i, half), half) + (c if kind == 0 else 1 - c)

    def row(i):
        return lax.rem(line + i, NK)

    def near(i):
        back = line >= 2
        me = jnp.where(back, NK - 1 - line, line)
        k = i - 1 + (i - 1 >= me).astype(jnp.int32)
        return jnp.where(back, NK - 1 - k, k)

    def part(i):
        return pl.ds(pl.multiple_of(i * rows, 16), rows)

    def arrived(ref, sem):
        pltpu.make_async_copy(ref, ref, sem).wait()

    def total(ref):
        out = ref[0].astype(F32)
        for i in range(1, ref.shape[0]):
            out = out + ref[i].astype(F32)
        return out.astype(BF16)

    gives = [remote(g_give.at[k], g_got.at[k], gh_send.at[k], gh_recv.at[k], partner) for k in range(NK)]
    shares = [
        remote(ref, ref, x_send.at[i], x_recv.at[i], partner)
        for i, ref in enumerate((kk.at[group, c], vv.at[group, c], rr.at[group, c], qq.at[c]))
    ]
    halo = [
        remote(src.at[group, c], dst, h_send.at[i], h_recv.at[i], beside)
        for i, (src, dst) in enumerate(((kk, hk), (vv, hv)))
    ]
    group_of = (kk, vv, rr)

    def scatter0():
        first = y - line

        def send(i, carry):
            k = i

            def place_z(j):
                zt = column(j, 0)
                return zt, seq_at(y, zt)

            fan(half, place_z, lambda zt: g_send0.at[k, part(zt)], lambda zt: landz.at[k, z], az_send, az_recv.at[k])
            return carry

        def send_y(i, carry):
            zt = column(i, 1)

            def place_y(j):
                k = row(j + 1)
                return k, seq_at(first + k, z)

            fan(NK, place_y, lambda k: g_send0.at[k, part(zt)], lambda k: landy.at[zt // 2, line], ay_send, ay_recv.at[zt // 2])
            return carry

        for i in range(max(NK, half)):
            if i < NK:
                send(i, 0)
            if i < half:
                send_y(i, 0)

    def scatter0_end():
        def add_z(k):
            arrived(landz.at[k], az_recv.at[k])
            midz[k] = total(landz.at[k])
            pltpu.make_async_copy(midz.at[k], landp.at[k, line], p_recv.at[k]).start()
            for i in range(NK):
                remote(midz.at[k], landp.at[k, line], p_send.at[0], p_recv.at[k], seq_at(NK + row(i + 2), z)).start()

        def add_y(i):
            zt = column(i, 1)
            j = zt // 2
            arrived(landy.at[j], ay_recv.at[j])
            midy[j] = total(landy.at[j])

            @pl.when(zt == z)
            def _():
                pltpu.make_async_copy(midy.at[j], finz.at[z], bz_recv).start()

            @pl.when(zt != z)
            def _():
                remote(midy.at[j], finz.at[z], bz_send, bz_recv, seq_at(y, zt)).start()

        for i in range(max(NK, half)):
            if i < half:
                add_y(i)
            if i < NK:

                @pl.when(y_first)
                def _():
                    add_z(i)

        @pl.when(jnp.logical_not(y_first))
        def _():
            arrived(finz, bz_recv)
            g_all0[line, part(z), :] = total(finz)

    def to_z(block, send, recv):
        def one(i, carry):
            _, target = along_z(i)
            remote(block, block, send, recv, target).start()
            return carry

        lax.fori_loop(0, nz - 1, one, 0)

    def to_own_span(block, send, recv):
        for i in range(NK - 1, 0, -1):
            remote(block, block, send, recv, seq_at(y - line + near(i), z)).start()

    def to_span1(block, send, recv):
        for i in range(NK):
            remote(block, block, send, recv, seq_at(NK + row(i + 2), z)).start()

    def gather0():
        def block(k, zt):
            return g_all0.at[k, part(zt)]

        def column0(i):
            return 4 * lax.rem(z // 4 + i, fourth) + 3 - c

        own = block(line, z)

        def forward_z(k):
            arrived(block(k, z), y_recv.at[0, k])
            to_z(block(k, z), z_send.at[0], z_recv.at[0])

        def add_rows(k):
            arrived(landp.at[k], p_recv.at[k])
            g_all0[k, part(z), :] = total(landp.at[k])
            to_z(block(k, z), z_send.at[0], z_recv.at[0])

        owner_y = y_first0 & jnp.logical_not(y_first)

        @pl.when(span == 0)
        def _():
            @pl.when(owner_y)
            def _():
                to_span1(own, y_send.at[0], y_recv.at[0, line])
                to_own_span(own, y_send.at[1], y_recv.at[0, line])

            @pl.when(jnp.logical_not(y_first0))
            def _():
                to_z(own, zy_send.at[0], zy_recv.at[0, z])
                to_span1(own, fy_send.at[0], fy_recv.at[0])

            for i in range(fourth):
                zt = column0(i)

                @pl.when(zt != z)
                def _():
                    arrived(block(line, zt), zy_recv.at[0, zt])
                    to_span1(block(line, zt), fy_send.at[0], fy_recv.at[0])

            for i in range(fourth):
                to_own_span(block(line, column0(i)), fy_send.at[1], fy_recv.at[0])

            @pl.when(y_first)
            def _():
                for k in range(NK):
                    for i in range(1, NK):
                        remote(midz.at[k], landp.at[k, line], p_send.at[1], p_recv.at[k], seq_at(row(i), z)).start()

            @pl.when(owner_y)
            def _():
                to_z(own, z_send.at[0], z_recv.at[0])
                for i in range(1, NK):
                    forward_z(row(i))

        @pl.when((span == 1) & owner_y)
        def _():
            for i in range(NK):
                forward_z(jnp.where(line >= 2, i, NK - 1 - i))

        @pl.when(y_first)
        def _():
            for k in range(NK):
                add_rows(k)

    def gathered(p, along_y_first, columns):
        @pl.when(along_y_first)
        def _():
            arrived(landz.at[:, pl.ds(0, columns - 1)], z_recv.at[p])

        @pl.when(jnp.logical_not(along_y_first))
        def _():
            arrived(landz.at[:, pl.ds(0, columns)], z_recv.at[p])

    def place1(k, zt):
        return g_all1.at[lax.rem(k, 2) * 2 + lax.rem(zt, 2), part(k // 2 * half + zt // 2)]

    def gather1():
        own = place1(line, z)

        @pl.when(y_first)
        def _():
            to_own_span(own, y_send.at[0], y_recv.at[1, line])
            to_z(own, z_send.at[1], z_recv.at[1])

        @pl.when(jnp.logical_not(y_first))
        def _():
            to_z(own, zy_send.at[1], zy_recv.at[1, z])
            to_own_span(own, fy_send.at[0], fy_recv.at[1])

        for i in range(max(NK, half)):
            if 1 <= i < NK:

                @pl.when(y_first)
                def _():
                    k = near(i)
                    arrived(place1(k, z), y_recv.at[1, k])
                    to_z(place1(k, z), z_send.at[1], z_recv.at[1])

            if i < half:
                zt = column(half - 1 - i, 1)

                @pl.when(zt != z)
                def _():
                    arrived(place1(line, zt), zy_recv.at[1, zt])
                    to_own_span(place1(line, zt), fy_send.at[0], fy_recv.at[1])

    def initial_weights():
        first = pl.multiple_of(c * HALF, HALF)
        for m in range(3):
            w = w_in[m, :, pl.ds(first, HALF)].astype(F32).T
            for b in range(NL):
                for k in range(NK):
                    w_f[k, at(m, b), :] = w[k * BLOCK:(k + 1) * BLOCK, b * LANES:(b + 1) * LANES]

    def attention():
        @pl.when(c == 0)
        def _():
            for copy in halo:
                copy.wait_recv()

        @pl.when(c == 1)
        def _():
            hk[...] = kk[group, 0]
            hv[...] = vv[group, 0]

        q = qq[c]
        inv = jnp.sqrt(jnp.float32(DH))
        before = dot_nt(q, hk[...]) / inv
        here = dot_nt(q, kk[group, c]) / inv
        t_q = lax.broadcasted_iota(jnp.int32, (T, T), 0)
        t_k = lax.broadcasted_iota(jnp.int32, (T, T), 1)
        before = jnp.where((t_k > t_q) & (s > 0), before, jnp.float32(-1e30))
        here = jnp.where(t_k <= t_q, here, jnp.float32(-1e30))
        top = jnp.maximum(jnp.max(before, axis=1, keepdims=True), jnp.max(here, axis=1, keepdims=True))
        before, here = jnp.exp(before - top), jnp.exp(here - top)
        norm = jnp.sum(before, axis=1, keepdims=True) + jnp.sum(here, axis=1, keepdims=True)
        before, here = (before / norm).astype(BF16), (here / norm).astype(BF16)
        attn[...] = dot_nn(before, hv[...]) + dot_nn(here, vv[group, c])

    last_chip = chip == NK * nz - 1

    def start_halo():
        for copy in halo:
            copy.start()

    @pl.when(span == 0)
    def _():
        for give in gives:
            give.start()
        for share in shares:
            share.start()
        pl.when((c == 1) & last_chip)(start_halo)
        for k, give in enumerate(gives):
            give.wait_recv()
            g_send0[k] = (g_own[k] + g_got[k].astype(F32)).astype(BF16)
        scatter0()
        initial_weights()
        for share in shares:
            share.wait_recv()
        scatter0_end()
        gather0()
        pl.when((c == 1) & jnp.logical_not(last_chip))(start_halo)
        attention()
        arrived(landy.at[pl.ds(0, fourth), pl.ds(0, NK - 1)], fy_recv.at[0])

    @pl.when(span == 1)
    def _():
        for share in shares:
            share.start()
        pl.when(c == 1)(start_halo)
        for target, _ in pairs:
            for j, ref in enumerate(group_of):
                own = ref.at[group, c]
                remote(own, own, col_send.at[j], col_recv.at[j, group], target).start()
        initial_weights()
        gather0()
        for _, k in pairs:
            for j, ref in enumerate(group_of):
                block = ref.at[k, c]
                arrived(block, col_recv.at[j, k])
                remote(block, block, fwd_send.at[j], fwd_recv.at[j, k], partner).start()
        for share in shares:
            share.wait_recv()
        attention()
        for _, k in pairs:
            for j, ref in enumerate(group_of):
                arrived(ref.at[k, 1 - c], fwd_recv.at[j, k])
        arrived(landy.at[pl.ds(0, fourth)], fy_recv.at[0])

    def row_scales(p, g_all):
        ss_own[p] = jnp.zeros((16, LANES), F32)
        for m in range(3):
            for b in range(NL):
                g = g_all[:, at(m, b), :].astype(F32)
                ss_own[p, m * NL + b:m * NL + b + 1, :] = jnp.sum(jnp.sum(g * g, axis=0), axis=0, keepdims=True)
        swap = remote(ss_own.at[p], ss_got.at[p], ss_send.at[p], ss_recv.at[p], partner)
        swap.start()
        swap.wait()

    def descend(p, g_all, blocks):
        scale = 0.05 * lax.rsqrt((ss_own[p] + ss_got[p]) * (1.0 / FH) + 1e-06)
        for k in blocks:
            for m in range(3):
                for b in range(NL):
                    j = m * NL + b
                    new = w_f[k, at(m, b), :] - g_all[k, at(m, b), :].astype(F32) * scale[j:j + 1]
                    w_f[k, at(m, b), :] = new
                    first = m * HALF + k * BLOCK
                    place = slice(first, first + BLOCK) if isinstance(k, int) else pl.ds(pl.multiple_of(first, BLOCK), BLOCK)
                    for i, term in enumerate(split(new)):
                        w_b[i, place, b * LANES:(b + 1) * LANES] = term

    gathered(0, y_first0, nz - fourth)
    row_scales(0, g_all0)

    @pl.when(span == 0)
    def _():
        descend(0, g_all0, range(NK))

    def gradient1():
        n = 2 * NK * T
        x, y_val = kk[...].reshape(n, DH), vv[...].reshape(n, DH)
        minus_r = -jnp.concatenate([rr[k, i][0:1] for k in range(NK) for i in range(2)], axis=1)

        def block(i, m):
            return w_b[i, pl.ds(pl.multiple_of(m * HALF + group * BLOCK, BLOCK), BLOCK), :]

        h = dot_nt(jnp.concatenate([block(0, 0), block(0, 1), block(1, 0), block(1, 1)], axis=0), x)
        h = h[:2 * BLOCK] + h[2 * BLOCK:]
        dg = dot_nt(jnp.concatenate([block(0, 2), block(1, 2)], axis=0), y_val)
        dg = (dg[:BLOCK] + dg[BLOCK:]) * minus_r
        a_gate, a_up, a_down = slopes(h[:BLOCK], h[BLOCK:], dg, minus_r)
        on_x = dot_nn(jnp.concatenate([a_gate, a_up], axis=0).astype(BF16), x).astype(BF16)
        on_y = dot_nn(a_down.astype(BF16), y_val).astype(BF16)
        for m, grad in enumerate((on_x[:BLOCK], on_x[BLOCK:], on_y)):
            for b in range(NL):
                g_send1[at(m, b), :] = grad[:, b * LANES:(b + 1) * LANES]

    @pl.when(span == 1)
    def _():
        descend(0, g_all0, [group])
        gradient1()

        def counterpart(i):
            k = lax.rem(line + 2 - 2 * lax.rem(i, 2), NK)
            zt = 2 * lax.rem(z // 2 + far_first(i // 2, half), half) + right
            return k // 2 * half + zt // 2, seq_at(NK + k, zt)

        mine = line // 2 * half + z // 2
        fan(nz, counterpart, lambda i: g_send1.at[part(i)], lambda i: land1.at[mine], r1_send, r1_recv)
        descend(0, g_all0, [lax.rem(group + i, NK) for i in range(1, NK)])
        arrived(land1, r1_recv)
        g_all1[group, part(mine), :] = total(land1)
        gather1()
        arrived(landy.at[:, pl.ds(0, NK - 1)], fy_recv.at[1])
        gathered(1, y_first, half)
        row_scales(1, g_all1)
        descend(1, g_all1, range(NK))

    def apply():
        def half_sum(q):
            h1 = dot_nt(q, w_b[0, 0:HALF]) + dot_nt(q, w_b[1, 0:HALF])
            h3 = dot_nt(q, w_b[0, HALF:2 * HALF]) + dot_nt(q, w_b[1, HALF:2 * HALF])
            high, low = split(h1 * jax.nn.sigmoid(h1) * h3)
            w_high, w_low = w_b[0, 2 * HALF:3 * HALF], w_b[1, 2 * HALF:3 * HALF]
            return dot_nn(high, w_high) + (dot_nn(low, w_high) + dot_nn(high, w_low))

        f_give[...] = half_sum(qq[1 - c]).astype(BF16)
        swap = remote(f_give, f_got, f_send, f_recv, partner)
        swap.start()
        mine = half_sum(qq[c])
        swap.wait()
        f = mine + f_got[...].astype(F32)
        fast = (f * lax.rsqrt(jnp.mean(f * f, axis=1, keepdims=True) + 1e-06)).astype(BF16)
        out_ref[...] = (attn[...] + fast.astype(F32)).astype(BF16)

    apply()

    def left(whole, sem, one_stayed):
        @pl.when(one_stayed)
        def _():
            arrived(whole(1), sem)

        @pl.when(jnp.logical_not(one_stayed))
        def _():
            arrived(whole(0), sem)

    most = g_all0.at[:, pl.ds(0, ROWS - rows)]
    three = finy.at[pl.ds(0, NK - 1)]
    z_first = jnp.logical_not(y_first)
    for share in shares:
        share.wait_send()

    @pl.when(c == 1)
    def _():
        for copy in halo:
            copy.wait_send()

    @pl.when(y_first0)
    def _():
        arrived(most, z_send.at[0])

    @pl.when(span == 0)
    def _():
        for give in gives:
            give.wait_send()
        left(lambda n: landz.at[:, pl.ds(0, half - n)], az_send, y_first)
        arrived(landy.at[:, pl.ds(0, NK - 1)], ay_send)
        left(lambda n: finz.at[pl.ds(0, half - n)], bz_send, z_first)
        arrived(landy.at[pl.ds(0, fourth)], fy_send.at[0])
        arrived(landy.at[pl.ds(0, fourth), pl.ds(0, NK - 1)], fy_send.at[1])

        @pl.when(y_first)
        def _():
            arrived(landp, p_send.at[0])
            arrived(landp.at[:, pl.ds(0, NK - 1)], p_send.at[1])

        @pl.when(y_first0 & z_first)
        def _():
            arrived(finy, y_send.at[0])
            arrived(three, y_send.at[1])

        @pl.when(jnp.logical_not(y_first0))
        def _():
            arrived(finz.at[pl.ds(0, nz - 1)], zy_send.at[0])

    @pl.when(span == 1)
    def _():
        for j, ref in enumerate(group_of):
            arrived(ref.at[pl.ds(0, 3), 0], col_send.at[j])
            arrived(ref.at[pl.ds(0, 3), 0], fwd_send.at[j])
        arrived(land1.at[pl.ds(0, nz - 1)], r1_send)
        arrived(landy.at[:, pl.ds(0, NK - 1)], fy_send.at[0])

        @pl.when(y_first)
        def _():
            arrived(three, y_send.at[0])
            arrived(most, z_send.at[1])

        @pl.when(z_first)
        def _():
            arrived(finz.at[pl.ds(0, nz - 1)], zy_send.at[1])


def local(ny, nz, queries, keys, values, rates, gate_fast, up_fast, down_fast):
    rows = ROWS // nz
    dma = pltpu.SemaphoreType.DMA
    full = (NK, ROWS, LANES)
    return pl.pallas_call(
        functools.partial(kernel, ny, nz),
        out_shape=jax.ShapeDtypeStruct((T, DH), BF16),
        in_specs=[pl.BlockSpec(memory_space=pl.ANY)] * 7,
        out_specs=pl.BlockSpec(memory_space=pltpu.VMEM),
        scratch_shapes=[
            pltpu.VMEM((2, T, DH), BF16),
            pltpu.VMEM((NK, 2, T, DH), BF16),
            pltpu.VMEM((NK, 2, T, DH), BF16),
            pltpu.VMEM((NK, 2, 8, LANES), F32),
            pltpu.VMEM((T, DH), BF16),
            pltpu.VMEM((T, DH), BF16),
            pltpu.VMEM((1, T), F32),
            pltpu.VMEM((3, DH, FH), BF16),
            pltpu.VMEM(full, F32),
            pltpu.VMEM((2, 3 * HALF, DH), BF16),
            pltpu.VMEM(full, F32),
            pltpu.VMEM(full, BF16),
            pltpu.VMEM(full, BF16),
            pltpu.VMEM(full, BF16),
            pltpu.VMEM((ROWS, LANES), BF16),
            pltpu.VMEM(full, BF16),
            pltpu.VMEM(full, BF16),
            pltpu.VMEM((NK, nz, rows, LANES), BF16),
            pltpu.VMEM((NK, rows, LANES), BF16),
            pltpu.VMEM((NK, NK, rows, LANES), BF16),
            pltpu.VMEM((NK, rows, LANES), BF16),
            pltpu.VMEM((nz // 2, NK, rows, LANES), BF16),
            pltpu.VMEM((nz // 2, rows, LANES), BF16),
            pltpu.VMEM((nz, rows, LANES), BF16),
            pltpu.VMEM((nz, rows, LANES), BF16),
            pltpu.VMEM((2, 16, LANES), F32),
            pltpu.VMEM((2, 16, LANES), F32),
            pltpu.VMEM((T, DH), F32),
            pltpu.VMEM((T, DH), BF16),
            pltpu.VMEM((T, DH), BF16),
            dma((7,)),
            dma((4,)),
            dma((4,)),
            dma((2,)),
            dma((2,)),
            dma((NK,)),
            dma((NK,)),
            dma((3,)),
            dma((3, NK)),
            dma((3,)),
            dma((3, NK)),
            dma,
            dma((NK,)),
            dma,
            dma((nz // 2,)),
            dma,
            dma,
            dma((2,)),
            dma((NK,)),
            dma,
            dma,
            dma((2,)),
            dma((2, NK)),
            dma((2,)),
            dma((2,)),
            dma((2,)),
            dma((2, nz)),
            dma((2,)),
            dma((2,)),
            dma((2,)),
            dma((2,)),
            dma,
            dma,
        ],
        compiler_params=pltpu.CompilerParams(
            collective_id=0, has_side_effects=True, vmem_limit_bytes=55040 * 1024
        ),
        name="fast_layer",
    )(queries, keys, values, rates.reshape(1, T), gate_fast, up_fast, down_fast)


def solution(mesh):
    ny = 2 * NK
    nz = mesh.shape["seq"] // 2 // ny
    return jax.shard_map(
        functools.partial(local, ny, nz),
        mesh=mesh,
        in_specs=(
            P("seq", "head"),
            P("seq", "head"),
            P("seq", "head"),
            P("seq", "head"),
            P("head", None, None),
            P("head", None, None),
            P("head", None, None),
        ),
        out_specs=P("seq", "head"),
        check_vma=False,
    )
```

```python
import functools
import math

import jax
import jax.numpy as jnp
from jax import lax
from jax.experimental import pallas as pl
from jax.experimental.pallas import tpu as pltpu
from jax.sharding import PartitionSpec as P

T = 128
DH = 512
FH = 256
HALF = 128
LANES = 128
NL = DH // LANES
NK = 4
BLOCK = HALF // NK
ROWS = NL * 3 * BLOCK
MESH = pl.DeviceIdType.MESH
F32 = jnp.float32
BF16 = jnp.bfloat16


def dot_nt(a, b):
    return lax.dot_general(a, b, (((1,), (1,)), ((), ())), preferred_element_type=F32)


def dot_nn(a, b):
    return jnp.dot(a, b, preferred_element_type=F32)


def split(a):
    high = a.astype(BF16)
    return high, (a - high.astype(F32)).astype(BF16)


def far_first(j, n):
    h = (j + 1) // 2
    return lax.rem(n // 2 + n + jnp.where(lax.rem(j, 2) == 1, -h, h), n)


def far_offsets(n):
    return sorted(range(1, n), key=lambda d: -min(d, n - d))


def kernel(
    ny, nz,
    q_hbm, k_hbm, v_hbm, r_hbm, wg_hbm, wu_hbm, wd_hbm,
    out_ref,
    qq, kk, vv, rr, hk, hv, r_in, w_in, w_f, w_b,
    g_own, g_give, g_got, g_send0, g_send1, g_all0, g_all1,
    landz, midz, landp, finy, landy, midy, finz, land1,
    ss_own, ss_got, attn, f_give, f_got,
    in_sem, x_send, x_recv, h_send, h_recv, gh_send, gh_recv, col_send, col_recv, fwd_send, fwd_recv,
    az_send, az_recv, ay_send, ay_recv, bz_send, bz_recv, p_send, p_recv, r1_send, r1_recv,
    y_send, y_recv, z_send, z_recv, zy_send, zy_recv, fy_send, fy_recv,
    ss_send, ss_recv, f_send, f_recv,
):
    s = lax.axis_index("seq")
    c = lax.rem(s, 2)
    chip = s // 2
    z = lax.rem(chip, nz)
    y = chip // nz
    rows = ROWS // nz
    n_seq = ny * nz * 2
    span = y // NK
    line = y - span * NK
    partner = s + 1 - 2 * c
    half = nz // 2
    y_first = lax.rem(z + c, 2) == 0
    fourth = nz // 4
    y_first0 = lax.rem(z + c, 4) != 3
    up, right = lax.rem(line, 2), lax.rem(z, 2)
    group = up * 2 + right

    def seq_at(row, column):
        return (row * nz + column) * 2 + c

    loads = [
        pltpu.make_async_copy(k_hbm, kk.at[group, c], in_sem.at[0]),
        pltpu.make_async_copy(v_hbm, vv.at[group, c], in_sem.at[1]),
        pltpu.make_async_copy(r_hbm, r_in, in_sem.at[2]),
        pltpu.make_async_copy(wg_hbm.at[0], w_in.at[0], in_sem.at[3]),
        pltpu.make_async_copy(wu_hbm.at[0], w_in.at[1], in_sem.at[4]),
        pltpu.make_async_copy(wd_hbm.at[0], w_in.at[2], in_sem.at[5]),
        pltpu.make_async_copy(q_hbm, qq.at[c], in_sem.at[6]),
    ]
    for load in loads:
        load.start()

    barrier = pltpu.get_barrier_semaphore()

    def greet(target):
        pl.semaphore_signal(barrier, inc=1, device_id={"seq": target}, device_id_type=MESH)

    for d in far_offsets(ny):
        greet(seq_at(lax.rem(y + d, ny), z))
    for d in far_offsets(nz):
        greet(seq_at(y, lax.rem(z + d, nz)))
    beside = lax.rem(s + 2 * c - 1 + n_seq, n_seq)
    greet(beside)
    greet(partner)
    y_pair, z_pair = y + 1 - 2 * up, z + 1 - 2 * right
    pairs = [
        (seq_at(y_pair, z_pair), (1 - up) * 2 + 1 - right),
        (seq_at(y_pair, z), (1 - up) * 2 + right),
        (seq_at(y, z_pair), up * 2 + 1 - right),
    ]
    greet(pairs[0][0])
    other_row = y - line + lax.rem(line + 2, NK)
    for d in range(1, half):
        greet(seq_at(other_row, lax.rem(z + 2 * d, nz)))

    for load in loads:
        load.wait()
    rr[group, c] = jnp.broadcast_to(r_in[...], (8, LANES))

    def slopes(h1, h3, dg, rate):
        sig = jax.nn.sigmoid(h1)
        s1 = h1 * sig
        a_gate = dg * h3 * sig * (1.0 + h1 * (1.0 - sig))
        return a_gate, dg * s1, (s1 * h3) * rate

    def at(m, b):
        first = (b * 3 + m) * BLOCK
        return slice(first, first + BLOCK)

    @pl.when(span == 0)
    def _():
        x, y_val = kk[group, c], vv[group, c]
        minus_r = -jnp.broadcast_to(r_in[...], (LANES, T)).T[:, 0:1]
        acts = slopes(dot_nn(x, w_in[0]), dot_nn(x, w_in[1]), dot_nn(y_val, w_in[2]) * minus_r, minus_r)
        for m in range(3):
            grad = dot_nn(acts[m].T.astype(BF16), x if m < 2 else y_val)
            low, high = grad[:HALF], grad[HALF:]
            mine = jnp.where(c == 0, low, high)
            theirs = jnp.where(c == 0, high, low).astype(BF16)
            for b in range(NL):
                for k in range(NK):
                    g_own[k, at(m, b), :] = mine[k * BLOCK:(k + 1) * BLOCK, b * LANES:(b + 1) * LANES]
                    g_give[k, at(m, b), :] = theirs[k * BLOCK:(k + 1) * BLOCK, b * LANES:(b + 1) * LANES]

    pl.semaphore_wait(barrier, ny + nz + half)

    def remote(src, dst, send, recv, target):
        return pltpu.make_async_remote_copy(
            src_ref=src, dst_ref=dst, send_sem=send, recv_sem=recv, device_id={"seq": target}, device_id_type=MESH
        )

    def fan(n, place, src, dst, send, recv):
        def one(i, carry):
            index, target = place(i)
            from_ref, to_ref = src(index), dst(index)

            @pl.when(target == s)
            def _():
                pltpu.make_async_copy(from_ref, to_ref, recv).start()

            @pl.when(target != s)
            def _():
                remote(from_ref, to_ref, send, recv, target).start()

            return carry

        lax.fori_loop(0, n, one, 0)

    def along_z(i):
        zt = lax.rem(z + far_first(i, nz), nz)
        return zt, seq_at(y, zt)

    def column(i, kind):
        return 2 * lax.rem(z // 2 + far_first(i, half), half) + (c if kind == 0 else 1 - c)

    def row(i):
        return lax.rem(line + i, NK)

    def across(i):
        return jnp.where(line < 2, i, NK - 1 - i)

    def near(i):
        back = line >= 2
        me = jnp.where(back, NK - 1 - line, line)
        k = i - 1 + (i - 1 >= me).astype(jnp.int32)
        return jnp.where(back, NK - 1 - k, k)

    def part(i):
        return pl.ds(pl.multiple_of(i * rows, 16), rows)

    def arrived(ref, sem):
        pltpu.make_async_copy(ref, ref, sem).wait()

    def total(ref):
        out = ref[0].astype(F32)
        for i in range(1, ref.shape[0]):
            out = out + ref[i].astype(F32)
        return out.astype(BF16)

    gives = [remote(g_give.at[k], g_got.at[k], gh_send.at[k], gh_recv.at[k], partner) for k in range(NK)]
    shares = [
        remote(ref, ref, x_send.at[i], x_recv.at[i], partner)
        for i, ref in enumerate((kk.at[group, c], vv.at[group, c], rr.at[group, c], qq.at[c]))
    ]
    halo = [
        remote(src.at[group, c], dst, h_send.at[i], h_recv.at[i], beside)
        for i, (src, dst) in enumerate(((kk, hk), (vv, hv)))
    ]
    group_of = (kk, vv, rr)

    def scatter0():
        first = y - line

        def send(i, carry):
            k = i

            def place_z(j):
                zt = column(j, 0)
                return zt, seq_at(y, zt)

            fan(half, place_z, lambda zt: g_send0.at[k, part(zt)], lambda zt: landz.at[k, z], az_send, az_recv.at[k])
            return carry

        def send_y(i, carry):
            zt = column(i, 1)

            def place_y(j):
                k = row(j + 1)
                return k, seq_at(first + k, z)

            fan(NK, place_y, lambda k: g_send0.at[k, part(zt)], lambda k: landy.at[zt // 2, line], ay_send, ay_recv.at[zt // 2])
            return carry

        for i in range(max(NK, half)):
            if i < NK:
                send(i, 0)
            if i < half:
                send_y(i, 0)

    def scatter0_end():
        def add_z(k):
            arrived(landz.at[k], az_recv.at[k])
            midz[k] = total(landz.at[k])
            pltpu.make_async_copy(midz.at[k], landp.at[k, line], p_recv.at[k]).start()
            for i in range(NK):
                remote(midz.at[k], landp.at[k, line], p_send.at[0], p_recv.at[k], seq_at(NK + across(i), z)).start()

        def add_y(i):
            zt = column(i, 1)
            j = zt // 2
            arrived(landy.at[j], ay_recv.at[j])
            midy[j] = total(landy.at[j])

            @pl.when(zt == z)
            def _():
                pltpu.make_async_copy(midy.at[j], finz.at[z], bz_recv).start()

            @pl.when(zt != z)
            def _():
                remote(midy.at[j], finz.at[z], bz_send, bz_recv, seq_at(y, zt)).start()

        for i in range(max(NK, half)):
            if i < half:
                add_y(i)
            if i < NK:

                @pl.when(y_first)
                def _():
                    add_z(i)

        @pl.when(jnp.logical_not(y_first))
        def _():
            arrived(finz, bz_recv)
            g_all0[line, part(z), :] = total(finz)

    def to_z(block, send, recv):
        def one(i, carry):
            _, target = along_z(i)
            remote(block, block, send, recv, target).start()
            return carry

        lax.fori_loop(0, nz - 1, one, 0)

    def to_own_span(block, send, recv):
        for i in range(NK - 1, 0, -1):
            remote(block, block, send, recv, seq_at(y - line + near(i), z)).start()

    def to_span1(block, send, recv):
        for i in range(NK):
            remote(block, block, send, recv, seq_at(NK + across(i), z)).start()

    def gather0():
        def block(k, zt):
            return g_all0.at[k, part(zt)]

        def column0(i):
            return 4 * lax.rem(z // 4 + i, fourth) + 3 - c

        own = block(line, z)

        def forward_z(k):
            arrived(block(k, z), y_recv.at[0, k])
            to_z(block(k, z), z_send.at[0], z_recv.at[0])

        def add_rows(k):
            arrived(landp.at[k], p_recv.at[k])
            g_all0[k, part(z), :] = total(landp.at[k])
            to_z(block(k, z), z_send.at[0], z_recv.at[0])

        owner_y = y_first0 & jnp.logical_not(y_first)

        @pl.when(span == 0)
        def _():
            @pl.when(owner_y)
            def _():
                to_span1(own, y_send.at[0], y_recv.at[0, line])
                to_own_span(own, y_send.at[1], y_recv.at[0, line])

            @pl.when(jnp.logical_not(y_first0))
            def _():
                to_z(own, zy_send.at[0], zy_recv.at[0, z])
                to_span1(own, fy_send.at[0], fy_recv.at[0])

            for i in range(fourth):
                zt = column0(i)

                @pl.when(zt != z)
                def _():
                    arrived(block(line, zt), zy_recv.at[0, zt])
                    to_span1(block(line, zt), fy_send.at[0], fy_recv.at[0])

            for i in range(fourth):
                to_own_span(block(line, column0(i)), fy_send.at[1], fy_recv.at[0])

            @pl.when(y_first)
            def _():
                for k in range(NK):
                    for i in range(1, NK):
                        remote(midz.at[k], landp.at[k, line], p_send.at[1], p_recv.at[k], seq_at(row(i), z)).start()

            @pl.when(owner_y)
            def _():
                to_z(own, z_send.at[0], z_recv.at[0])
                for i in range(1, NK):
                    forward_z(row(i))

        @pl.when((span == 1) & owner_y)
        def _():
            for i in range(NK):
                forward_z(jnp.where(line >= 2, i, NK - 1 - i))

        @pl.when(y_first)
        def _():
            for k in range(NK):
                add_rows(k)

    def gathered(p, along_y_first, columns):
        @pl.when(along_y_first)
        def _():
            arrived(landz.at[:, pl.ds(0, columns - 1)], z_recv.at[p])

        @pl.when(jnp.logical_not(along_y_first))
        def _():
            arrived(landz.at[:, pl.ds(0, columns)], z_recv.at[p])

    def place1(k, zt):
        return g_all1.at[lax.rem(k, 2) * 2 + lax.rem(zt, 2), part(k // 2 * half + zt // 2)]

    def gather1():
        own = place1(line, z)

        @pl.when(y_first)
        def _():
            to_own_span(own, y_send.at[0], y_recv.at[1, line])
            to_z(own, z_send.at[1], z_recv.at[1])

        @pl.when(jnp.logical_not(y_first))
        def _():
            to_z(own, zy_send.at[1], zy_recv.at[1, z])
            to_own_span(own, fy_send.at[0], fy_recv.at[1])

        for i in range(max(NK, half)):
            if 1 <= i < NK:

                @pl.when(y_first)
                def _():
                    k = near(i)
                    arrived(place1(k, z), y_recv.at[1, k])
                    to_z(place1(k, z), z_send.at[1], z_recv.at[1])

            if i < half:
                zt = column(half - 1 - i, 1)

                @pl.when(zt != z)
                def _():
                    arrived(place1(line, zt), zy_recv.at[1, zt])
                    to_own_span(place1(line, zt), fy_send.at[0], fy_recv.at[1])

    def initial_weights():
        first = pl.multiple_of(c * HALF, HALF)
        for m in range(3):
            w = w_in[m, :, pl.ds(first, HALF)].astype(F32).T
            for b in range(NL):
                for k in range(NK):
                    w_f[k, at(m, b), :] = w[k * BLOCK:(k + 1) * BLOCK, b * LANES:(b + 1) * LANES]

    def attention():
        @pl.when(c == 0)
        def _():
            for copy in halo:
                copy.wait_recv()

        @pl.when(c == 1)
        def _():
            hk[...] = kk[group, 0]
            hv[...] = vv[group, 0]

        q = qq[c]
        inv = jnp.sqrt(jnp.float32(DH))
        before = dot_nt(q, hk[...]) / inv
        here = dot_nt(q, kk[group, c]) / inv
        t_q = lax.broadcasted_iota(jnp.int32, (T, T), 0)
        t_k = lax.broadcasted_iota(jnp.int32, (T, T), 1)
        before = jnp.where((t_k > t_q) & (s > 0), before, jnp.float32(-1e30))
        here = jnp.where(t_k <= t_q, here, jnp.float32(-1e30))
        top = jnp.maximum(jnp.max(before, axis=1, keepdims=True), jnp.max(here, axis=1, keepdims=True))
        before, here = jnp.exp(before - top), jnp.exp(here - top)
        norm = jnp.sum(before, axis=1, keepdims=True) + jnp.sum(here, axis=1, keepdims=True)
        before, here = (before / norm).astype(BF16), (here / norm).astype(BF16)
        attn[...] = dot_nn(before, hv[...]) + dot_nn(here, vv[group, c])

    last_chip = chip == NK * nz - 1

    def start_halo():
        for copy in halo:
            copy.start()

    @pl.when(span == 0)
    def _():
        for give in gives:
            give.start()
        for share in shares:
            share.start()
        pl.when((c == 1) & last_chip)(start_halo)
        for k, give in enumerate(gives):
            give.wait_recv()
            g_send0[k] = (g_own[k] + g_got[k].astype(F32)).astype(BF16)
        scatter0()
        initial_weights()
        for share in shares:
            share.wait_recv()
        scatter0_end()
        gather0()
        pl.when((c == 1) & jnp.logical_not(last_chip))(start_halo)
        attention()
        arrived(landy.at[pl.ds(0, fourth), pl.ds(0, NK - 1)], fy_recv.at[0])

    @pl.when(span == 1)
    def _():
        for share in shares:
            share.start()
        pl.when(c == 1)(start_halo)
        for target, _ in pairs:
            for j, ref in enumerate(group_of):
                own = ref.at[group, c]
                remote(own, own, col_send.at[j], col_recv.at[j, group], target).start()
        initial_weights()
        gather0()
        for _, k in pairs:
            for j, ref in enumerate(group_of):
                block = ref.at[k, c]
                arrived(block, col_recv.at[j, k])
                remote(block, block, fwd_send.at[j], fwd_recv.at[j, k], partner).start()
        for share in shares:
            share.wait_recv()
        attention()
        for _, k in pairs:
            for j, ref in enumerate(group_of):
                arrived(ref.at[k, 1 - c], fwd_recv.at[j, k])
        arrived(landy.at[pl.ds(0, fourth)], fy_recv.at[0])

    def row_scales(p, g_all):
        ss_own[p] = jnp.zeros((16, LANES), F32)
        for m in range(3):
            for b in range(NL):
                g = g_all[:, at(m, b), :].astype(F32)
                ss_own[p, m * NL + b:m * NL + b + 1, :] = jnp.sum(jnp.sum(g * g, axis=0), axis=0, keepdims=True)
        swap = remote(ss_own.at[p], ss_got.at[p], ss_send.at[p], ss_recv.at[p], partner)
        swap.start()
        swap.wait()

    def descend(p, g_all, blocks):
        scale = 0.05 * lax.rsqrt((ss_own[p] + ss_got[p]) * (1.0 / FH) + 1e-06)
        for k in blocks:
            for m in range(3):
                for b in range(NL):
                    j = m * NL + b
                    new = w_f[k, at(m, b), :] - g_all[k, at(m, b), :].astype(F32) * scale[j:j + 1]
                    w_f[k, at(m, b), :] = new
                    first = m * HALF + k * BLOCK
                    place = slice(first, first + BLOCK) if isinstance(k, int) else pl.ds(pl.multiple_of(first, BLOCK), BLOCK)
                    for i, term in enumerate(split(new)):
                        w_b[i, place, b * LANES:(b + 1) * LANES] = term

    gathered(0, y_first0, nz - fourth)
    row_scales(0, g_all0)

    @pl.when(span == 0)
    def _():
        descend(0, g_all0, range(NK))

    def gradient1():
        n = 2 * NK * T
        x, y_val = kk[...].reshape(n, DH), vv[...].reshape(n, DH)
        minus_r = -jnp.concatenate([rr[k, i][0:1] for k in range(NK) for i in range(2)], axis=1)

        def block(i, m):
            return w_b[i, pl.ds(pl.multiple_of(m * HALF + group * BLOCK, BLOCK), BLOCK), :]

        h = dot_nt(jnp.concatenate([block(0, 0), block(0, 1), block(1, 0), block(1, 1)], axis=0), x)
        h = h[:2 * BLOCK] + h[2 * BLOCK:]
        dg = dot_nt(jnp.concatenate([block(0, 2), block(1, 2)], axis=0), y_val)
        dg = (dg[:BLOCK] + dg[BLOCK:]) * minus_r
        a_gate, a_up, a_down = slopes(h[:BLOCK], h[BLOCK:], dg, minus_r)
        on_x = dot_nn(jnp.concatenate([a_gate, a_up], axis=0).astype(BF16), x).astype(BF16)
        on_y = dot_nn(a_down.astype(BF16), y_val).astype(BF16)
        for m, grad in enumerate((on_x[:BLOCK], on_x[BLOCK:], on_y)):
            for b in range(NL):
                g_send1[at(m, b), :] = grad[:, b * LANES:(b + 1) * LANES]

    @pl.when(span == 1)
    def _():
        descend(0, g_all0, [group])
        gradient1()

        def counterpart(i):
            k = lax.rem(line + 2 - 2 * lax.rem(i, 2), NK)
            zt = 2 * lax.rem(z // 2 + far_first(i // 2, half), half) + right
            return k // 2 * half + zt // 2, seq_at(NK + k, zt)

        mine = line // 2 * half + z // 2
        fan(nz, counterpart, lambda i: g_send1.at[part(i)], lambda i: land1.at[mine], r1_send, r1_recv)
        descend(0, g_all0, [lax.rem(group + i, NK) for i in range(1, NK)])
        arrived(land1, r1_recv)
        g_all1[group, part(mine), :] = total(land1)
        gather1()
        arrived(landy.at[:, pl.ds(0, NK - 1)], fy_recv.at[1])
        gathered(1, y_first, half)
        row_scales(1, g_all1)
        descend(1, g_all1, range(NK))

    def apply():
        def half_sum(q):
            h1 = dot_nt(q, w_b[0, 0:HALF]) + dot_nt(q, w_b[1, 0:HALF])
            h3 = dot_nt(q, w_b[0, HALF:2 * HALF]) + dot_nt(q, w_b[1, HALF:2 * HALF])
            high, low = split(h1 * jax.nn.sigmoid(h1) * h3)
            w_high, w_low = w_b[0, 2 * HALF:3 * HALF], w_b[1, 2 * HALF:3 * HALF]
            return dot_nn(high, w_high) + (dot_nn(low, w_high) + dot_nn(high, w_low))

        f_give[...] = half_sum(qq[1 - c]).astype(BF16)
        swap = remote(f_give, f_got, f_send, f_recv, partner)
        swap.start()
        mine = half_sum(qq[c])
        swap.wait()
        f = mine + f_got[...].astype(F32)
        fast = (f * lax.rsqrt(jnp.mean(f * f, axis=1, keepdims=True) + 1e-06)).astype(BF16)
        out_ref[...] = (attn[...] + fast.astype(F32)).astype(BF16)

    apply()

    def left(whole, sem, one_stayed):
        @pl.when(one_stayed)
        def _():
            arrived(whole(1), sem)

        @pl.when(jnp.logical_not(one_stayed))
        def _():
            arrived(whole(0), sem)

    most = g_all0.at[:, pl.ds(0, ROWS - rows)]
    three = finy.at[pl.ds(0, NK - 1)]
    z_first = jnp.logical_not(y_first)
    for share in shares:
        share.wait_send()

    @pl.when(c == 1)
    def _():
        for copy in halo:
            copy.wait_send()

    @pl.when(y_first0)
    def _():
        arrived(most, z_send.at[0])

    @pl.when(span == 0)
    def _():
        for give in gives:
            give.wait_send()
        left(lambda n: landz.at[:, pl.ds(0, half - n)], az_send, y_first)
        arrived(landy.at[:, pl.ds(0, NK - 1)], ay_send)
        left(lambda n: finz.at[pl.ds(0, half - n)], bz_send, z_first)
        arrived(landy.at[pl.ds(0, fourth)], fy_send.at[0])
        arrived(landy.at[pl.ds(0, fourth), pl.ds(0, NK - 1)], fy_send.at[1])

        @pl.when(y_first)
        def _():
            arrived(landp, p_send.at[0])
            arrived(landp.at[:, pl.ds(0, NK - 1)], p_send.at[1])

        @pl.when(y_first0 & z_first)
        def _():
            arrived(finy, y_send.at[0])
            arrived(three, y_send.at[1])

        @pl.when(jnp.logical_not(y_first0))
        def _():
            arrived(finz.at[pl.ds(0, nz - 1)], zy_send.at[0])

    @pl.when(span == 1)
    def _():
        for j, ref in enumerate(group_of):
            arrived(ref.at[pl.ds(0, 3), 0], col_send.at[j])
            arrived(ref.at[pl.ds(0, 3), 0], fwd_send.at[j])
        arrived(land1.at[pl.ds(0, nz - 1)], r1_send)
        arrived(landy.at[:, pl.ds(0, NK - 1)], fy_send.at[0])

        @pl.when(y_first)
        def _():
            arrived(three, y_send.at[0])
            arrived(most, z_send.at[1])

        @pl.when(z_first)
        def _():
            arrived(finz.at[pl.ds(0, nz - 1)], zy_send.at[1])


def local(ny, nz, queries, keys, values, rates, gate_fast, up_fast, down_fast):
    rows = ROWS // nz
    dma = pltpu.SemaphoreType.DMA
    full = (NK, ROWS, LANES)
    return pl.pallas_call(
        functools.partial(kernel, ny, nz),
        out_shape=jax.ShapeDtypeStruct((T, DH), BF16),
        in_specs=[pl.BlockSpec(memory_space=pl.ANY)] * 7,
        out_specs=pl.BlockSpec(memory_space=pltpu.VMEM),
        scratch_shapes=[
            pltpu.VMEM((2, T, DH), BF16),
            pltpu.VMEM((NK, 2, T, DH), BF16),
            pltpu.VMEM((NK, 2, T, DH), BF16),
            pltpu.VMEM((NK, 2, 8, LANES), F32),
            pltpu.VMEM((T, DH), BF16),
            pltpu.VMEM((T, DH), BF16),
            pltpu.VMEM((1, T), F32),
            pltpu.VMEM((3, DH, FH), BF16),
            pltpu.VMEM(full, F32),
            pltpu.VMEM((2, 3 * HALF, DH), BF16),
            pltpu.VMEM(full, F32),
            pltpu.VMEM(full, BF16),
            pltpu.VMEM(full, BF16),
            pltpu.VMEM(full, BF16),
            pltpu.VMEM((ROWS, LANES), BF16),
            pltpu.VMEM(full, BF16),
            pltpu.VMEM(full, BF16),
            pltpu.VMEM((NK, nz, rows, LANES), BF16),
            pltpu.VMEM((NK, rows, LANES), BF16),
            pltpu.VMEM((NK, NK, rows, LANES), BF16),
            pltpu.VMEM((NK, rows, LANES), BF16),
            pltpu.VMEM((nz // 2, NK, rows, LANES), BF16),
            pltpu.VMEM((nz // 2, rows, LANES), BF16),
            pltpu.VMEM((nz, rows, LANES), BF16),
            pltpu.VMEM((nz, rows, LANES), BF16),
            pltpu.VMEM((2, 16, LANES), F32),
            pltpu.VMEM((2, 16, LANES), F32),
            pltpu.VMEM((T, DH), F32),
            pltpu.VMEM((T, DH), BF16),
            pltpu.VMEM((T, DH), BF16),
            dma((7,)),
            dma((4,)),
            dma((4,)),
            dma((2,)),
            dma((2,)),
            dma((NK,)),
            dma((NK,)),
            dma((3,)),
            dma((3, NK)),
            dma((3,)),
            dma((3, NK)),
            dma,
            dma((NK,)),
            dma,
            dma((nz // 2,)),
            dma,
            dma,
            dma((2,)),
            dma((NK,)),
            dma,
            dma,
            dma((2,)),
            dma((2, NK)),
            dma((2,)),
            dma((2,)),
            dma((2,)),
            dma((2, nz)),
            dma((2,)),
            dma((2,)),
            dma((2,)),
            dma((2,)),
            dma,
            dma,
        ],
        compiler_params=pltpu.CompilerParams(
            collective_id=0, has_side_effects=True, vmem_limit_bytes=55040 * 1024
        ),
        name="fast_layer",
    )(queries, keys, values, rates.reshape(1, T), gate_fast, up_fast, down_fast)


def solution(mesh):
    ny = 2 * NK
    nz = mesh.shape["seq"] // 2 // ny
    return jax.shard_map(
        functools.partial(local, ny, nz),
        mesh=mesh,
        in_specs=(
            P("seq", "head"),
            P("seq", "head"),
            P("seq", "head"),
            P("seq", "head"),
            P("head", None, None),
            P("head", None, None),
            P("head", None, None),
        ),
        out_specs=P("seq", "head"),
        check_vma=False,
    )
```

```python
import functools
import math

import jax
import jax.numpy as jnp
from jax import lax
from jax.experimental import pallas as pl
from jax.experimental.pallas import tpu as pltpu
from jax.sharding import PartitionSpec as P

T = 128
DH = 512
FH = 256
HALF = 128
LANES = 128
NL = DH // LANES
NK = 4
BLOCK = HALF // NK
ROWS = NL * 3 * BLOCK
MESH = pl.DeviceIdType.MESH
F32 = jnp.float32
BF16 = jnp.bfloat16


def dot_nt(a, b):
    return lax.dot_general(a, b, (((1,), (1,)), ((), ())), preferred_element_type=F32)


def dot_nn(a, b):
    return jnp.dot(a, b, preferred_element_type=F32)


def split(a):
    high = a.astype(BF16)
    return high, (a - high.astype(F32)).astype(BF16)


def far_first(j, n):
    h = (j + 1) // 2
    return lax.rem(n // 2 + n + jnp.where(lax.rem(j, 2) == 1, -h, h), n)


def far_offsets(n):
    return sorted(range(1, n), key=lambda d: -min(d, n - d))


def kernel(
    ny, nz,
    q_hbm, k_hbm, v_hbm, r_hbm, wg_hbm, wu_hbm, wd_hbm,
    out_ref,
    qq, kk, vv, rr, hk, hv, r_in, w_in, w_f, w_b,
    g_own, g_give, g_got, g_send0, g_send1, g_all0, g_all1,
    landz, midz, landp, finy, landy, midy, finz, land1,
    ss_own, ss_got, attn, f_give, f_got,
    in_sem, x_send, x_recv, h_send, h_recv, gh_send, gh_recv, col_send, col_recv, fwd_send, fwd_recv,
    az_send, az_recv, ay_send, ay_recv, bz_send, bz_recv, p_send, p_recv, r1_send, r1_recv,
    y_send, y_recv, z_send, z_recv, zy_send, zy_recv, fy_send, fy_recv,
    ss_send, ss_recv, f_send, f_recv,
):
    s = lax.axis_index("seq")
    c = lax.rem(s, 2)
    chip = s // 2
    z = lax.rem(chip, nz)
    y = chip // nz
    rows = ROWS // nz
    n_seq = ny * nz * 2
    span = y // NK
    line = y - span * NK
    partner = s + 1 - 2 * c
    half = nz // 2
    y_first = lax.rem(z + c, 2) == 0
    fourth = nz // 4
    y_first0 = lax.rem(z + c, 4) != 3
    up, right = lax.rem(line, 2), lax.rem(z, 2)
    group = up * 2 + right

    def seq_at(row, column):
        return (row * nz + column) * 2 + c

    loads = [
        pltpu.make_async_copy(k_hbm, kk.at[group, c], in_sem.at[0]),
        pltpu.make_async_copy(v_hbm, vv.at[group, c], in_sem.at[1]),
        pltpu.make_async_copy(r_hbm, r_in, in_sem.at[2]),
        pltpu.make_async_copy(wg_hbm.at[0], w_in.at[0], in_sem.at[3]),
        pltpu.make_async_copy(wu_hbm.at[0], w_in.at[1], in_sem.at[4]),
        pltpu.make_async_copy(wd_hbm.at[0], w_in.at[2], in_sem.at[5]),
        pltpu.make_async_copy(q_hbm, qq.at[c], in_sem.at[6]),
    ]
    for load in loads:
        load.start()

    barrier = pltpu.get_barrier_semaphore()

    def greet(target):
        pl.semaphore_signal(barrier, inc=1, device_id={"seq": target}, device_id_type=MESH)

    for d in far_offsets(ny):
        greet(seq_at(lax.rem(y + d, ny), z))
    for d in far_offsets(nz):
        greet(seq_at(y, lax.rem(z + d, nz)))
    beside = lax.rem(s + 2 * c - 1 + n_seq, n_seq)
    greet(beside)
    greet(partner)
    y_pair, z_pair = y + 1 - 2 * up, z + 1 - 2 * right
    pairs = [
        (seq_at(y_pair, z_pair), (1 - up) * 2 + 1 - right),
        (seq_at(y_pair, z), (1 - up) * 2 + right),
        (seq_at(y, z_pair), up * 2 + 1 - right),
    ]
    greet(pairs[0][0])
    other_row = y - line + lax.rem(line + 2, NK)
    for d in range(1, half):
        greet(seq_at(other_row, lax.rem(z + 2 * d, nz)))

    for load in loads:
        load.wait()
    rr[group, c] = jnp.broadcast_to(r_in[...], (8, LANES))

    def slopes(h1, h3, dg, rate):
        sig = jax.nn.sigmoid(h1)
        s1 = h1 * sig
        a_gate = dg * h3 * sig * (1.0 + h1 * (1.0 - sig))
        return a_gate, dg * s1, (s1 * h3) * rate

    def at(m, b):
        first = (b * 3 + m) * BLOCK
        return slice(first, first + BLOCK)

    @pl.when(span == 0)
    def _():
        x, y_val = kk[group, c], vv[group, c]
        minus_r = -jnp.broadcast_to(r_in[...], (LANES, T)).T[:, 0:1]
        acts = slopes(dot_nn(x, w_in[0]), dot_nn(x, w_in[1]), dot_nn(y_val, w_in[2]) * minus_r, minus_r)
        for m in range(3):
            grad = dot_nn(acts[m].T.astype(BF16), x if m < 2 else y_val)
            low, high = grad[:HALF], grad[HALF:]
            mine = jnp.where(c == 0, low, high)
            theirs = jnp.where(c == 0, high, low).astype(BF16)
            for b in range(NL):
                for k in range(NK):
                    g_own[k, at(m, b), :] = mine[k * BLOCK:(k + 1) * BLOCK, b * LANES:(b + 1) * LANES]
                    g_give[k, at(m, b), :] = theirs[k * BLOCK:(k + 1) * BLOCK, b * LANES:(b + 1) * LANES]

    pl.semaphore_wait(barrier, ny + nz + half)

    def remote(src, dst, send, recv, target):
        return pltpu.make_async_remote_copy(
            src_ref=src, dst_ref=dst, send_sem=send, recv_sem=recv, device_id={"seq": target}, device_id_type=MESH
        )

    def fan(n, place, src, dst, send, recv):
        def one(i, carry):
            index, target = place(i)
            from_ref, to_ref = src(index), dst(index)

            @pl.when(target == s)
            def _():
                pltpu.make_async_copy(from_ref, to_ref, recv).start()

            @pl.when(target != s)
            def _():
                remote(from_ref, to_ref, send, recv, target).start()

            return carry

        lax.fori_loop(0, n, one, 0)

    def along_z(i):
        zt = lax.rem(z + far_first(i, nz), nz)
        return zt, seq_at(y, zt)

    def column(i, kind):
        return 2 * lax.rem(z // 2 + far_first(i, half), half) + (c if kind == 0 else 1 - c)

    def row(i):
        return lax.rem(line + i, NK)

    def across(i):
        return jnp.where(line < 2, i, NK - 1 - i)

    def near(i):
        back = line >= 2
        me = jnp.where(back, NK - 1 - line, line)
        k = i - 1 + (i - 1 >= me).astype(jnp.int32)
        return jnp.where(back, NK - 1 - k, k)

    def part(i):
        return pl.ds(pl.multiple_of(i * rows, 16), rows)

    def arrived(ref, sem):
        pltpu.make_async_copy(ref, ref, sem).wait()

    def total(ref):
        out = ref[0].astype(F32)
        for i in range(1, ref.shape[0]):
            out = out + ref[i].astype(F32)
        return out.astype(BF16)

    gives = [remote(g_give.at[k], g_got.at[k], gh_send.at[k], gh_recv.at[k], partner) for k in range(NK)]
    shares = [
        remote(ref, ref, x_send.at[i], x_recv.at[i], partner)
        for i, ref in enumerate((kk.at[group, c], vv.at[group, c], rr.at[group, c], qq.at[c]))
    ]
    halo = [
        remote(src.at[group, c], dst, h_send.at[i], h_recv.at[i], beside)
        for i, (src, dst) in enumerate(((kk, hk), (vv, hv)))
    ]
    group_of = (kk, vv, rr)

    def scatter0():
        first = y - line

        def send(i, carry):
            k = i

            def place_z(j):
                zt = column(j, 0)
                return zt, seq_at(y, zt)

            fan(half, place_z, lambda zt: g_send0.at[k, part(zt)], lambda zt: landz.at[k, z], az_send, az_recv.at[k])
            return carry

        def send_y(i, carry):
            zt = column(i, 1)

            def place_y(j):
                k = jnp.where(j == NK - 1, line, near(NK - 1 - j))
                return k, seq_at(first + k, z)

            fan(NK, place_y, lambda k: g_send0.at[k, part(zt)], lambda k: landy.at[zt // 2, line], ay_send, ay_recv.at[zt // 2])
            return carry

        for i in range(max(NK, half)):
            if i < NK:
                send(i, 0)
            if i < half:
                send_y(i, 0)

    def scatter0_end():
        def add_z(k):
            arrived(landz.at[k], az_recv.at[k])
            midz[k] = total(landz.at[k])
            pltpu.make_async_copy(midz.at[k], landp.at[k, line], p_recv.at[k]).start()
            for i in range(NK):
                remote(midz.at[k], landp.at[k, line], p_send.at[0], p_recv.at[k], seq_at(NK + across(i), z)).start()

        def add_y(i):
            zt = column(i, 1)
            j = zt // 2
            arrived(landy.at[j], ay_recv.at[j])
            midy[j] = total(landy.at[j])

            @pl.when(zt == z)
            def _():
                pltpu.make_async_copy(midy.at[j], finz.at[z], bz_recv).start()

            @pl.when(zt != z)
            def _():
                remote(midy.at[j], finz.at[z], bz_send, bz_recv, seq_at(y, zt)).start()

        for i in range(max(NK, half)):
            if i < half:
                add_y(i)
            if i < NK:

                @pl.when(y_first)
                def _():
                    add_z(i)

        @pl.when(jnp.logical_not(y_first))
        def _():
            arrived(finz, bz_recv)
            g_all0[line, part(z), :] = total(finz)

    def to_z(block, send, recv):
        def one(i, carry):
            _, target = along_z(i)
            remote(block, block, send, recv, target).start()
            return carry

        lax.fori_loop(0, nz - 1, one, 0)

    def to_own_span(block, send, recv):
        for i in range(NK - 1, 0, -1):
            remote(block, block, send, recv, seq_at(y - line + near(i), z)).start()

    def to_span1(block, send, recv):
        for i in range(NK):
            remote(block, block, send, recv, seq_at(NK + across(i), z)).start()

    def gather0():
        def block(k, zt):
            return g_all0.at[k, part(zt)]

        def column0(i):
            return 4 * lax.rem(z // 4 + i, fourth) + 3 - c

        own = block(line, z)

        def forward_z(k):
            arrived(block(k, z), y_recv.at[0, k])
            to_z(block(k, z), z_send.at[0], z_recv.at[0])

        def add_rows(k):
            arrived(landp.at[k], p_recv.at[k])
            g_all0[k, part(z), :] = total(landp.at[k])
            to_z(block(k, z), z_send.at[0], z_recv.at[0])

        owner_y = y_first0 & jnp.logical_not(y_first)

        @pl.when(span == 0)
        def _():
            @pl.when(owner_y)
            def _():
                to_span1(own, y_send.at[0], y_recv.at[0, line])
                to_own_span(own, y_send.at[1], y_recv.at[0, line])

            @pl.when(jnp.logical_not(y_first0))
            def _():
                to_z(own, zy_send.at[0], zy_recv.at[0, z])
                to_span1(own, fy_send.at[0], fy_recv.at[0])

            for i in range(fourth):
                zt = column0(i)

                @pl.when(zt != z)
                def _():
                    arrived(block(line, zt), zy_recv.at[0, zt])
                    to_span1(block(line, zt), fy_send.at[0], fy_recv.at[0])

            for i in range(fourth):
                to_own_span(block(line, column0(i)), fy_send.at[1], fy_recv.at[0])

            @pl.when(y_first)
            def _():
                for k in range(NK):
                    for i in range(1, NK):
                        remote(midz.at[k], landp.at[k, line], p_send.at[1], p_recv.at[k], seq_at(row(i), z)).start()

            @pl.when(owner_y)
            def _():
                to_z(own, z_send.at[0], z_recv.at[0])
                for i in range(1, NK):
                    forward_z(row(i))

        @pl.when((span == 1) & owner_y)
        def _():
            for i in range(NK):
                forward_z(jnp.where(line >= 2, i, NK - 1 - i))

        @pl.when(y_first)
        def _():
            for k in range(NK):
                add_rows(k)

    def gathered(p, along_y_first, columns):
        @pl.when(along_y_first)
        def _():
            arrived(landz.at[:, pl.ds(0, columns - 1)], z_recv.at[p])

        @pl.when(jnp.logical_not(along_y_first))
        def _():
            arrived(landz.at[:, pl.ds(0, columns)], z_recv.at[p])

    def place1(k, zt):
        return g_all1.at[lax.rem(k, 2) * 2 + lax.rem(zt, 2), part(k // 2 * half + zt // 2)]

    def gather1():
        own = place1(line, z)

        @pl.when(y_first)
        def _():
            to_own_span(own, y_send.at[0], y_recv.at[1, line])
            to_z(own, z_send.at[1], z_recv.at[1])

        @pl.when(jnp.logical_not(y_first))
        def _():
            to_z(own, zy_send.at[1], zy_recv.at[1, z])
            to_own_span(own, fy_send.at[0], fy_recv.at[1])

        for i in range(max(NK, half)):
            if 1 <= i < NK:

                @pl.when(y_first)
                def _():
                    k = near(i)
                    arrived(place1(k, z), y_recv.at[1, k])
                    to_z(place1(k, z), z_send.at[1], z_recv.at[1])

            if i < half:
                zt = column(half - 1 - i, 1)

                @pl.when(zt != z)
                def _():
                    arrived(place1(line, zt), zy_recv.at[1, zt])
                    to_own_span(place1(line, zt), fy_send.at[0], fy_recv.at[1])

    def initial_weights():
        first = pl.multiple_of(c * HALF, HALF)
        for m in range(3):
            w = w_in[m, :, pl.ds(first, HALF)].astype(F32).T
            for b in range(NL):
                for k in range(NK):
                    w_f[k, at(m, b), :] = w[k * BLOCK:(k + 1) * BLOCK, b * LANES:(b + 1) * LANES]

    def attention():
        @pl.when(c == 0)
        def _():
            for copy in halo:
                copy.wait_recv()

        @pl.when(c == 1)
        def _():
            hk[...] = kk[group, 0]
            hv[...] = vv[group, 0]

        q = qq[c]
        inv = jnp.sqrt(jnp.float32(DH))
        before = dot_nt(q, hk[...]) / inv
        here = dot_nt(q, kk[group, c]) / inv
        t_q = lax.broadcasted_iota(jnp.int32, (T, T), 0)
        t_k = lax.broadcasted_iota(jnp.int32, (T, T), 1)
        before = jnp.where((t_k > t_q) & (s > 0), before, jnp.float32(-1e30))
        here = jnp.where(t_k <= t_q, here, jnp.float32(-1e30))
        top = jnp.maximum(jnp.max(before, axis=1, keepdims=True), jnp.max(here, axis=1, keepdims=True))
        before, here = jnp.exp(before - top), jnp.exp(here - top)
        norm = jnp.sum(before, axis=1, keepdims=True) + jnp.sum(here, axis=1, keepdims=True)
        before, here = (before / norm).astype(BF16), (here / norm).astype(BF16)
        attn[...] = dot_nn(before, hv[...]) + dot_nn(here, vv[group, c])

    last_chip = chip == NK * nz - 1

    def start_halo():
        for copy in halo:
            copy.start()

    @pl.when(span == 0)
    def _():
        for give in gives:
            give.start()
        for share in shares:
            share.start()
        pl.when((c == 1) & last_chip)(start_halo)
        for k, give in enumerate(gives):
            give.wait_recv()
            g_send0[k] = (g_own[k] + g_got[k].astype(F32)).astype(BF16)
        scatter0()
        initial_weights()
        for share in shares:
            share.wait_recv()
        scatter0_end()
        gather0()
        pl.when((c == 1) & jnp.logical_not(last_chip))(start_halo)
        attention()
        arrived(landy.at[pl.ds(0, fourth), pl.ds(0, NK - 1)], fy_recv.at[0])

    @pl.when(span == 1)
    def _():
        for share in shares:
            share.start()
        pl.when(c == 1)(start_halo)
        for target, _ in pairs:
            for j, ref in enumerate(group_of):
                own = ref.at[group, c]
                remote(own, own, col_send.at[j], col_recv.at[j, group], target).start()
        initial_weights()
        gather0()
        for _, k in pairs:
            for j, ref in enumerate(group_of):
                block = ref.at[k, c]
                arrived(block, col_recv.at[j, k])
                remote(block, block, fwd_send.at[j], fwd_recv.at[j, k], partner).start()
        for share in shares:
            share.wait_recv()
        attention()
        for _, k in pairs:
            for j, ref in enumerate(group_of):
                arrived(ref.at[k, 1 - c], fwd_recv.at[j, k])
        arrived(landy.at[pl.ds(0, fourth)], fy_recv.at[0])

    def row_scales(p, g_all):
        ss_own[p] = jnp.zeros((16, LANES), F32)
        for m in range(3):
            for b in range(NL):
                g = g_all[:, at(m, b), :].astype(F32)
                ss_own[p, m * NL + b:m * NL + b + 1, :] = jnp.sum(jnp.sum(g * g, axis=0), axis=0, keepdims=True)
        swap = remote(ss_own.at[p], ss_got.at[p], ss_send.at[p], ss_recv.at[p], partner)
        swap.start()
        swap.wait()

    def descend(p, g_all, blocks):
        scale = 0.05 * lax.rsqrt((ss_own[p] + ss_got[p]) * (1.0 / FH) + 1e-06)
        for k in blocks:
            for m in range(3):
                for b in range(NL):
                    j = m * NL + b
                    new = w_f[k, at(m, b), :] - g_all[k, at(m, b), :].astype(F32) * scale[j:j + 1]
                    w_f[k, at(m, b), :] = new
                    first = m * HALF + k * BLOCK
                    place = slice(first, first + BLOCK) if isinstance(k, int) else pl.ds(pl.multiple_of(first, BLOCK), BLOCK)
                    for i, term in enumerate(split(new)):
                        w_b[i, place, b * LANES:(b + 1) * LANES] = term

    gathered(0, y_first0, nz - fourth)
    row_scales(0, g_all0)

    @pl.when(span == 0)
    def _():
        descend(0, g_all0, range(NK))

    def gradient1():
        n = 2 * NK * T
        x, y_val = kk[...].reshape(n, DH), vv[...].reshape(n, DH)
        minus_r = -jnp.concatenate([rr[k, i][0:1] for k in range(NK) for i in range(2)], axis=1)

        def block(i, m):
            return w_b[i, pl.ds(pl.multiple_of(m * HALF + group * BLOCK, BLOCK), BLOCK), :]

        h = dot_nt(jnp.concatenate([block(0, 0), block(0, 1), block(1, 0), block(1, 1)], axis=0), x)
        h = h[:2 * BLOCK] + h[2 * BLOCK:]
        dg = dot_nt(jnp.concatenate([block(0, 2), block(1, 2)], axis=0), y_val)
        dg = (dg[:BLOCK] + dg[BLOCK:]) * minus_r
        a_gate, a_up, a_down = slopes(h[:BLOCK], h[BLOCK:], dg, minus_r)
        on_x = dot_nn(jnp.concatenate([a_gate, a_up], axis=0).astype(BF16), x).astype(BF16)
        on_y = dot_nn(a_down.astype(BF16), y_val).astype(BF16)
        for m, grad in enumerate((on_x[:BLOCK], on_x[BLOCK:], on_y)):
            for b in range(NL):
                g_send1[at(m, b), :] = grad[:, b * LANES:(b + 1) * LANES]

    @pl.when(span == 1)
    def _():
        descend(0, g_all0, [group])
        gradient1()

        def counterpart(i):
            k = lax.rem(line + 2 - 2 * lax.rem(i, 2), NK)
            zt = 2 * lax.rem(z // 2 + far_first(i // 2, half), half) + right
            return k // 2 * half + zt // 2, seq_at(NK + k, zt)

        mine = line // 2 * half + z // 2
        fan(nz, counterpart, lambda i: g_send1.at[part(i)], lambda i: land1.at[mine], r1_send, r1_recv)
        descend(0, g_all0, [lax.rem(group + i, NK) for i in range(1, NK)])
        arrived(land1, r1_recv)
        g_all1[group, part(mine), :] = total(land1)
        gather1()
        arrived(landy.at[:, pl.ds(0, NK - 1)], fy_recv.at[1])
        gathered(1, y_first, half)
        row_scales(1, g_all1)
        descend(1, g_all1, range(NK))

    def apply():
        def half_sum(q):
            h1 = dot_nt(q, w_b[0, 0:HALF]) + dot_nt(q, w_b[1, 0:HALF])
            h3 = dot_nt(q, w_b[0, HALF:2 * HALF]) + dot_nt(q, w_b[1, HALF:2 * HALF])
            high, low = split(h1 * jax.nn.sigmoid(h1) * h3)
            w_high, w_low = w_b[0, 2 * HALF:3 * HALF], w_b[1, 2 * HALF:3 * HALF]
            return dot_nn(high, w_high) + (dot_nn(low, w_high) + dot_nn(high, w_low))

        f_give[...] = half_sum(qq[1 - c]).astype(BF16)
        swap = remote(f_give, f_got, f_send, f_recv, partner)
        swap.start()
        mine = half_sum(qq[c])
        swap.wait()
        f = mine + f_got[...].astype(F32)
        fast = (f * lax.rsqrt(jnp.mean(f * f, axis=1, keepdims=True) + 1e-06)).astype(BF16)
        out_ref[...] = (attn[...] + fast.astype(F32)).astype(BF16)

    apply()

    def left(whole, sem, one_stayed):
        @pl.when(one_stayed)
        def _():
            arrived(whole(1), sem)

        @pl.when(jnp.logical_not(one_stayed))
        def _():
            arrived(whole(0), sem)

    most = g_all0.at[:, pl.ds(0, ROWS - rows)]
    three = finy.at[pl.ds(0, NK - 1)]
    z_first = jnp.logical_not(y_first)
    for share in shares:
        share.wait_send()

    @pl.when(c == 1)
    def _():
        for copy in halo:
            copy.wait_send()

    @pl.when(y_first0)
    def _():
        arrived(most, z_send.at[0])

    @pl.when(span == 0)
    def _():
        for give in gives:
            give.wait_send()
        left(lambda n: landz.at[:, pl.ds(0, half - n)], az_send, y_first)
        arrived(landy.at[:, pl.ds(0, NK - 1)], ay_send)
        left(lambda n: finz.at[pl.ds(0, half - n)], bz_send, z_first)
        arrived(landy.at[pl.ds(0, fourth)], fy_send.at[0])
        arrived(landy.at[pl.ds(0, fourth), pl.ds(0, NK - 1)], fy_send.at[1])

        @pl.when(y_first)
        def _():
            arrived(landp, p_send.at[0])
            arrived(landp.at[:, pl.ds(0, NK - 1)], p_send.at[1])

        @pl.when(y_first0 & z_first)
        def _():
            arrived(finy, y_send.at[0])
            arrived(three, y_send.at[1])

        @pl.when(jnp.logical_not(y_first0))
        def _():
            arrived(finz.at[pl.ds(0, nz - 1)], zy_send.at[0])

    @pl.when(span == 1)
    def _():
        for j, ref in enumerate(group_of):
            arrived(ref.at[pl.ds(0, 3), 0], col_send.at[j])
            arrived(ref.at[pl.ds(0, 3), 0], fwd_send.at[j])
        arrived(land1.at[pl.ds(0, nz - 1)], r1_send)
        arrived(landy.at[:, pl.ds(0, NK - 1)], fy_send.at[0])

        @pl.when(y_first)
        def _():
            arrived(three, y_send.at[0])
            arrived(most, z_send.at[1])

        @pl.when(z_first)
        def _():
            arrived(finz.at[pl.ds(0, nz - 1)], zy_send.at[1])


def local(ny, nz, queries, keys, values, rates, gate_fast, up_fast, down_fast):
    rows = ROWS // nz
    dma = pltpu.SemaphoreType.DMA
    full = (NK, ROWS, LANES)
    return pl.pallas_call(
        functools.partial(kernel, ny, nz),
        out_shape=jax.ShapeDtypeStruct((T, DH), BF16),
        in_specs=[pl.BlockSpec(memory_space=pl.ANY)] * 7,
        out_specs=pl.BlockSpec(memory_space=pltpu.VMEM),
        scratch_shapes=[
            pltpu.VMEM((2, T, DH), BF16),
            pltpu.VMEM((NK, 2, T, DH), BF16),
            pltpu.VMEM((NK, 2, T, DH), BF16),
            pltpu.VMEM((NK, 2, 8, LANES), F32),
            pltpu.VMEM((T, DH), BF16),
            pltpu.VMEM((T, DH), BF16),
            pltpu.VMEM((1, T), F32),
            pltpu.VMEM((3, DH, FH), BF16),
            pltpu.VMEM(full, F32),
            pltpu.VMEM((2, 3 * HALF, DH), BF16),
            pltpu.VMEM(full, F32),
            pltpu.VMEM(full, BF16),
            pltpu.VMEM(full, BF16),
            pltpu.VMEM(full, BF16),
            pltpu.VMEM((ROWS, LANES), BF16),
            pltpu.VMEM(full, BF16),
            pltpu.VMEM(full, BF16),
            pltpu.VMEM((NK, nz, rows, LANES), BF16),
            pltpu.VMEM((NK, rows, LANES), BF16),
            pltpu.VMEM((NK, NK, rows, LANES), BF16),
            pltpu.VMEM((NK, rows, LANES), BF16),
            pltpu.VMEM((nz // 2, NK, rows, LANES), BF16),
            pltpu.VMEM((nz // 2, rows, LANES), BF16),
            pltpu.VMEM((nz, rows, LANES), BF16),
            pltpu.VMEM((nz, rows, LANES), BF16),
            pltpu.VMEM((2, 16, LANES), F32),
            pltpu.VMEM((2, 16, LANES), F32),
            pltpu.VMEM((T, DH), F32),
            pltpu.VMEM((T, DH), BF16),
            pltpu.VMEM((T, DH), BF16),
            dma((7,)),
            dma((4,)),
            dma((4,)),
            dma((2,)),
            dma((2,)),
            dma((NK,)),
            dma((NK,)),
            dma((3,)),
            dma((3, NK)),
            dma((3,)),
            dma((3, NK)),
            dma,
            dma((NK,)),
            dma,
            dma((nz // 2,)),
            dma,
            dma,
            dma((2,)),
            dma((NK,)),
            dma,
            dma,
            dma((2,)),
            dma((2, NK)),
            dma((2,)),
            dma((2,)),
            dma((2,)),
            dma((2, nz)),
            dma((2,)),
            dma((2,)),
            dma((2,)),
            dma((2,)),
            dma,
            dma,
        ],
        compiler_params=pltpu.CompilerParams(
            collective_id=0, has_side_effects=True, vmem_limit_bytes=55040 * 1024
        ),
        name="fast_layer",
    )(queries, keys, values, rates.reshape(1, T), gate_fast, up_fast, down_fast)


def solution(mesh):
    ny = 2 * NK
    nz = mesh.shape["seq"] // 2 // ny
    return jax.shard_map(
        functools.partial(local, ny, nz),
        mesh=mesh,
        in_specs=(
            P("seq", "head"),
            P("seq", "head"),
            P("seq", "head"),
            P("seq", "head"),
            P("head", None, None),
            P("head", None, None),
            P("head", None, None),
        ),
        out_specs=P("seq", "head"),
        check_vma=False,
    )
```
